32 devices in a mesh: dom: 8 (over z, x), rep: 4 (over y, core).
Axes of the slice: x: 2, y: 2, z: 4, core: 2. Of those that a mesh axis runs over, the one named last changes fastest.
Arguments:
- features: bfloat16 [32768, 100], P('dom'), may hold values from -6 to 6
- labels: int32 [32768], P('dom'), may hold values from 0 to 46
- train_mask: int32 [32768], P('dom'), may hold values from 0 to 1
- edge_src: int32 [32768, 16], P('dom'), may hold values from 0 to 4351
- edge_norm: float32 [32768, 16], P('dom'), may hold values from 0.15 to 0.35
- send_rows: int32 [8, 8, 32], P('dom'), may hold values from 0 to 4095
- changed: int32 [3, 8], P(None, 'dom'), may hold values 0 or 1
- cache_hidden: bfloat16 [2, 2048, 256], P(None, 'dom', 'rep'), may hold values from -6 to 6
- cache_out: bfloat16 [2048, 47], P('dom'), may hold values from -5 to 5
- first_weight: float32 [100, 256], P(None, 'rep'), may hold values from -0.625 to 0.625
- second_weight: float32 [256, 256], P(None, 'rep'), may hold values from -0.375 to 0.375
- last_weight: float32 [256, 47], replicated, may hold values from -0.375 to 0.375
- hidden_bias: float32 [2, 256], P(None, 'rep'), may hold values from -2 to 2
- out_bias: float32 [47], replicated, may hold values from -2 to 2
- moment_first: float32 [100, 256], P(None, 'rep'), may hold values from -0.0078125 to 0.0078125
- moment_second: float32 [256, 256], P(None, 'rep'), may hold values from -0.0078125 to 0.0078125
- moment_last: float32 [256, 47], replicated, may hold values from -0.0078125 to 0.0078125
- moment_hidden: float32 [2, 256], P(None, 'rep'), may hold values from -0.015625 to 0.015625
- moment_out: float32 [47], replicated, may hold values from -0.015625 to 0.015625
- square_first: float32 [100, 256], P(None, 'rep'), may hold values from 1.5258789e-07 to 1.2207031e-06
- square_second: float32 [256, 256], P(None, 'rep'), may hold values from 1.5258789e-07 to 1.2207031e-06
- square_last: float32 [256, 47], replicated, may hold values from 1.5258789e-07 to 1.2207031e-06
- square_hidden: float32 [2, 256], P(None, 'rep'), may hold values from 1e-05 to 0.1, as said below
- square_out: float32 [47], replicated, may hold values from 6.1035155e-07 to 4.8828124e-06
Outputs:
- loss_sum: float32 [], replicated
- train_count: float32 [], replicated
- next_first: float32 [100, 256], P(None, 'rep')
- next_moment_first: float32 [100, 256], P(None, 'rep')
- next_square_first: float32 [100, 256], P(None, 'rep')
- next_second: float32 [256, 256], P(None, 'rep')
- next_moment_second: float32 [256, 256], P(None, 'rep')
- next_square_second: float32 [256, 256], P(None, 'rep')
- next_last: float32 [256, 47], replicated
- next_moment_last: float32 [256, 47], replicated
- next_square_last: float32 [256, 47], replicated
- next_hidden: float32 [2, 256], P(None, 'rep')
- next_moment_hidden: float32 [2, 256], P(None, 'rep')
- next_square_hidden: float32 [2, 256], P(None, 'rep')
- next_out: float32 [47], replicated
- next_moment_out: float32 [47], replicated
- next_square_out: float32 [47], replicated
The draws below stay inside these ranges and needn't reach their ends.
Inputs may be any that keep to these rules, and one draw needn't show every extreme that they name: `square_hidden`: positive.
All inputs are finite; a program needn't handle non-finite values. No bound on the sum of `changed` on one device may be relied on, other than what follows from the above.
Results may differ from the reference program's by a relative error of at most 0.00145.
The reference program's roundings to bfloat16 on the way count: a program that leaves them out, or rounds other values in their place, can miss the bound.
Values may be sent and summed in bfloat16 or wider, within the bound.
No kernel may reach another device: no remote copies, remote signals or barrier semaphores. Data moves between devices by JAX's collectives and lax.ppermute only.
A program may use at most 128 MiB of HBM per device.

```python
import math
import jax
import jax.numpy as jnp
from jax import lax

IN_FEAT = 100
UNITS = 256
CLASSES = 47
NODE_DEV = 4096
BND = 32
DEG = 16
STEP = 5
NODES = 32768
HALO_ALL = 2048
N_DOM = 8


def draw_train_mask(key, part):
    key = jax.random.fold_in(key, 7)
    rolls = jax.random.randint(key, (NODES,), 0, 1000)
    limits = 250 + 500 * jnp.arange(NODES, dtype=jnp.int32) // NODES
    return (rolls < limits).astype(jnp.int32)


def draw_square_hidden(key, part):
    key = jax.random.fold_in(key, 11)
    spots = jax.random.uniform(key, (2, UNITS), jnp.float32)
    floor_log = math.log(0.0001)
    range_log = math.log(100.0)
    return jnp.exp(floor_log + range_log * spots).astype(jnp.float32)


def place_ends(entries, stream_key, smallest, largest):
    longest = entries.shape.index(max(entries.shape))
    spots = []
    for shift in (0, 1):
        where = [jax.random.randint(jax.random.fold_in(stream_key, axis), (), 0, length) for axis, length in enumerate(entries.shape)]
        where[longest] = (where[longest] + shift) % entries.shape[longest]
        spots.append(tuple(where))
    return entries.at[spots[0]].set(smallest).at[spots[1]].set(largest)


def shard_levels(own_key, shape, split, least, top_value):
    gain = 1.0
    for dim, shards_of in split:
        draws = jax.random.uniform(jax.random.fold_in(jax.random.fold_in(own_key, 6), dim), (shards_of,), jnp.float32, least / len(split), top_value / len(split))
        gain = gain * jnp.repeat(jnp.exp(draws), shape[dim] // shards_of).reshape((-1,) + (1,) * (len(shape) - 1 - dim))
    return gain


def normal_values(rng, dims, scale, most, shards=(), kind=jnp.bfloat16):
    result = jax.random.normal(rng, dims, jnp.float32) * scale
    if len(shards) > 0:
        result = shard_levels(rng, dims, shards, -0.22, 0.18) * result
    return jnp.clip(result, min=-most, max=most).astype(kind)


def setup_inputs(seed: int = 0) -> dict:
    streams_of = jax.random.split(jax.random.key(seed), 25)
    return {
        "features": normal_values(streams_of[0], (NODES, IN_FEAT), 1.0, 6.0, ((0, 8),)),
        "labels": place_ends(jax.random.randint(streams_of[1], (NODES,), 0, CLASSES), jax.random.fold_in(streams_of[1], 1), 0, CLASSES - 1).astype(jnp.int32),
        "train_mask": draw_train_mask(jax.random.fold_in(streams_of[24], 71), 0),
        "edge_src": place_ends(jax.random.randint(streams_of[3], (NODES, DEG), 0, NODE_DEV + N_DOM * BND), jax.random.fold_in(streams_of[3], 1), 0, (NODE_DEV + N_DOM * BND) - 1).astype(jnp.int32),
        "edge_norm": jnp.clip(0.15 + 0.19999999 * jax.random.uniform(streams_of[4], (NODES, DEG), jnp.float32) ** shard_levels(streams_of[4], (NODES, DEG), ((0, 8),), -0.2, 0.2), 0.15, 0.35),
        "send_rows": place_ends(jax.random.randint(streams_of[5], (N_DOM, N_DOM, BND), 0, NODE_DEV), jax.random.fold_in(streams_of[5], 1), 0, NODE_DEV - 1).astype(jnp.int32),
        "changed": place_ends((jax.random.randint(streams_of[6], (3, N_DOM), 0, 2) < 1).astype(jnp.int32), jax.random.fold_in(streams_of[6], 1), 0, 1),
        "cache_hidden": normal_values(streams_of[7], (2, HALO_ALL, UNITS), 1.0, 6.0, ((1, 8), (2, 4))),
        "cache_out": normal_values(streams_of[8], (HALO_ALL, CLASSES), 0.7, 5.0, ((0, 8),)),
        "first_weight": normal_values(streams_of[9], (IN_FEAT, UNITS), IN_FEAT ** -0.5, 0.625, ((1, 4),), jnp.float32),
        "second_weight": normal_values(streams_of[10], (UNITS, UNITS), UNITS ** -0.5, 0.375, ((1, 4),), jnp.float32),
        "last_weight": normal_values(streams_of[11], (UNITS, CLASSES), UNITS ** -0.5, 0.375, (), jnp.float32),
        "hidden_bias": normal_values(streams_of[12], (2, UNITS), 0.3, 2.0, ((1, 4),), jnp.float32),
        "out_bias": normal_values(streams_of[13], (CLASSES,), 0.3, 2.0, (), jnp.float32),
        "moment_first": normal_values(streams_of[14], (IN_FEAT, UNITS), (0.1 / NODES ** 0.5), 0.0078125, ((1, 4),), jnp.float32),
        "moment_second": normal_values(streams_of[15], (UNITS, UNITS), (0.1 / NODES ** 0.5), 0.0078125, ((1, 4),), jnp.float32),
        "moment_last": normal_values(streams_of[16], (UNITS, CLASSES), (0.1 / NODES ** 0.5), 0.0078125, (), jnp.float32),
        "moment_hidden": normal_values(streams_of[17], (2, UNITS), (0.2 / NODES ** 0.5), 0.015625, ((1, 4),), jnp.float32),
        "moment_out": normal_values(streams_of[18], (CLASSES,), (0.2 / NODES ** 0.5), 0.015625, (), jnp.float32),
        "square_first": jnp.clip(jnp.exp(math.log(1.220703097715159e-06) - 2.0794415 * jax.random.uniform(streams_of[19], (IN_FEAT, UNITS), jnp.float32) ** shard_levels(streams_of[19], (IN_FEAT, UNITS), ((1, 4),), -0.2, 0.2)), 1.5258788721439487e-07, 1.220703097715159e-06),
        "square_second": jnp.clip(jnp.exp(math.log(1.220703097715159e-06) - 2.0794415 * jax.random.uniform(streams_of[20], (UNITS, UNITS), jnp.float32) ** shard_levels(streams_of[20], (UNITS, UNITS), ((1, 4),), -0.2, 0.2)), 1.5258788721439487e-07, 1.220703097715159e-06),
        "square_last": jnp.clip(jnp.exp(jax.random.uniform(streams_of[21], (UNITS, CLASSES), jnp.float32, math.log(1.5258788721439487e-07), math.log(1.220703097715159e-06))), 1.5258788721439487e-07, 1.220703097715159e-06),
        "square_hidden": draw_square_hidden(jax.random.fold_in(streams_of[24], 71), 0),
        "square_out": jnp.clip(jnp.exp(jax.random.uniform(streams_of[23], (CLASSES,), jnp.float32, math.log(6.103515488575795e-07), math.log(4.882812390860636e-06))), 6.103515488575795e-07, 4.882812390860636e-06),
    }


@jax.custom_vjp
def low(v):
    return lax.optimization_barrier(v.astype(jnp.bfloat16)).astype(jnp.float32)

@jax.custom_vjp
def low_back(v):
    return v

def low_keep(v):
    return (low(v), None)

def low_pass(kept, grad):
    return (grad,)

def back_keep(v):
    return (v, None)

def back_low(kept, grad):
    return (low(grad),)
low.defvjp(low_keep, low_pass)
low_back.defvjp(back_keep, back_low)
beta_one = 0.5
beta_two = 0.5
rate_step = 0.03
decay_rate = 0.01
epsilon = 1e-08

def matmul(left, right):
    return jnp.dot(left, right, precision=lax.Precision.HIGHEST, preferred_element_type=jnp.float32)

def aggregate(values, stored, fresh, send_rows, edge_src, edge_norm):
    breadth = values.shape[1]
    owners = (jnp.arange(N_DOM, dtype=jnp.int32) * NODE_DEV)[:, None, None]
    sources = (owners + send_rows).reshape(-1)
    arrived = values[sources].reshape(N_DOM, N_DOM, BND, breadth)
    arrived = jnp.transpose(arrived, (1, 0, 2, 3))
    stale = stored.reshape(N_DOM, N_DOM, BND, breadth)
    border = jnp.where((fresh == 1)[None, :, None, None], arrived, stale)
    lookup = jnp.concatenate([values.reshape(N_DOM, NODE_DEV, breadth), border.reshape(N_DOM, N_DOM * BND, breadth)], axis=1)
    slots = edge_src.reshape(N_DOM, NODE_DEV * DEG)
    picked = jax.vmap(lambda table_part, slot_part: table_part[slot_part])(lookup, slots)
    picked = picked.reshape(NODES, DEG, breadth)
    return lax.optimization_barrier(jnp.sum(picked * edge_norm[:, :, None], axis=1))

def adamw(weight, moment, square, gradient):
    moment = beta_one * moment + (1.0 - beta_one) * gradient
    square = beta_two * square + (1.0 - beta_two) * gradient * gradient
    moment_hat = moment / (1.0 - beta_one ** STEP)
    square_hat = square / (1.0 - beta_two ** STEP)
    weight = weight - rate_step * (moment_hat / (jnp.sqrt(square_hat) + epsilon) + decay_rate * weight)
    return (weight, moment, square)

def reference(features, labels, train_mask, edge_src, edge_norm, send_rows, changed, cache_hidden, cache_out, first_weight, second_weight, last_weight, hidden_bias, out_bias, moment_first, moment_second, moment_last, moment_hidden, moment_out, square_first, square_second, square_last, square_hidden, square_out):
    inputs = features.astype(jnp.float32)
    caches = cache_hidden.astype(jnp.float32)
    last_cache = cache_out.astype(jnp.float32)
    masked = train_mask.astype(jnp.float32)
    train_count = jnp.sum(masked)
    target = 0.9 * jax.nn.one_hot(labels, CLASSES, dtype=jnp.float32) + 0.1 / CLASSES

    def spread(values, stored, fresh):
        return aggregate(values, stored, fresh, send_rows, edge_src, edge_norm)

    def loss_of(params):
        weight_one, weight_two, weight_three, bias_hidden, bias_out = params
        z_one = low_back(low(matmul(inputs, low(weight_one))))
        h_one = low(jax.nn.gelu(spread(z_one, caches[0], changed[0]) + bias_hidden[0]))
        z_two = low_back(low(matmul(h_one, low(weight_two))))
        h_two = low(jax.nn.gelu(spread(z_two, caches[1], changed[1]) + bias_hidden[1]))
        z_three = low_back(low(matmul(h_two, low(weight_three))))
        logits = spread(z_three, last_cache, changed[2]) + bias_out
        logp = jax.nn.log_softmax(logits, axis=-1)
        row_loss = -lax.optimization_barrier(jnp.sum(target * logp, axis=-1))
        return jnp.sum(row_loss * masked)
    params = (first_weight, second_weight, last_weight, hidden_bias, out_bias)
    loss_sum, pull = jax.vjp(loss_of, params)
    grads = pull(jnp.ones((), jnp.float32) / train_count)[0]
    moments = (moment_first, moment_second, moment_last, moment_hidden, moment_out)
    squares = (square_first, square_second, square_last, square_hidden, square_out)
    results = [adamw(w, m, v, g) for w, m, v, g in zip(params, moments, squares, grads)]
    return (loss_sum, train_count, results[0][0], results[0][1], results[0][2], results[1][0], results[1][1], results[1][2], results[2][0], results[2][1], results[2][2], results[3][0], results[3][1], results[3][2], results[4][0], results[4][1], results[4][2])
```

```python
import functools

import jax
import jax.numpy as jnp
from jax import lax
from jax.experimental import pallas as pl
from jax.experimental.pallas import tpu as pltpu
from jax.sharding import PartitionSpec as P

STEP = 5
beta_one = 0.5
beta_two = 0.5
rate_step = 0.03
decay_rate = 0.01
epsilon = 1e-08

BF16, F32, F8, I32 = jnp.bfloat16, jnp.float32, jnp.float8_e4m3fn, jnp.int32
REST_GAIN = 4096.0
TAIL_GAIN = 256.0
FLAG_LANE = 100
ROWS = 512
LIMIT = 36 << 20

SMEM = pl.BlockSpec(memory_space=pltpu.SMEM)
HBM = pl.BlockSpec(memory_space=pltpu.HBM)


def whole(array):
    rank = len(array.shape)
    return array, pl.BlockSpec(array.shape, lambda *_: (0,) * rank)


def wholes(*arrays):
    return [whole(a) for a in arrays]


def columns_of(array, size=ROWS):
    return array, pl.BlockSpec((array.shape[0], size), lambda i: (0, i))


def run(kernel, name, grid, args, outs, scratch=(), flops=0):
    shapes = [jax.ShapeDtypeStruct(shape, kind) for shape, kind, _ in outs]
    return pl.pallas_call(
        kernel,
        grid=(grid,),
        in_specs=[spec for _, spec in args],
        out_specs=[spec if spec is not None else whole(s)[1] for s, (_, _, spec) in zip(shapes, outs)],
        out_shape=shapes,
        scratch_shapes=list(scratch),
        name=name,
        cost_estimate=pl.CostEstimate(flops=flops, bytes_accessed=1 << 20, transcendentals=0),
        compiler_params=pltpu.CompilerParams(vmem_limit_bytes=LIMIT),
    )(*[a for a, _ in args])


def dot_nn(left, right):
    return lax.dot_general(left, right, (((1,), (0,)), ((), ())), preferred_element_type=F32)


def dot_nt(left, right):
    return lax.dot_general(left, right, (((1,), (1,)), ((), ())), preferred_element_type=F32)


def dot_tn(left, right):
    return lax.dot_general(left, right, (((0,), (0,)), ((), ())), preferred_element_type=F32)


def scale_of(value):
    most = jnp.maximum(jnp.max(jnp.abs(value)), 1e-30)
    return 256.0 / most, most * (1.0 / 256.0)


def span(start, size):
    return pl.ds(pl.multiple_of(start, size), size)


def pick_rows(send, first, count):
    nodes = lax.broadcasted_iota(I32, (send.shape[0], count), 1) + first
    return jnp.where(send == nodes, 1.0, 0.0).astype(BF16)


class Ring:
    def __init__(self, refs, bufs, sems, cut):
        self.refs, self.bufs, self.sems, self.cut = refs, bufs, sems, cut
        self.step, self.steps = pl.program_id(0), pl.num_programs(0)
        self.slot = lax.rem(self.step, 2)

    def copies(self, step, slot):
        return [
            pltpu.make_async_copy(ref.at[self.cut(step)], buf.at[slot], self.sems.at[k, slot])
            for k, (ref, buf) in enumerate(zip(self.refs, self.bufs))
        ]

    def begin(self):
        @pl.when(self.step == 0)
        def _():
            for copy in self.copies(0, 0):
                copy.start()

        @pl.when((self.step == 0) & (self.steps > 1))
        def _():
            for copy in self.copies(1, 1):
                copy.start()

    def wait(self):
        for copy in self.copies(self.step, self.slot):
            copy.wait()
        return [buf.at[self.slot] for buf in self.bufs]

    def end(self):
        @pl.when(self.step + 2 < self.steps)
        def _():
            for copy in self.copies(self.step + 2, self.slot):
                copy.start()


def ring_scratch(shape, kinds):
    return [pltpu.VMEM((2, *shape), kind) for kind in kinds] + [pltpu.SemaphoreType.DMA((len(kinds), 2))]


def pack_kernel(feat_t, send, changed, mask, first_t, second_t, cache_t, bias, rows_out, pack_out):
    nodes, halo = feat_t.shape[1], send.shape[0]
    width, cols = feat_t.shape[0], first_t.shape[0]

    def pick(i, total):
        return total + dot_nt(pick_rows(send[...], i * ROWS, ROWS), feat_t[:, span(i * ROWS, ROWS)])

    total = lax.fori_loop(0, nodes // ROWS, pick, jnp.zeros((halo, width), F32))
    count = jnp.sum(mask[...].astype(F32))
    many = jnp.floor(count * (1.0 / 64.0))
    lane = lax.broadcasted_iota(I32, (halo, 128), 1)
    row = jnp.concatenate([total, jnp.zeros((halo, 128 - width), F32)], axis=1)
    for layer in range(3):
        row = jnp.where(lane == FLAG_LANE + layer, changed[layer, 0].astype(F32), row)
    row = jnp.where(lane == FLAG_LANE + 3, many, row)
    row = jnp.where(lane == FLAG_LANE + 4, count - 64.0 * many, row)
    rows_out[...] = row.astype(BF16).reshape(rows_out.shape)

    units = second_t.shape[1]
    pack_out[:, 0:128] = jnp.concatenate(
        [first_t[...], jnp.zeros((cols, 128 - width), F32)], axis=1
    ).astype(BF16)
    pack_out[:, 128 : 128 + units] = second_t[...].astype(BF16)
    left = jnp.concatenate([bias[...], jnp.zeros((2, 128 - cols), F32)], axis=1)
    terms = []
    for _ in range(3):
        term = left.astype(BF16).astype(F32)
        terms.append(term)
        left = left - term
    terms = jnp.concatenate(terms + [jnp.zeros((122, 128), F32)], axis=0).T
    pack_out[:, 128 + units : 256 + units] = terms[0:cols, :].astype(BF16)
    base = 256 + units
    for layer in range(2):
        pack_out[:, base + layer * halo : base + (layer + 1) * halo] = cache_t[layer]


def bias_column(packs, layer):
    units = packs.shape[0]
    terms = packs[:, 128 + units : 256 + units].astype(F32)
    return terms[:, layer : layer + 1] + terms[:, layer + 2 : layer + 3] + terms[:, layer + 4 : layer + 5]


def stale_columns(packs, layer, halo):
    base = 256 + packs.shape[0] + layer * halo
    return packs[:, base : base + halo].astype(F32)


def build_kernel(place, src_t, norm_t, high, rest):
    slots = src_t.shape[0]
    half = src_t.shape[1] // 2
    blocks = high.shape[1] // 256
    per_group = 256 // slots
    here = span(place[0] * half + pl.program_id(0) * 128, 128)
    lean = lambda tile: [
        pltpu.roll(tile[first : first + 8, :], 0, 1, stride=per_group, stride_axis=0)
        for first in range(0, slots, 8)
    ]
    source, weights = lean(src_t[:, here]), lean(norm_t[:, here])
    in_slot = lax.broadcasted_iota(I32, (8, 128), 1) // per_group == lax.broadcasted_iota(I32, (8, 128), 0)
    node_row = lax.broadcasted_iota(I32, (per_group, 256), 0)
    mine = lax.rem(lax.broadcasted_iota(I32, (per_group, 256), 1), per_group) == node_row
    inner = lax.broadcasted_iota(I32, (256, 256), 0)

    def flat(tiles, group):
        moved = [pltpu.roll(tile, (128 - per_group * group) % 128, 1) for tile in tiles]
        return jnp.concatenate(
            [jnp.sum(jnp.where(in_slot, tile, 0), axis=0, keepdims=True) for tile in moved], axis=1
        )

    def one(group):
        at = flat(source, group)
        weight = flat(weights, group)
        weight_high = weight.astype(BF16).astype(F32)
        hit = inner == jnp.bitwise_and(at, 255)
        right = jnp.concatenate(
            [
                jnp.where(hit, weight_high, 0.0).astype(BF16),
                jnp.where(hit, weight - weight_high, 0.0).astype(BF16),
            ],
            axis=1,
        )
        block = jnp.where(mine, jnp.right_shift(at, 8), -1)
        left = jnp.concatenate(
            [jnp.where(block == j, 1.0, 0.0).astype(BF16) for j in range(blocks)], axis=0
        )
        return dot_nt(jnp.concatenate([left, left], axis=1), right)

    parts = [one(group) for group in range(128 // per_group)]
    for j in range(blocks):
        full = jnp.concatenate([p[per_group * j : per_group * (j + 1), :] for p in parts], axis=0)
        top = full.astype(BF16)
        cols = slice(256 * j, 256 * (j + 1))
        high[:, cols] = top
        rest[:, cols] = ((full - top.astype(F32)) * REST_GAIN).astype(F8)


def gelu_both(u):
    square = u * u
    t = jnp.tanh(0.79788456 * (u + 0.044715 * u * square))
    half = 0.5 * (1.0 + t)
    slope = half + 0.5 * u * (1.0 - t * t) * (0.79788456 * (1.0 + 3.0 * 0.044715 * square))
    return u * half, slope


def layer_one_kernel(place, rows, feat_t, packs, send, high, rest, hidden_t, slope_t, z_own, z_send, flags_t, table, table8, back, hbuf, rbuf, sems):
    width, nodes = feat_t.shape
    halo = send.shape[0]
    step = pl.program_id(0)
    ring = Ring((high, rest), (hbuf, rbuf), sems, lambda i: (span(i * ROWS, ROWS), slice(None)))
    ring.begin()

    @pl.when(step == 0)
    def _():
        weight = packs[:, 0:width]
        flat = rows[...].reshape(halo, 128)
        flags = flat.astype(F32).T[FLAG_LANE : FLAG_LANE + 8, :]
        counts = jnp.sum(rows[...].astype(F32)[:, 0, :], axis=0, keepdims=True)
        count = 64.0 * counts[:, FLAG_LANE + 3 : FLAG_LANE + 4] + counts[:, FLAG_LANE + 4 : FLAG_LANE + 5]
        row = lax.broadcasted_iota(I32, flags.shape, 0)
        flags_t[...] = jnp.where(row == 3, count, flags)

        def first(i, most):
            here = span(i * ROWS, ROWS)
            z = dot_nn(weight, feat_t[:, here])
            table[:, here] = z.astype(BF16)
            return jnp.maximum(most, jnp.abs(z))

        most = lax.fori_loop(0, nodes // ROWS, first, jnp.zeros((table.shape[0], ROWS), F32))
        border = dot_nt(weight, flat[:, 0:width]).astype(BF16).astype(F32)
        border = jnp.where(flags[0:1, :] == 1.0, border, stale_columns(packs, 0, halo))
        table[:, nodes : nodes + halo] = border.astype(BF16)
        scale, inverse = scale_of(jnp.maximum(jnp.max(most), jnp.max(jnp.abs(border))))
        back[0] = inverse * (1.0 / REST_GAIN)

        def small(i, carry):
            here = span(i * 256, 256)
            table8[:, here] = (table[:, here].astype(F32) * scale).astype(F8)
            return carry

        lax.fori_loop(0, (nodes + halo) // 256, small, 0)
        z_send[...] = jnp.zeros(z_send.shape, BF16)

    units = packs.shape[0]
    top, low = ring.wait()
    total = dot_nt(table[...], top[...]) + dot_nt(table8[...], low[...]) * back[0]
    ring.end()
    value, slope = gelu_both(total + bias_column(packs, 0))
    value = value.astype(BF16)
    hidden_t[...] = value
    slope_t[...] = slope
    z = dot_nn(packs[:, 128 : 128 + units], value).astype(BF16)
    z_own[...] = z
    half = nodes // 2
    chosen = dot_nt(pick_rows(send[...], place[0] * half + step * ROWS, ROWS), z)
    z_send[...] = (z_send[...].astype(F32) + chosen.reshape(z_send.shape)).astype(BF16)


def own_part_kernel(place, high, rest, z_own, z_oth, total, high8, table, table8, back, hbuf, rbuf, sems):
    half = z_own.shape[1]
    nodes = 2 * half
    ring = Ring((high, rest), (hbuf, rbuf), sems, lambda i: (span(i * ROWS, ROWS), slice(None)))
    ring.begin()

    @pl.when(pl.program_id(0) == 0)
    def _():
        def larger(i, most):
            here = span(i * ROWS, ROWS)
            both = jnp.maximum(jnp.abs(z_own[:, here].astype(F32)), jnp.abs(z_oth[:, here].astype(F32)))
            return jnp.maximum(most, both)

        most = lax.fori_loop(0, half // ROWS, larger, jnp.zeros((z_own.shape[0], ROWS), F32))
        scale, inverse = scale_of(most)
        back[0] = inverse * (1.0 / REST_GAIN)
        for ref, first in ((z_own, place[0] * half), (z_oth, (1 - place[0]) * half)):

            def put(i, carry):
                value = ref[:, span(i * ROWS, ROWS)]
                cols = span(first + i * ROWS, ROWS)
                table[:, cols] = value
                table8[:, cols] = (value.astype(F32) * scale).astype(F8)
                return carry

            lax.fori_loop(0, half // ROWS, put, 0)

    top, low = ring.wait()
    total[...] = dot_nt(table[...], top[:, 0:nodes]) + dot_nt(table8[...], low[:, 0:nodes]) * back[0]
    if high8 is not None:
        high8[...] = top[...].astype(F8)
    ring.end()


def own_part_plain_kernel(place, high, rest, z_own, z_oth, total, *scratch):
    own_part_kernel(place, high, rest, z_own, z_oth, total, None, *scratch)


def layer_two_end_kernel(place, flags_t, packs, send, high, rest, total, came, came_oth, last_t, hidden_t, slope_t, z_own, z_send, border, border8, back):
    halo = send.shape[0]
    width = hidden_t.shape[0]
    kinds = last_t.shape[0]
    step = pl.program_id(0)
    half = ROWS * pl.num_programs(0)

    @pl.when(step == 0)
    def _():
        both = came[...].reshape(halo, width).astype(F32) + came_oth[...].reshape(halo, width).astype(F32)
        value = jnp.where(flags_t[1:2, :] == 1.0, both.T, stale_columns(packs, 1, halo))
        scale, inverse = scale_of(value)
        border[...] = value.astype(BF16)
        border8[...] = (value * scale).astype(F8)
        back[0] = inverse * (1.0 / REST_GAIN)
        z_send[...] = jnp.zeros(z_send.shape, BF16)

    sums = total[...] + dot_nt(border[...], high[...]) + dot_nt(border8[...], rest[...]) * back[0]
    value, slope = gelu_both(sums + bias_column(packs, 1))
    value = value.astype(BF16)
    hidden_t[...] = value
    slope_t[...] = slope
    z = dot_nn(last_t[...].astype(BF16), value).astype(BF16)
    z_own[...] = z
    chosen = dot_nt(pick_rows(send[...], place[0] * half + step * ROWS, ROWS), z)
    chosen = jnp.concatenate([chosen, jnp.zeros((halo, 128 - kinds), F32)], axis=1)
    z_send[...] = (z_send[...].astype(F32) + chosen.reshape(z_send.shape)).astype(BF16)


def put_scales(back_out, step, rest_value, tail_value):
    lane = lax.broadcasted_iota(I32, (1, 128), 1)
    back_out[pl.ds(step, 1), :] = jnp.where(lane == 0, rest_value, tail_value)


def put_border(border_grad, total, keep):
    value = (total * keep).T
    bound = value.shape[0] // border_grad.shape[0]
    border_grad[:, 0:bound, :] = value.reshape(border_grad.shape[0], bound, value.shape[1])


def loss_kernel(classes, place, flags_t, high, rest, total, came, came_oth, stale_t, bias, labels, mask, sums, grads, grads8, back_out, border_grad, border, border8, back, border_sum):
    kinds = total.shape[0]
    halo = stale_t.shape[1]
    step = pl.program_id(0)

    @pl.when(step == 0)
    def _():
        both = came[...].reshape(halo, 128).astype(F32) + came_oth[...].reshape(halo, 128).astype(F32)
        old = jnp.concatenate([stale_t[...].astype(F32), jnp.zeros((kinds - classes, halo), F32)], axis=0)
        value = jnp.where(flags_t[2:3, :] == 1.0, both.T[0:kinds, :], old)
        scale, inverse = scale_of(value)
        border[...] = value.astype(BF16)
        border8[...] = (value * scale).astype(F8)
        back[0] = inverse * (1.0 / REST_GAIN)
        sums[...] = jnp.zeros(sums.shape, F32)
        border_sum[...] = jnp.zeros(border_sum.shape, F32)

    count = flags_t[3:4, 0:1]
    logits = total[...] + dot_nt(border[...], high[...]) + dot_nt(border8[...], rest[...]) * back[0]
    logits = logits + bias[...]
    kind = lax.broadcasted_iota(I32, logits.shape, 0)
    real = kind < classes
    logits = jnp.where(real, logits, -jnp.inf)
    shifted = logits - jnp.max(logits, axis=0, keepdims=True)
    powers = jnp.exp(shifted)
    norm = jnp.sum(powers, axis=0, keepdims=True)
    logp = jnp.where(real, shifted - jnp.log(norm), 0.0)
    here = span(step * ROWS, ROWS)
    target = jnp.where(kind == labels[pl.ds(place[0], 1), here], 0.9, 0.0) + 0.1 / classes
    used = mask[pl.ds(place[0], 1), here].astype(F32)
    loss = -jnp.sum(jnp.sum(target * logp, axis=0, keepdims=True) * used)
    grad = jnp.where(real, (powers / norm - target) * (used / count), 0.0)
    sums[0:kinds, :] += jnp.broadcast_to(jnp.sum(grad, axis=1, keepdims=True), (kinds, 128))
    sums[kinds : kinds + 8, :] += jnp.full((8, 128), loss, F32)
    top = grad.astype(BF16)
    tail = (grad - top.astype(F32)).astype(BF16)
    stacked = jnp.concatenate([top, tail], axis=0)
    small = (top.astype(F32) * (256.0 * count)).astype(F8)
    grads[...] = stacked
    grads8[...] = small
    inverse = (1.0 / (256.0 * REST_GAIN)) / count
    back_out[...] = jnp.broadcast_to(inverse, back_out.shape)
    both = dot_nn(stacked, high[...])
    border_sum[0:kinds, :] += both[0:kinds] + both[kinds : 2 * kinds] + dot_nn(small, rest[...]) * inverse

    @pl.when(step == pl.num_programs(0) - 1)
    def _():
        put_border(border_grad, border_sum[...], flags_t[2:3, :])


def back_three_kernel(other, place, high, rest, grads, grads8, back, out, hbuf, rbuf, sems):
    kinds, size = out.shape
    half = size * pl.num_programs(0)
    owner = 1 - place[0] if other else place[0]
    ring = Ring((high, rest), (hbuf, rbuf), sems, lambda i: (slice(None), span(owner * half + i * size, size)))
    ring.begin()
    top, low = ring.wait()
    both = dot_nn(grads[...], top[...])
    out[...] = both[0:kinds] + both[kinds : 2 * kinds] + dot_nn(grads8[...], low[...]) * back[0:1, 0:1]
    ring.end()


def back_kernel(other, halves, place, high, rest, high8, grads, grads8, tails8, back, out, hbuf, rbuf, tbuf, sems):
    size = out.shape[1]
    count = size * pl.num_programs(0)
    owner = 1 - place[0] if other else place[0]
    base = owner * count * halves + (place[1] * count if halves == 2 else 0)
    ring = Ring((high, rest, high8), (hbuf, rbuf, tbuf), sems, lambda i: (slice(None), span(base + i * size, size)))
    ring.begin()
    top, low, eight = ring.wait()
    total = dot_nn(grads[...], top[...])
    for b in range(grads.shape[1] // ROWS):
        cut = slice(b * ROWS, (b + 1) * ROWS)
        total = total + dot_nn(grads8[:, cut], low[cut, :]) * back[b : b + 1, 0:1]
        total = total + dot_nn(tails8[:, cut], eight[cut, :]) * back[b : b + 1, 1:2]
    out[...] = total
    ring.end()


def returned_terms(ret, ret_oth, bound, kinds):
    value = ret[:, 0:bound, :] + ret_oth[:, 0:bound, :]
    value = value.reshape(value.shape[0] * bound, value.shape[2]).T[0:kinds, :]
    top = value.astype(BF16)
    return top, (value - top.astype(F32)).astype(BF16)


def round_gradient(own, came_part, terms, send, first_node):
    chosen = pick_rows(send, first_node, own.shape[1])
    total = own[...] + came_part[...]
    for term in terms:
        total = total + dot_nn(term[...], chosen)
    return total.astype(BF16)


def upstream(grad, high, rest, high8, sums, grads, grads8, tails8, back_out, border_sum):
    sums[...] += jnp.broadcast_to(jnp.sum(grad, axis=1, keepdims=True), sums.shape)
    scale, inverse = scale_of(grad)
    top = grad.astype(BF16)
    wide = top.astype(F32)
    small = (wide * scale).astype(F8)
    tail = ((grad - wide) * (scale * TAIL_GAIN)).astype(F8)
    grads[...] = top
    grads8[...] = small
    tails8[...] = tail
    back_rest = inverse * (1.0 / REST_GAIN)
    back_tail = inverse * (1.0 / TAIL_GAIN)
    put_scales(back_out, pl.program_id(0), back_rest, back_tail)
    got = dot_nn(top, high[...])
    got = got + dot_nn(small, rest[...]) * back_rest
    border_sum[...] += got + dot_nn(tail, high8[...]) * back_tail


def end_three_kernel(place, flags_t, high, rest, high8, own, came_part, ret, ret_oth, send, hidden_t, slope_t, last, sums, grads, grads8, tails8, back_out, border_grad, border_sum, term_one, term_two, grad_last):
    kinds = own.shape[0]
    step = pl.program_id(0)
    half = ROWS * pl.num_programs(0)
    bound = send.shape[0] // ret.shape[0]

    @pl.when(step == 0)
    def _():
        term_one[...], term_two[...] = returned_terms(ret, ret_oth, bound, kinds)
        sums[...] = jnp.zeros(sums.shape, F32)
        border_sum[...] = jnp.zeros(border_sum.shape, F32)
        grad_last[...] = jnp.zeros(grad_last.shape, F32)

    d_z = round_gradient(own, came_part, (term_one, term_two), send[...], place[0] * half + step * ROWS)
    grad_last[0:kinds, :] += dot_nt(d_z, hidden_t[...])
    grad = dot_nn(last[...].astype(BF16), d_z) * slope_t[...]
    upstream(grad, high, rest, high8, sums, grads, grads8, tails8, back_out, border_sum)

    @pl.when(step == pl.num_programs(0) - 1)
    def _():
        put_border(border_grad, border_sum[...], flags_t[1:2, :])
        parts, _, width = border_grad.shape
        border_grad[:, bound:, :] = grad_last[...].reshape(parts, 64 // parts, width)


def end_two_kernel(place, flags_t, packs, high, rest, high8, own, came_part, ret, ret_oth, send, hidden_t, slope_t, sums, grads, grads8, tails8, back_out, border_grad, last_chunk, border_sum, term_one, term_two, grad_second):
    units = own.shape[0]
    step = pl.program_id(0)
    half = ROWS * pl.num_programs(0)
    bound = send.shape[0] // ret.shape[0]

    @pl.when(step == 0)
    def _():
        term_one[...], term_two[...] = returned_terms(ret, ret_oth, bound, units)
        last_chunk[...] = jnp.sum(ret[:, bound:, :] + ret_oth[:, bound:, :], axis=0)
        sums[...] = jnp.zeros(sums.shape, F32)
        border_sum[...] = jnp.zeros(border_sum.shape, F32)
        grad_second[...] = jnp.zeros(grad_second.shape, F32)

    d_z = round_gradient(own, came_part, (term_one, term_two), send[...], place[0] * half + step * ROWS)
    grad_second[...] += dot_nt(d_z, hidden_t[...])
    grad = dot_tn(packs[:, 128 : 128 + units], d_z) * slope_t[...]
    upstream(grad, high, rest, high8, sums, grads, grads8, tails8, back_out, border_sum)

    @pl.when(step == pl.num_programs(0) - 1)
    def _():
        put_border(border_grad, border_sum[...], flags_t[0:1, :])
        parts, _, width = border_grad.shape
        size = 64 // parts
        for core in range(2):
            block = grad_second[span(place[1] * 128 + core * 64, 64), :]
            first = bound + core * size
            border_grad[:, first : first + size, :] = block.reshape(parts, size, width)


def end_one_kernel(place, own, came_part, ret, ret_oth, send, feat_t, sums_one, sums_two, sums_out, *rest_refs):
    outs, second_chunk, term_one, term_two, grad_first = (
        rest_refs[0:4],
        rest_refs[4],
        rest_refs[5],
        rest_refs[6],
        rest_refs[7],
    )
    units = own.shape[0]
    step = pl.program_id(0)
    size = ROWS * pl.num_programs(0)
    parts = ret.shape[0]
    bound = send.shape[0] // parts
    width = feat_t.shape[0]
    chunk = 64 // parts

    @pl.when(step == 0)
    def _():
        term_one[...], term_two[...] = returned_terms(ret, ret_oth, bound, units)
        mine = pl.ds(bound + place[0] * chunk, chunk)
        second_chunk[...] = jnp.sum(ret[:, mine, :] + ret_oth[:, mine, :], axis=0)
        grad_first[...] = jnp.zeros(grad_first.shape, F32)

    base = place[0] * 2 * size + place[1] * size + step * ROWS
    d_z = round_gradient(own, came_part, (term_one, term_two), send[...], base)
    grad_first[:, 0:width] += dot_nt(d_z, feat_t[:, span(base, ROWS)])

    @pl.when(step == pl.num_programs(0) - 1)
    def _():
        lead = jnp.where(place[1] == 0, 1.0, 0.0)
        lane = lax.broadcasted_iota(I32, (64, 128), 1)
        for k, out in enumerate(outs):
            rows = span(jnp.bitwise_xor(place[0] + 2 * place[1], k) * 64, 64)
            value = grad_first[rows, :]
            value = jnp.where(lane == FLAG_LANE, sums_one[rows, :] * lead, value)
            value = jnp.where(lane == FLAG_LANE + 1, sums_two[rows, :] * lead, value)
            out[...] = jnp.where(lane == FLAG_LANE + 2, sums_out[...] * lead, value)


def gather_kernel(mine, one, two, three, second_chunk, last_chunk, out):
    total = mine[...] + one[...] + two[...] + three[...]
    size = second_chunk.shape[0]
    parts = [total]
    for chunk in (second_chunk, last_chunk):
        parts += [chunk[:, 0:128], chunk[:, 128:256]]
    value = jnp.concatenate(parts, axis=0)
    for p in range(out.shape[0]):
        out[p] = value


def adamw(weight, moment, square, gradient):
    moment = beta_one * moment + (1.0 - beta_one) * gradient
    square = beta_two * square + (1.0 - beta_two) * gradient * gradient
    moment_hat = moment / (1.0 - beta_one**STEP)
    square_hat = square / (1.0 - beta_two**STEP)
    weight = weight - rate_step * (
        moment_hat / (jnp.sqrt(square_hat) + epsilon) + decay_rate * weight
    )
    return (weight, moment, square)


def update_kernel(came, flags_t, *refs):
    params, outs = refs[0:15], refs[15:]
    parts = came.shape[0]
    size = 64 // parts
    width, kinds = params[0].shape[1], params[6].shape[0]
    total = jnp.sum(came[:, 0:64, :], axis=0)

    def chunks(first):
        halves = [
            came[:, first + k * size : first + (k + 1) * size, :].reshape(64, 128) for k in range(2)
        ]
        return jnp.concatenate(halves, axis=1)

    turned = jnp.concatenate([total, jnp.zeros((64, 128), F32)], axis=0).T
    gradients = (
        total[:, 0:width],
        chunks(64),
        chunks(64 + 2 * size)[0:kinds, :],
        turned[FLAG_LANE : FLAG_LANE + 2, 0:64],
        turned[FLAG_LANE + 2 : FLAG_LANE + 3, 0:kinds],
    )
    for k, gradient in enumerate(gradients):
        values = adamw(*[ref[...] for ref in params[3 * k : 3 * k + 3]], gradient)
        for ref, value in zip(outs[3 * k : 3 * k + 3], values):
            ref[...] = value
    padded = turned[FLAG_LANE + 2 : FLAG_LANE + 3, 48:49]
    outs[15][...] = jnp.broadcast_to(padded, (1, 128))
    outs[16][...] = jnp.broadcast_to(flags_t[3:4, 0:1], (1, 128))


def body(
    parts,
    reps,
    features,
    labels,
    train_mask,
    edge_src,
    edge_norm,
    send_rows,
    changed,
    cache_hidden,
    cache_out,
    first_weight,
    second_weight,
    last_weight,
    hidden_bias,
    out_bias,
    moment_first,
    moment_second,
    moment_last,
    moment_hidden,
    moment_out,
    square_first,
    square_second,
    square_last,
    square_hidden,
    square_out,
):
    nodes, in_width = features.shape
    half = nodes // 2
    bound = send_rows.shape[2]
    halo = parts * bound
    table = nodes + halo
    units, classes = last_weight.shape
    kinds = -(-classes // 16) * 16
    steps = half // ROWS

    rep = lax.axis_index("rep")
    place = jnp.stack([lax.rem(rep, 2), lax.div(rep, 2)]).astype(I32)
    where = (place, SMEM)
    feat_t = features.T
    send = send_rows.reshape(halo, 1)
    last_t = jnp.pad(last_weight.T, ((0, kinds - classes), (0, 0)))
    last_pad = last_t.T
    bias_out = jnp.pad(out_bias, (0, kinds - classes)).reshape(kinds, 1)
    label_rows = labels.reshape(2, half)
    mask_rows = train_mask.reshape(2, half)

    def swap(x, k=1):
        return lax.ppermute(x, "rep", [(i, i ^ k) for i in range(reps)])

    def exchange(x):
        return lax.all_to_all(x, "dom", split_axis=0, concat_axis=0, tiled=True)

    def late(x, after):
        return lax.optimization_barrier((x, after))

    node_block = lambda size, rows: pl.BlockSpec((rows, size), lambda i: (0, i))
    border_rows = lambda a: (a, pl.BlockSpec((ROWS, halo), lambda i: (i, nodes // halo)))
    work = 2 * half * table * units

    rows_out, pack = run(
        pack_kernel,
        "pack",
        1,
        [*wholes(feat_t, send), (changed, SMEM)]
        + wholes(
            train_mask.reshape(nodes // 128, 128),
            first_weight.T,
            second_weight.T,
            jnp.transpose(cache_hidden, (0, 2, 1)),
            hidden_bias,
        ),
        [((parts, bound, 128), BF16, None), ((units // reps, 256 + units + 2 * halo), BF16, None)],
        flops=2 * halo * nodes * 128,
    )
    rows = exchange(rows_out)
    packs = lax.all_gather(pack, "rep", axis=0, tiled=True)
    row_block = pl.BlockSpec((128, table), lambda i: (i, 0))
    high, rest = run(
        build_kernel,
        "build",
        half // 128,
        [where, *wholes(edge_src.T, edge_norm.T)],
        [((half, table), BF16, row_block), ((half, table), F8, row_block)],
        flops=4 * 256 * table * half,
    )
    in_hbm = [(high, HBM), (rest, HBM)]
    row_ring = ring_scratch((ROWS, table), (BF16, F8))
    scalar = pltpu.SMEM((1,), F32)
    block = node_block(ROWS, units)

    hidden_one, slope_one, z_own, z_send, flags_t = run(
        layer_one_kernel,
        "layer_one",
        steps,
        [where, *wholes(rows, feat_t, packs, send), *in_hbm],
        [
            ((units, half), BF16, block),
            ((units, half), F32, block),
            ((units, half), BF16, block),
            ((parts, bound, units), BF16, None),
            ((8, halo), F32, None),
        ],
        [pltpu.VMEM((units, table), BF16), pltpu.VMEM((units, table), F8), scalar, *row_ring],
        flops=work,
    )
    z_oth = swap(z_own)
    came = exchange(z_send)
    total, high8 = run(
        own_part_kernel,
        "layer_two_own",
        steps,
        [where, *in_hbm, *wholes(z_own, z_oth)],
        [((units, half), F32, block), ((half, table), F8, pl.BlockSpec((ROWS, table), lambda i: (i, 0)))],
        [pltpu.VMEM((units, nodes), BF16), pltpu.VMEM((units, nodes), F8), scalar, *row_ring],
        flops=work,
    )
    came, total = late(came, total)
    came_oth = swap(came)
    small = node_block(ROWS, kinds)
    border_scratch = lambda n: [pltpu.VMEM((n, halo), BF16), pltpu.VMEM((n, halo), F8), scalar]
    hidden_two, slope_two, z_own, z_send = run(
        layer_two_end_kernel,
        "layer_two_end",
        steps,
        [where, *wholes(flags_t, packs, send), border_rows(high), border_rows(rest), columns_of(total)]
        + wholes(came, came_oth, last_t),
        [
            ((units, half), BF16, block),
            ((units, half), F32, block),
            ((kinds, half), BF16, small),
            ((parts, bound, 128), BF16, None),
        ],
        border_scratch(units),
        flops=work // 4,
    )
    z_oth = swap(z_own)
    came = exchange(z_send)
    total = run(
        own_part_plain_kernel,
        "layer_three_own",
        steps,
        [where, *in_hbm, *wholes(z_own, z_oth)],
        [((kinds, half), F32, small)],
        [pltpu.VMEM((kinds, nodes), BF16), pltpu.VMEM((kinds, nodes), F8), scalar, *row_ring],
        flops=work,
    )[0]
    came, total = late(came, total)
    came_oth = swap(came)
    sums_out, grads, grads8, back, border_grad = run(
        functools.partial(loss_kernel, classes),
        "loss",
        steps,
        [where, whole(flags_t), border_rows(high), border_rows(rest), columns_of(total)]
        + wholes(came, came_oth, cache_out.T, bias_out, label_rows, mask_rows),
        [
            ((64, 128), F32, None),
            ((2 * kinds, half), BF16, node_block(ROWS, 2 * kinds)),
            ((kinds, half), F8, small),
            ((8, 128), F32, None),
            ((parts, bound, 128), F32, None),
        ],
        border_scratch(kinds) + [pltpu.VMEM((128, halo), F32)],
        flops=work // 4,
    )
    ret = exchange(border_grad)
    far, near = [
        run(
            functools.partial(back_three_kernel, other),
            "back_three",
            steps,
            [where, *in_hbm, *wholes(grads, grads8, back)],
            [((kinds, half), F32, small)],
            ring_scratch((half, ROWS), (BF16, F8)),
            flops=work // 2,
        )[0]
        for other in (True, False)
    ]
    far = swap(far)
    ret, near = late(ret, near)
    ret_oth = swap(ret)
    all_borders = [border_rows(high), border_rows(rest), border_rows(high8)]
    in_hbm3 = [*in_hbm, (high8, HBM)]
    chunk = 64 // parts

    def upstream_outs(extra):
        return [
            ((units, 128), F32, None),
            ((units, half), BF16, block),
            ((units, half), F8, block),
            ((units, half), F8, block),
            ((8, 128), F32, None),
            ((parts, bound + extra, units), F32, None),
        ]

    def end_scratch(n):
        return [pltpu.VMEM((units, halo), F32), pltpu.VMEM((n, halo), BF16), pltpu.VMEM((n, halo), BF16)]

    sums_two, grads, grads8, tails8, back, border_grad = run(
        end_three_kernel,
        "end_three",
        steps,
        [where, whole(flags_t), *all_borders, columns_of(near), columns_of(far)]
        + [*wholes(ret, ret_oth, send), columns_of(hidden_two), columns_of(slope_two), whole(last_pad)],
        upstream_outs(chunk),
        end_scratch(kinds) + [pltpu.VMEM((64, units), F32)],
        flops=work // 4,
    )
    ret = exchange(border_grad)

    def back_pair(halves):
        return [
            run(
                functools.partial(back_kernel, other, halves),
                "back",
                steps // halves,
                [where, *in_hbm3, *wholes(grads, grads8, tails8, back)],
                [((units, half // halves), F32, block)],
                ring_scratch((half, ROWS), (BF16, F8, F8)),
                flops=work // 2,
            )[0]
            for other in (True, False)
        ]

    far, near = back_pair(1)
    far = swap(far)
    ret, near = late(ret, near)
    ret_oth = swap(ret)
    sums_one, grads, grads8, tails8, back, border_grad, last_chunk = run(
        end_two_kernel,
        "end_two",
        steps,
        [where, *wholes(flags_t, packs), *all_borders, columns_of(near), columns_of(far)]
        + [*wholes(ret, ret_oth, send), columns_of(hidden_one), columns_of(slope_one)],
        [*upstream_outs(2 * chunk), ((chunk, units), F32, None)],
        end_scratch(units) + [pltpu.VMEM((units, units), F32)],
        flops=work // 4,
    )
    ret = exchange(border_grad)
    far, near = back_pair(2)
    far = swap(far)
    ret, near = late(ret, near)
    ret_oth = swap(ret)
    *pieces, second_chunk = run(
        end_one_kernel,
        "end_one",
        steps // 2,
        [where, columns_of(near), columns_of(far), *wholes(ret, ret_oth, send, feat_t, sums_one, sums_two, sums_out)],
        [((64, 128), F32, None)] * 4 + [((chunk, units), F32, None)],
        end_scratch(units)[1:] + [pltpu.VMEM((units, 128), F32)],
        flops=work // 8,
    )
    pieces = [piece if k == 0 else swap(piece, k) for k, piece in enumerate(pieces)]
    gathered = run(
        gather_kernel,
        "gather",
        1,
        wholes(*pieces, second_chunk, last_chunk),
        [((parts, 64 + 4 * chunk, 128), F32, None)],
    )[0]
    came = exchange(gathered)

    turn = lambda x: x.T
    same = lambda x: x
    row = lambda x: x.reshape(1, -1)
    forms = (turn, turn, turn, same, row)
    weights = (first_weight, second_weight, last_weight, hidden_bias, out_bias)
    moments = (moment_first, moment_second, moment_last, moment_hidden, moment_out)
    squares = (square_first, square_second, square_last, square_hidden, square_out)
    params = [form(x) for form, triple in zip(forms, zip(weights, moments, squares)) for x in triple]
    outs = run(
        update_kernel,
        "update",
        1,
        wholes(came, flags_t, *params),
        [(p.shape, F32, None) for p in params] + [((1, 128), F32, None)] * 2,
    )
    undo = (turn, turn, turn, same, lambda x: x.reshape(-1))
    results = [undo[k // 3](x) for k, x in enumerate(outs[0:15])]
    return (outs[15][0, 0], outs[16][0, 0], *results)


def solution(mesh):
    placed = (
        P("dom", None),
        P("dom"),
        P("dom"),
        P("dom", None),
        P("dom", None),
        P("dom", None, None),
        P(None, "dom"),
        P(None, "dom", "rep"),
        P("dom", None),
        P(None, "rep"),
        P(None, "rep"),
        P(),
        P(None, "rep"),
        P(),
        P(None, "rep"),
        P(None, "rep"),
        P(),
        P(None, "rep"),
        P(),
        P(None, "rep"),
        P(None, "rep"),
        P(),
        P(None, "rep"),
        P(),
    )
    return jax.shard_map(
        functools.partial(body, mesh.shape["dom"], mesh.shape["rep"]),
        mesh=mesh,
        in_specs=placed,
        out_specs=(P(), P()) + (P(None, "rep"),) * 6 + (P(),) * 3 + (P(None, "rep"),) * 3 + (P(),) * 3,
        check_vma=False,
    )
```

```python
import functools

import jax
import jax.numpy as jnp
from jax import lax
from jax.experimental import pallas as pl
from jax.experimental.pallas import tpu as pltpu
from jax.sharding import PartitionSpec as P

STEP = 5
beta_one = 0.5
beta_two = 0.5
rate_step = 0.03
decay_rate = 0.01
epsilon = 1e-08

BF16, F32, F8, I32 = jnp.bfloat16, jnp.float32, jnp.float8_e4m3fn, jnp.int32
REST_GAIN = 4096.0
TAIL_GAIN = 256.0
FLAG_LANE = 100
ROWS = 512
FINE = 256
AHEAD = 3
LIMIT = 52 << 20

SMEM = pl.BlockSpec(memory_space=pltpu.SMEM)
VMEM = pl.BlockSpec(memory_space=pltpu.VMEM)
OWN = pl.BlockSpec(memory_space=pltpu.VMEM)
HBM = pl.BlockSpec(memory_space=pltpu.HBM)
ANY = pl.BlockSpec(memory_space=pl.ANY)


def whole_spec(shape):
    return pl.BlockSpec(shape, lambda *_: (0,) * len(shape))


def placed(spec, *arrays):
    return [(a, spec) for a in arrays]


def run(kernel, name, args, outs, scratch=(), flops=0, grid=()):
    pinned = [
        a if any(spec is s for s in (SMEM, VMEM, ANY)) else pltpu.with_memory_space_constraint(a, pltpu.HBM)
        for a, spec in args
    ]
    return pl.pallas_call(
        kernel,
        grid=grid,
        in_specs=[spec for _, spec in args],
        out_specs=[spec for _, _, spec in outs],
        out_shape=[
            jax.ShapeDtypeStruct(shape, kind) if spec is VMEM else pltpu.HBM(shape, kind)
            for shape, kind, spec in outs
        ],
        scratch_shapes=list(scratch),
        name=name,
        cost_estimate=pl.CostEstimate(flops=flops, bytes_accessed=1 << 20, transcendentals=0),
        compiler_params=pltpu.CompilerParams(vmem_limit_bytes=LIMIT),
    )(*pinned)


def dot_nn(left, right):
    return lax.dot_general(left, right, (((1,), (0,)), ((), ())), preferred_element_type=F32)


def dot_nt(left, right):
    return lax.dot_general(left, right, (((1,), (1,)), ((), ())), preferred_element_type=F32)


def dot_tn(left, right):
    return lax.dot_general(left, right, (((0,), (0,)), ((), ())), preferred_element_type=F32)


def scale_of(value):
    most = jnp.maximum(jnp.max(jnp.abs(value)), 1e-30)
    return 256.0 / most, most * (1.0 / 256.0)


def span(start, size):
    return pl.ds(pl.multiple_of(start, size), size)


def rows_at(size, cols=slice(None)):
    return lambda i: (span(i * size, size), cols)


def cols_at(size, base=0):
    return lambda i: (slice(None), span(base + i * size, size))


def all_of(i):
    return (slice(None), slice(None))


def loop(count, step):
    def one(i, carry):
        step(i)
        return carry

    lax.fori_loop(0, count, one, 0)


class Ring:
    def __init__(self, refs, bufs, sems, cut, first=0):
        self.refs, self.bufs, self.sems, self.cut = refs, bufs, sems, cut
        self.begins = pl.program_id(0) == 0
        self.step, self.steps = pl.program_id(0) - first, pl.num_programs(0) - first
        self.depth = bufs[0].shape[0]
        self.slot = lax.rem(self.step, self.depth)

    def copies(self, step, slot):
        return [
            pltpu.make_async_copy(ref.at[self.cut(step)], buf.at[slot], self.sems.at[k, slot])
            for k, (ref, buf) in enumerate(zip(self.refs, self.bufs))
        ]

    def begin(self):
        for step in range(self.depth):

            @pl.when(self.begins & (step < self.steps))
            def _():
                for copy in self.copies(step, step):
                    copy.start()

    def wait(self):
        for copy in self.copies(self.step, self.slot):
            copy.wait()
        return [buf.at[self.slot] for buf in self.bufs]

    def end(self):
        @pl.when(self.step + self.depth < self.steps)
        def _():
            for copy in self.copies(self.step + self.depth, self.slot):
                copy.start()


def ring_scratch(shape, depth=3):
    kinds = (BF16, F8)
    return [pltpu.VMEM((depth, *shape), kind) for kind in kinds] + [pltpu.SemaphoreType.DMA((len(kinds), depth))]


class Stream:
    def __init__(self, sems, *legs):
        self.sems, self.legs = sems, legs

    def copies(self, i):
        return [
            pltpu.make_async_copy(source.at[source_at(i)], target.at[target_at(i)], self.sems.at[k, i])
            for k, (source, source_at, target, target_at) in enumerate(self.legs)
        ]

    def start(self, i):
        for copy in self.copies(i):
            copy.start()

    def wait(self, i):
        for copy in self.copies(i):
            copy.wait()

    def wait_all(self, count):
        loop(count, self.wait)

    def start_first(self, count):
        for i in range(min(AHEAD, count)):
            self.start(i)

    def next(self, i, count):
        self.wait(i)

        @pl.when(i + AHEAD < count)
        def _():
            self.start(i + AHEAD)


def sems(legs, count):
    return pltpu.SemaphoreType.DMA((legs, count))


def pick_rows(send, first, count):
    nodes = lax.broadcasted_iota(I32, (send.shape[0], count), 1) + first
    return jnp.where(send == nodes, 1.0, 0.0).astype(BF16)


def pack_kernel(feat_t, send_list, changed, mask, first_t, second_t, cache_t, bias, rows_out, pack_out, send):
    nodes, halo = feat_t.shape[1], send.shape[0]
    parts, bound = send_list.shape
    turned = send_list[...].astype(F32)
    turned = jnp.concatenate([turned, jnp.zeros((parts, 128 - bound), F32)], axis=1)
    turned = turned.T.astype(I32)
    for q in range(parts):
        send[q * bound : (q + 1) * bound, :] = turned[0:bound, q : q + 1]
    width, cols = feat_t.shape[0], first_t.shape[0]

    def pick(i, total):
        return total + dot_nt(pick_rows(send[...], i * ROWS, ROWS), feat_t[:, span(i * ROWS, ROWS)])

    total = lax.fori_loop(0, nodes // ROWS, pick, jnp.zeros((halo, width), F32))
    count = jnp.sum(mask[...].astype(F32))
    many = jnp.floor(count * (1.0 / 64.0))
    lane = lax.broadcasted_iota(I32, (halo, 128), 1)
    row = jnp.concatenate([total, jnp.zeros((halo, 128 - width), F32)], axis=1)
    for layer in range(3):
        row = jnp.where(lane == FLAG_LANE + layer, changed[0, layer].astype(F32), row)
    row = jnp.where(lane == FLAG_LANE + 3, many, row)
    row = jnp.where(lane == FLAG_LANE + 4, count - 64.0 * many, row)
    rows_out[...] = row.astype(BF16).reshape(rows_out.shape)

    units = second_t.shape[1]
    pack_out[:, 0:128] = jnp.concatenate(
        [first_t[...], jnp.zeros((cols, 128 - width), F32)], axis=1
    ).astype(BF16)
    pack_out[:, 128 : 128 + units] = second_t[...].astype(BF16)
    left = jnp.concatenate([bias[...], jnp.zeros((2, 128 - cols), F32)], axis=1)
    terms = []
    for _ in range(3):
        term = left.astype(BF16).astype(F32)
        terms.append(term)
        left = left - term
    terms = jnp.concatenate(terms + [jnp.zeros((122, 128), F32)], axis=0).T
    pack_out[:, 128 + units : 256 + units] = terms[0:cols, :].astype(BF16)
    base = 256 + units
    for layer in range(2):
        pack_out[:, base + layer * halo : base + (layer + 1) * halo] = cache_t[layer]


def bias_column(packs, layer):
    units = packs.shape[0]
    terms = packs[:, 128 + units : 256 + units].astype(F32)
    return terms[:, layer : layer + 1] + terms[:, layer + 2 : layer + 3] + terms[:, layer + 4 : layer + 5]


def stale_columns(packs, layer, halo):
    base = 256 + packs.shape[0] + layer * halo
    return packs[:, base : base + halo].astype(F32)


def build_kernel(place, src_t, norm_t, high_hbm, rest_hbm, high, rest, out_sems):
    slots = src_t.shape[0]
    half = src_t.shape[1] // 2
    blocks = high.shape[1] // 256
    per_group = 256 // slots
    in_slot = lax.broadcasted_iota(I32, (8, 128), 1) // per_group == lax.broadcasted_iota(I32, (8, 128), 0)
    node_row = lax.broadcasted_iota(I32, (per_group, 256), 0)
    mine = lax.rem(lax.broadcasted_iota(I32, (per_group, 256), 1), per_group) == node_row
    inner = lax.broadcasted_iota(I32, (256, 256), 0)
    stores = Stream(out_sems, (high, rows_at(128), high_hbm, rows_at(128)), (rest, rows_at(128), rest_hbm, rows_at(128)))

    def lean(tile):
        return [
            pltpu.roll(tile[first : first + 8, :], 0, 1, stride=per_group, stride_axis=0)
            for first in range(0, slots, 8)
        ]

    def flat(tiles, group):
        moved = [pltpu.roll(tile, (128 - per_group * group) % 128, 1) for tile in tiles]
        return jnp.concatenate(
            [jnp.sum(jnp.where(in_slot, tile, 0), axis=0, keepdims=True) for tile in moved], axis=1
        )

    def one(at, weight):
        weight_high = weight.astype(BF16).astype(F32)
        hit = inner == jnp.bitwise_and(at, 255)
        right = jnp.where(hit, weight_high, 0.0).astype(BF16)
        right_rest = jnp.where(hit, (weight - weight_high) * REST_GAIN, 0.0).astype(BF16)
        block = jnp.where(mine, jnp.right_shift(at, 8), -1)
        left = jnp.concatenate(
            [jnp.where(block == j, 1.0, 0.0).astype(BF16) for j in range(blocks)], axis=0
        )
        return dot_nt(left, right), dot_nt(left, right_rest)

    def step(i):
        here = span(place[0] * half + i * 128, 128)
        at, weight = src_t[:, here], norm_t[:, here]
        slot = lax.broadcasted_iota(I32, at.shape, 0)
        merged, repeat = weight, slot < 0
        for shift in range(1, slots):
            same = at == pltpu.roll(at, shift, 0)
            merged = merged + jnp.where(same, pltpu.roll(weight, shift, 0), 0.0)
            repeat = repeat | (same & (slot >= shift))
        source, weights = lean(at), lean(jnp.where(repeat, 0.0, merged))
        pairs = [one(flat(source, group), flat(weights, group)) for group in range(128 // per_group)]
        rows = span(i * 128, 128)
        for j in range(blocks):
            cols = slice(256 * j, 256 * (j + 1))
            for ref, parts in zip((high, rest), zip(*pairs)):
                piece = jnp.concatenate([p[per_group * j : per_group * (j + 1), :] for p in parts], axis=0)
                ref[rows, cols] = piece.astype(ref.dtype)
        stores.start(i)

    loop(half // 128, step)
    stores.wait_all(half // 128)


def gelu_both(u):
    square = u * u
    t = jnp.tanh(0.79788456 * (u + 0.044715 * u * square))
    half = 0.5 * (1.0 + t)
    slope = half + 0.5 * u * (1.0 - t * t) * (0.79788456 * (1.0 + 3.0 * 0.044715 * square))
    return u * half, slope


def layer_one_kernel(place, rows, feat_t, pack, pack_one, pack_two, pack_three, send, high, rest, packs, hidden_t, slope_t, z_own, z_send, flags_t, table, table8, back, hbuf, rbuf, sems):
    width, nodes = feat_t.shape
    halo = send.shape[0]
    step = pl.program_id(0)
    ring = Ring((high, rest), (hbuf, rbuf), sems, lambda i: (span(i * ROWS, ROWS), slice(None)))
    ring.begin()

    @pl.when(step == 0)
    def _():
        for k, ref in enumerate((pack, pack_one, pack_two, pack_three)):
            packs[span(jnp.bitwise_xor(place[0] + 2 * place[1], k) * 64, 64), :] = ref[...]
        weight = packs[:, 0:width]
        flat = rows[...].reshape(halo, 128)
        flags = flat.astype(F32).T[FLAG_LANE : FLAG_LANE + 8, :]
        counts = jnp.sum(rows[...].astype(F32)[:, 0, :], axis=0, keepdims=True)
        count = 64.0 * counts[:, FLAG_LANE + 3 : FLAG_LANE + 4] + counts[:, FLAG_LANE + 4 : FLAG_LANE + 5]
        row = lax.broadcasted_iota(I32, flags.shape, 0)
        flags_t[...] = jnp.where(row == 3, count, flags)

        def first(i, most):
            here = span(i * ROWS, ROWS)
            z = dot_nn(weight, feat_t[:, here])
            table[:, here] = z.astype(BF16)
            return jnp.maximum(most, jnp.abs(z))

        most = lax.fori_loop(0, nodes // ROWS, first, jnp.zeros((table.shape[0], ROWS), F32))
        border = dot_nt(weight, flat[:, 0:width]).astype(BF16).astype(F32)
        border = jnp.where(flags[0:1, :] == 1.0, border, stale_columns(packs, 0, halo))
        table[:, nodes : nodes + halo] = border.astype(BF16)
        scale, inverse = scale_of(jnp.maximum(jnp.max(most), jnp.max(jnp.abs(border))))
        back[0] = inverse * (1.0 / REST_GAIN)

        def small(i, carry):
            here = span(i * 256, 256)
            table8[:, here] = (table[:, here].astype(F32) * scale).astype(F8)
            return carry

        lax.fori_loop(0, (nodes + halo) // 256, small, 0)
        z_send[...] = jnp.zeros(z_send.shape, BF16)

    units = packs.shape[0]
    top, low = ring.wait()
    total = dot_nt(table[...], top[...]) + dot_nt(table8[...], low[...]) * back[0]
    ring.end()
    value, slope = gelu_both(total + bias_column(packs, 0))
    value = value.astype(BF16)
    hidden_t[...] = value
    slope_t[...] = slope
    z = dot_nn(packs[:, 128 : 128 + units], value).astype(BF16)
    z_own[...] = z
    half = nodes // 2
    chosen = dot_nt(pick_rows(send[...], place[0] * half + step * ROWS, ROWS), z)
    z_send[...] = (z_send[...].astype(F32) + chosen.reshape(z_send.shape)).astype(BF16)


def own_part_kernel(place, high, rest, z_own, z_oth, total, table, table8, back, hbuf, rbuf, sems):
    half = z_own.shape[1]
    nodes = 2 * half
    ring = Ring((high, rest), (hbuf, rbuf), sems, lambda i: (span(i * FINE, FINE), slice(0, nodes)))
    ring.begin()

    @pl.when(pl.program_id(0) == 0)
    def _():
        def larger(i, most):
            here = span(i * ROWS, ROWS)
            both = jnp.maximum(jnp.abs(z_own[:, here].astype(F32)), jnp.abs(z_oth[:, here].astype(F32)))
            return jnp.maximum(most, both)

        most = lax.fori_loop(0, half // ROWS, larger, jnp.zeros((z_own.shape[0], ROWS), F32))
        scale, inverse = scale_of(most)
        back[0] = inverse * (1.0 / REST_GAIN)
        for ref, first in ((z_own, place[0] * half), (z_oth, (1 - place[0]) * half)):

            def put(i, carry):
                value = ref[:, span(i * ROWS, ROWS)]
                cols = span(first + i * ROWS, ROWS)
                table[:, cols] = value
                table8[:, cols] = (value.astype(F32) * scale).astype(F8)
                return carry

            lax.fori_loop(0, half // ROWS, put, 0)

    top, low = ring.wait()
    total[...] = dot_nt(table[...], top[...]) + dot_nt(table8[...], low[...]) * back[0]
    ring.end()


def padded_rows(ref, count):
    value = ref[...]
    extra = jnp.zeros((count - value.shape[0], value.shape[1]), value.dtype)
    return jnp.concatenate([value, extra], axis=0).astype(BF16)


def border_cut(nodes, halo):
    return lambda i: (span(i * ROWS, ROWS), slice(nodes, nodes + halo))


def layer_two_end_kernel(place, flags_t, packs, send, high, rest, total, came, came_oth, last_t, hidden_t, slope_t, z_own, z_send, border, border8, back):
    halo = send.shape[0]
    width = hidden_t.shape[0]
    kinds = z_own.shape[0]
    step = pl.program_id(0)
    half = ROWS * pl.num_programs(0)

    @pl.when(step == 0)
    def _():
        both = came[...].reshape(halo, width).astype(F32) + came_oth[...].reshape(halo, width).astype(F32)
        value = jnp.where(flags_t[1:2, :] == 1.0, both.T, stale_columns(packs, 1, halo))
        scale, inverse = scale_of(value)
        border[...] = value.astype(BF16)
        border8[...] = (value * scale).astype(F8)
        back[0] = inverse * (1.0 / REST_GAIN)
        z_send[...] = jnp.zeros(z_send.shape, BF16)

    sums = total[...] + dot_nt(border[...], high[...]) + dot_nt(border8[...], rest[...]) * back[0]
    value, slope = gelu_both(sums + bias_column(packs, 1))
    value = value.astype(BF16)
    hidden_t[...] = value
    slope_t[...] = slope
    z = dot_nn(padded_rows(last_t, kinds), value).astype(BF16)
    z_own[...] = z
    chosen = dot_nt(pick_rows(send[...], place[0] * half + step * ROWS, ROWS), z)
    chosen = jnp.concatenate([chosen, jnp.zeros((halo, 128 - kinds), F32)], axis=1)
    z_send[...] = (z_send[...].astype(F32) + chosen.reshape(z_send.shape)).astype(BF16)


def put_border(border_grad, total, keep):
    value = (total * keep).T
    bound = value.shape[0] // border_grad.shape[0]
    border_grad[:, 0:bound, :] = value.reshape(border_grad.shape[0], bound, value.shape[1])


def loss_kernel(classes, place, flags_t, came, came_oth, stale_t, bias, labels, mask, total_hbm, high, rest, sums, back_out, border_grad, grads_hbm, grads8_hbm, far_hbm, border_sum, hrows, rrows, total, grads, grads8, far, hbuf, rbuf, in_sems, edge_sems, out_sems, far_sems):
    kinds, half = total.shape
    halo = stale_t.shape[1]
    steps = half // ROWS
    cut = border_cut(2 * half, halo)
    blocks = Stream(
        in_sems,
        (high, cut, hrows, rows_at(ROWS)),
        (rest, cut, rrows, rows_at(ROWS)),
        (total_hbm, cols_at(ROWS), total, cols_at(ROWS)),
    )
    others = cols_at(ROWS, (1 - place[0]) * half)
    edges = Stream(edge_sems, (high, others, hbuf, cols_at(ROWS)), (rest, others, rbuf, cols_at(ROWS)))
    stores = Stream(
        out_sems, *[(a, cols_at(ROWS), b, cols_at(ROWS)) for a, b in ((grads, grads_hbm), (grads8, grads8_hbm))]
    )
    far_stores = Stream(far_sems, (far, cols_at(ROWS), far_hbm, cols_at(ROWS)))
    blocks.start_first(steps)
    both = came[...].reshape(halo, 128).astype(F32) + came_oth[...].reshape(halo, 128).astype(F32)
    old = jnp.concatenate([stale_t[...].astype(F32), jnp.zeros((kinds - classes, halo), F32)], axis=0)
    value = jnp.where(flags_t[2:3, :] == 1.0, both.T[0:kinds, :], old)
    scale, back = scale_of(value)
    back = back * (1.0 / REST_GAIN)
    border = value.astype(BF16)
    border8 = (value * scale).astype(F8)
    row = jnp.concatenate([bias[...], jnp.zeros((1, 128 - classes), F32)], axis=1)
    bias_col = jnp.broadcast_to(row, (8, 128)).T[0:kinds, 0:1]
    sums[...] = jnp.zeros(sums.shape, F32)
    border_sum[...] = jnp.zeros(border_sum.shape, F32)
    count = flags_t[3:4, 0:1]
    inverse = (1.0 / (256.0 * REST_GAIN)) / count
    back_out[...] = jnp.broadcast_to(inverse, back_out.shape)

    def step(i):
        blocks.next(i, steps)
        edges.start(i)
        here = span(i * ROWS, ROWS)
        logits = total[:, here] + dot_nt(border, hrows[here, :]) + dot_nt(border8, rrows[here, :]) * back
        logits = logits + bias_col
        kind = lax.broadcasted_iota(I32, logits.shape, 0)
        real = kind < classes
        logits = jnp.where(real, logits, -jnp.inf)
        shifted = logits - jnp.max(logits, axis=0, keepdims=True)
        powers = jnp.exp(shifted)
        norm = jnp.sum(powers, axis=0, keepdims=True)
        logp = jnp.where(real, shifted - jnp.log(norm), 0.0)
        first = (place[0] * steps + i) * (ROWS // 128)
        row_of = lambda ref: jnp.concatenate([ref[pl.ds(first + k, 1), :] for k in range(ROWS // 128)], axis=1)
        target = jnp.where(kind == row_of(labels), 0.9, 0.0) + 0.1 / classes
        used = row_of(mask).astype(F32)
        loss = jnp.sum(target * logp, axis=0, keepdims=True) * used
        grad = jnp.where(real, (powers / norm - target) * (used / count), 0.0)
        sums[0:kinds, :] += lane_sums(grad)
        sums[kinds : kinds + 1, :] -= lane_sums(loss)
        top = grad.astype(BF16)
        tail = (grad - top.astype(F32)).astype(BF16)
        stacked = jnp.concatenate([top, tail], axis=0)
        small = (top.astype(F32) * (256.0 * count)).astype(F8)
        grads[:, here] = stacked
        grads8[:, here] = small
        stores.start(i)
        both = dot_nn(stacked, hrows[here, :])
        low = dot_nn(small, rrows[here, :]) * inverse
        border_sum[0:kinds, :] += both[0:kinds] + both[kinds : 2 * kinds] + low

    loop(steps, step)
    put_border(border_grad, border_sum[...], flags_t[2:3, :])

    def far_step(i):
        edges.wait(i)
        here = span(i * ROWS, ROWS)
        both = dot_nn(grads[...], hbuf[:, here])
        far[:, here] = both[0:kinds] + both[kinds : 2 * kinds] + dot_nn(grads8[...], rbuf[:, here]) * inverse
        far_stores.start(i)

    loop(steps, far_step)
    stores.wait_all(steps)
    far_stores.wait_all(steps)


def lane_sums(value):
    total = value[:, 0:128]
    for first in range(128, value.shape[1], 128):
        total = total + value[:, first : first + 128]
    return total


def back_three_kernel(place, high, rest, grads, grads8, back, out, hbuf, rbuf, sems):
    kinds, size = out.shape
    base = place[0] * size * pl.num_programs(0)
    ring = Ring((high, rest), (hbuf, rbuf), sems, lambda i: (slice(None), span(base + i * size, size)))
    ring.begin()
    top, low = ring.wait()
    both = dot_nn(grads[...], top[...])
    out[...] = both[0:kinds] + both[kinds : 2 * kinds] + dot_nn(grads8[...], low[...]) * back[0:1, 0:1]
    ring.end()


def back_block(grads, grads8, tails8, back_rest, back_tail, top, low):
    total = dot_nn(grads[...], top) + dot_nn(grads8[...], low) * back_rest
    return total + dot_nn(tails8[...], top.astype(F8)) * back_tail


def back_kernel(halves, place, high, rest, grads, grads8, tails8, back, *refs):
    *outs, hbuf, rbuf, sems = refs
    size = outs[0].shape[1]
    steps = pl.num_programs(0) // len(outs)
    base = place[1] * size * steps if halves == 2 else 0

    def cut(i):
        owner = jnp.where(i < steps * (len(outs) - 1), 1 - place[0], place[0])
        return slice(None), span(owner * size * steps * halves + base + lax.rem(i, steps) * size, size)

    ring = Ring((high, rest), (hbuf, rbuf), sems, cut)
    ring.begin()
    top, low = ring.wait()
    total = back_block(grads, grads8, tails8, back[0:1, 0:1], back[0:1, 1:2], top[...], low[...])
    for k, out in enumerate(outs):

        @pl.when((ring.step >= k * steps) & (ring.step < (k + 1) * steps))
        def _():
            out[...] = total

    ring.end()


def returned_terms(ret, ret_oth, bound, kinds):
    value = ret[:, 0:bound, :] + ret_oth[:, 0:bound, :]
    value = value.reshape(value.shape[0] * bound, value.shape[2]).T[0:kinds, :]
    top = value.astype(BF16)
    return top, (value - top.astype(F32)).astype(BF16)


def round_gradient(own, came_part, terms, send, first_node):
    chosen = pick_rows(send, first_node, own.shape[1])
    total = own + came_part
    for term in terms:
        total = total + dot_nn(term, chosen)
    return total.astype(BF16)


def end_kernel(layer, place, flags_t, ret, ret_oth, weight_ref, send, far_in_any, near_hbm, hidden_hbm, slope_hbm, high, rest, sums, back_out, border_grad, chunk_out, grads_hbm, grads8_hbm, tails8_hbm, *more):
    if layer == 1:
        far_hbm, far, hbuf, rbuf, edge_sems, far_sems = more[0], *more[-5:]
        more = more[1:-5]
    near, far_in, hidden_t, slope_t, hrows, rrows, grad_rows, grad_weight, border_sum, grads, grads8, tails8, in_sems, row_sems, out_sems = more
    kinds, half = near.shape
    units = slope_t.shape[0]
    parts = ret.shape[0]
    bound = send.shape[0] // parts
    halo = send.shape[0]
    steps = half // ROWS
    size = 64 // parts
    cut = border_cut(2 * half, halo)
    blocks = Stream(
        in_sems,
        *[
            (a, cols_at(ROWS), b, cols_at(ROWS))
            for a, b in ((near_hbm, near), (far_in_any, far_in), (hidden_hbm, hidden_t), (slope_hbm, slope_t))
        ],
    )
    borders = Stream(row_sems, (high, cut, hrows, rows_at(ROWS)), (rest, cut, rrows, rows_at(ROWS)))
    stores = Stream(
        out_sems,
        *[
            (a, cols_at(ROWS), b, cols_at(ROWS))
            for a, b in ((grads, grads_hbm), (grads8, grads8_hbm), (tails8, tails8_hbm))
        ],
    )
    if layer == 1:
        others = cols_at(ROWS, (1 - place[0]) * half)
        edges = Stream(edge_sems, (high, others, hbuf, cols_at(ROWS)), (rest, others, rbuf, cols_at(ROWS)))
        far_stores = Stream(far_sems, (far, cols_at(ROWS), far_hbm, cols_at(ROWS)))
    blocks.start_first(steps)
    terms = returned_terms(ret, ret_oth, bound, kinds)
    if layer == 0:
        chunk_out[...] = jnp.sum(ret[:, bound:, :] + ret_oth[:, bound:, :], axis=0)
        weight = weight_ref[:, 128 : 128 + units]
    else:
        chunk_out[...] = jnp.zeros(chunk_out.shape, F32)
        weight = padded_rows(weight_ref, kinds)
    sums[...] = jnp.zeros(sums.shape, F32)
    grad_weight[...] = jnp.zeros(grad_weight.shape, F32)
    border_sum[...] = jnp.zeros(border_sum.shape, F32)

    def first_step(i, most):
        blocks.next(i, steps)
        borders.start(i)
        here = span(i * ROWS, ROWS)
        d_z = round_gradient(near[:, here], far_in[:, here], terms, send[...], (place[0] * steps + i) * ROWS)
        grad_weight[0:kinds, :] += dot_nt(d_z, hidden_t[:, here])
        grad = dot_tn(weight, d_z) * slope_t[:, here]
        sums[...] += lane_sums(grad)
        grad_rows[:, here] = grad
        return jnp.maximum(most, jnp.max(jnp.abs(grad), axis=0, keepdims=True))

    most = lax.fori_loop(0, steps, first_step, jnp.zeros((1, ROWS), F32))
    if layer == 1:
        edges.start_first(steps)
    scale, back = scale_of(most)
    back_rest, back_tail = back * (1.0 / REST_GAIN), back * (1.0 / TAIL_GAIN)
    lane = lax.broadcasted_iota(I32, back_out.shape, 1)
    back_out[...] = jnp.where(lane == 0, back_rest, back_tail)

    def second_step(i):
        borders.wait(i)
        here = span(i * ROWS, ROWS)
        grad = grad_rows[:, here]
        top = grad.astype(BF16)
        wide = top.astype(F32)
        small = (wide * scale).astype(F8)
        tail = ((grad - wide) * (scale * TAIL_GAIN)).astype(F8)
        grads[:, here] = top
        grads8[:, here] = small
        tails8[:, here] = tail
        stores.start(i)
        border_sum[...] += back_block(top, small, tail, back_rest, back_tail, hrows[here, :], rrows[here, :])

    loop(steps, second_step)
    put_border(border_grad, border_sum[...], flags_t[layer : layer + 1, :])
    if layer == 1:
        border_grad[:, bound:, :] = grad_weight[...].reshape(parts, size, units)
    else:
        for core in range(2):
            block = grad_weight[span(place[1] * 128 + core * 64, 64), :]
            first = bound + core * size
            border_grad[:, first : first + size, :] = block.reshape(parts, size, units)

    def far_step(i):
        edges.next(i, steps)
        here = span(i * ROWS, ROWS)
        far[:, here] = back_block(grads, grads8, tails8, back_rest, back_tail, hbuf[:, here], rbuf[:, here])
        far_stores.start(i)

    if layer == 1:
        loop(steps, far_step)
        far_stores.wait_all(steps)
    stores.wait_all(steps)


def end_one_kernel(place, ret, ret_oth, send, sums_one, sums_two, sums_out, far_any, near_hbm, feat_hbm, out, out_one, out_two, out_three, second_chunk, near, far, feat_t, grad_first, in_sems):
    units, size = near.shape
    parts = ret.shape[0]
    bound = send.shape[0] // parts
    width = feat_t.shape[0]
    chunk = 64 // parts
    steps = size // ROWS
    base = place[0] * 2 * size + place[1] * size
    blocks = Stream(
        in_sems,
        (near_hbm, cols_at(ROWS), near, cols_at(ROWS)),
        (far_any, cols_at(ROWS), far, cols_at(ROWS)),
        (feat_hbm, cols_at(ROWS, base), feat_t, cols_at(ROWS)),
    )
    blocks.start_first(steps)
    terms = returned_terms(ret, ret_oth, bound, units)
    mine = pl.ds(bound + place[0] * chunk, chunk)
    second_chunk[...] = jnp.sum(ret[:, mine, :] + ret_oth[:, mine, :], axis=0)
    grad_first[...] = jnp.zeros(grad_first.shape, F32)

    def step(i):
        blocks.next(i, steps)
        here = span(i * ROWS, ROWS)
        d_z = round_gradient(near[:, here], far[:, here], terms, send[...], base + i * ROWS)
        grad_first[:, 0:width] += dot_nt(d_z, feat_t[:, here])

    loop(steps, step)
    lead = jnp.where(place[1] == 0, 1.0, 0.0)
    lane = lax.broadcasted_iota(I32, (64, 128), 1)
    column = lambda value: jnp.sum(value, axis=1, keepdims=True) * lead
    for k, ref in enumerate((out, out_one, out_two, out_three)):
        rows = span(jnp.bitwise_xor(place[0] + 2 * place[1], k) * 64, 64)
        value = grad_first[rows, :]
        value = jnp.where(lane == FLAG_LANE, column(sums_one[rows, :]), value)
        value = jnp.where(lane == FLAG_LANE + 1, column(sums_two[rows, :]), value)
        ref[...] = jnp.where(lane == FLAG_LANE + 2, column(sums_out[...]), value)


def gather_kernel(mine, one, two, three, second_chunk, last_chunk, out):
    total = mine[...] + one[...] + two[...] + three[...]
    size = second_chunk.shape[0]
    parts = [total]
    for chunk in (second_chunk, last_chunk):
        parts += [chunk[:, 0:128], chunk[:, 128:256]]
    value = jnp.concatenate(parts, axis=0)
    for p in range(out.shape[0]):
        out[p] = value


def adamw(weight, moment, square, gradient):
    moment = beta_one * moment + (1.0 - beta_one) * gradient
    square = beta_two * square + (1.0 - beta_two) * gradient * gradient
    moment_hat = moment / (1.0 - beta_one**STEP)
    square_hat = square / (1.0 - beta_two**STEP)
    weight = weight - rate_step * (
        moment_hat / (jnp.sqrt(square_hat) + epsilon) + decay_rate * weight
    )
    return (weight, moment, square)


def update_kernel(came, flags_t, *refs):
    params, outs = refs[0:15], refs[15:]
    parts = came.shape[0]
    size = 64 // parts
    width, kinds = params[0].shape[1], params[6].shape[0]
    total = jnp.sum(came[:, 0:64, :], axis=0)

    def chunks(first):
        halves = [
            came[:, first + k * size : first + (k + 1) * size, :].reshape(64, 128) for k in range(2)
        ]
        return jnp.concatenate(halves, axis=1)

    turned = jnp.concatenate([total, jnp.zeros((64, 128), F32)], axis=0).T
    gradients = (
        total[:, 0:width],
        chunks(64),
        chunks(64 + 2 * size)[0:kinds, :],
        turned[FLAG_LANE : FLAG_LANE + 2, 0:64],
        turned[FLAG_LANE + 2 : FLAG_LANE + 3, 0:kinds],
    )
    for k, gradient in enumerate(gradients):
        values = adamw(*[ref[...] for ref in params[3 * k : 3 * k + 3]], gradient)
        for ref, value in zip(outs[3 * k : 3 * k + 3], values):
            ref[...] = value
    padded = turned[FLAG_LANE + 2 : FLAG_LANE + 3, 48:49]
    outs[15][...] = jnp.broadcast_to(padded, (1, 128))
    outs[16][...] = jnp.broadcast_to(flags_t[3:4, 0:1], (1, 128))


def body(
    parts,
    reps,
    features,
    labels,
    train_mask,
    edge_src,
    edge_norm,
    send_rows,
    changed,
    cache_hidden,
    cache_out,
    first_weight,
    second_weight,
    last_weight,
    hidden_bias,
    out_bias,
    moment_first,
    moment_second,
    moment_last,
    moment_hidden,
    moment_out,
    square_first,
    square_second,
    square_last,
    square_hidden,
    square_out,
):
    nodes, in_width = features.shape
    half = nodes // 2
    bound = send_rows.shape[2]
    halo = parts * bound
    table = nodes + halo
    units, classes = last_weight.shape
    kinds = -(-classes // 16) * 16
    steps, fine = half // ROWS, half // FINE

    rep = lax.axis_index("rep")
    place = jnp.stack([lax.rem(rep, 2), lax.div(rep, 2)]).astype(I32)
    where = (place, SMEM)
    feat_t = features.T
    last_t = last_weight.T
    label_rows = labels.reshape(nodes // 128, 128)
    mask_rows = train_mask.reshape(nodes // 128, 128)

    def swap(x, k=1):
        return lax.ppermute(x, "rep", [(i, i ^ k) for i in range(reps)])

    def exchange(x):
        return lax.all_to_all(x, "dom", split_axis=0, concat_axis=0, tiled=True)

    def late(after, *arrays):
        return lax.optimization_barrier((*arrays, after))

    vm = pltpu.VMEM
    whole = lambda a: (a, whole_spec(a.shape))
    work = 2 * half * table * units
    pack_width = 256 + units + 2 * halo
    rows_out, pack, send = run(
        pack_kernel,
        "pack",
        [
            whole(feat_t),
            whole(send_rows.reshape(parts, bound)),
            (changed.T, SMEM),
            *[whole(a) for a in (mask_rows, first_weight.T, second_weight.T)],
            *[whole(a) for a in (jnp.transpose(cache_hidden, (0, 2, 1)), hidden_bias)],
        ],
        [
            ((parts, bound, 128), BF16, VMEM),
            ((units // reps, pack_width), BF16, VMEM),
            ((halo, 1), I32, VMEM),
        ],
        flops=2 * halo * nodes * 128,
        grid=(1,),
    )
    packs = [pack if k == 0 else swap(pack, k) for k in range(reps)]
    rows = exchange(rows_out)
    node_block = lambda size, rows: pl.BlockSpec((rows, size), lambda i: (0, i))
    block, fine_block = node_block(ROWS, units), node_block(FINE, units)
    scalar = pltpu.SMEM((1,), F32)
    high, rest = run(
        build_kernel,
        "build",
        [where, *placed(OWN, edge_src.T, edge_norm.T)],
        [((half, table), BF16, HBM), ((half, table), F8, HBM)],
        [vm((half, table), BF16), vm((half, table), F8), sems(2, half // 128)],
        flops=4 * 256 * table * half,
    )
    edge = placed(HBM, high, rest)

    packs, hidden_one, slope_one, z_own, z_send, flags_t = run(
        layer_one_kernel,
        "layer_one",
        [where, *placed(VMEM, rows), whole(feat_t), *placed(VMEM, *packs, send), *edge],
        [
            ((units, pack_width), BF16, whole_spec((units, pack_width))),
            ((units, half), BF16, block),
            ((units, half), F32, block),
            ((units, half), BF16, block),
            ((parts, bound, units), BF16, whole_spec((parts, bound, units))),
            ((8, halo), F32, whole_spec((8, halo))),
        ],
        [vm((units, table), BF16), vm((units, table), F8), scalar, *ring_scratch((ROWS, table), 2)],
        flops=work,
        grid=(steps,),
    )

    def own_part(z_own, z_oth, name):
        n = z_own.shape[0]
        return run(
            own_part_kernel,
            name,
            [where, *edge, whole(z_own), (z_oth, VMEM)],
            [((n, half), F32, node_block(FINE, n))],
            [vm((n, nodes), BF16), vm((n, nodes), F8), scalar, *ring_scratch((FINE, nodes))],
            flops=work,
            grid=(fine,),
        )[0]

    z_oth = swap(z_own)
    came = exchange(z_send)
    total = own_part(z_own, z_oth, "layer_two_own")
    came, total = late(total, came)
    came_oth = swap(came)
    border_block = lambda array: (array, pl.BlockSpec((ROWS, halo), lambda i: (i, nodes // halo)))
    hidden_two, slope_two, z_own, z_send = run(
        layer_two_end_kernel,
        "layer_two_end",
        [where, whole(flags_t), whole(packs), (send, VMEM), border_block(high), border_block(rest), (total, block)]
        + placed(VMEM, came, came_oth)
        + [whole(last_t)],
        [
            ((units, half), BF16, block),
            ((units, half), F32, block),
            ((kinds, half), BF16, node_block(ROWS, kinds)),
            ((parts, bound, 128), BF16, whole_spec((parts, bound, 128))),
        ],
        [vm((units, halo), BF16), vm((units, halo), F8), scalar],
        flops=work // 4,
        grid=(steps,),
    )
    z_oth = swap(z_own)
    came = exchange(z_send)
    total = own_part(z_own, z_oth, "layer_three_own")
    came, total = late(total, came)
    came_oth = swap(came)
    border_rows = [vm((half, halo), BF16), vm((half, halo), F8)]
    sums_out, back, border_grad, grads, grads8, far = run(
        functools.partial(loss_kernel, classes),
        "loss",
        [
            where,
            *placed(VMEM, flags_t, came, came_oth, cache_out.T, out_bias.reshape(1, classes), label_rows, mask_rows),
            (total, HBM),
            *edge,
        ],
        [
            ((64, 128), F32, VMEM),
            ((8, 128), F32, VMEM),
            ((parts, bound, 128), F32, VMEM),
            ((2 * kinds, half), BF16, HBM),
            ((kinds, half), F8, HBM),
            ((kinds, half), F32, HBM),
        ],
        [
            vm((128, halo), F32),
            *border_rows,
            vm((kinds, half), F32),
            vm((2 * kinds, half), BF16),
            vm((kinds, half), F8),
            vm((kinds, half), F32),
            vm((half, half), BF16),
            vm((half, half), F8),
            sems(3, steps),
            sems(2, steps),
            sems(2, steps),
            sems(1, steps),
        ],
        flops=work,
    )
    far = swap(far)
    ret = exchange(border_grad)
    near = run(
        back_three_kernel,
        "back_three",
        [where, *edge, whole(grads), whole(grads8), (back, VMEM)],
        [((kinds, half), F32, node_block(FINE, kinds))],
        ring_scratch((half, FINE)),
        flops=work // 2,
        grid=(fine,),
    )[0]
    ret, far, near = late(near, ret, far)
    ret_oth = swap(ret)
    chunk = 64 // parts

    def end(layer, name, ret, ret_oth, weight, near, far, hidden, slope):
        n = near.shape[0]
        with_far = layer == 1
        return run(
            functools.partial(end_kernel, layer),
            name,
            [
                where,
                *placed(VMEM, flags_t, ret, ret_oth, weight, send),
                (far, ANY),
                *placed(HBM, near, hidden, slope),
                *edge,
            ],
            [
                ((units, 128), F32, VMEM),
                ((8, 128), F32, VMEM),
                ((parts, bound + (1 if with_far else 2) * chunk, units), F32, VMEM),
                ((chunk, units), F32, VMEM),
                ((units, half), BF16, HBM),
                ((units, half), F8, HBM),
                ((units, half), F8, HBM),
                *([((units, half), F32, HBM)] if with_far else []),
            ],
            [
                vm((n, half), F32),
                vm((n, half), F32),
                vm((units, half), BF16),
                vm((units, half), F32),
                *border_rows,
                vm((units, half), F32),
                vm((max(n, 64), units), F32),
                vm((units, halo), F32),
                vm((units, half), BF16),
                vm((units, half), F8),
                vm((units, half), F8),
                sems(4, steps),
                sems(2, steps),
                sems(3, steps),
            ]
            + (
                [vm((units, half), F32), vm((half, half), BF16), vm((half, half), F8), sems(2, steps), sems(1, steps)]
                if with_far
                else []
            ),
            flops=work,
        )

    def back_part(halves, back, grads, grads8, tails8):
        each = fine // halves
        out_block = lambda k: pl.BlockSpec((units, FINE), lambda i: (0, jnp.clip(i - k * each, 0, each - 1)))
        return run(
            functools.partial(back_kernel, halves),
            "back",
            [where, *edge, whole(grads), whole(grads8), whole(tails8), (back, VMEM)],
            [((units, half // halves), F32, out_block(k)) for k in range(halves)],
            ring_scratch((half, FINE)),
            flops=work // 2,
            grid=(fine,),
        )

    sums_two, back, border_grad, _, grads, grads8, tails8, far = end(
        1, "end_three", ret, ret_oth, last_t, near, far, hidden_two, slope_two
    )
    far = swap(far)
    ret = exchange(border_grad)
    near = back_part(1, back, grads, grads8, tails8)[0]
    ret, far, near = late(near, ret, far)
    ret_oth = swap(ret)
    sums_one, back, border_grad, last_chunk, grads, grads8, tails8 = end(
        0, "end_two", ret, ret_oth, packs, near, far, hidden_one, slope_one
    )
    ret = exchange(border_grad)
    far, near = back_part(2, back, grads, grads8, tails8)
    far = swap(far)
    ret, near = late(near, ret)
    ret_oth = swap(ret)
    *pieces, second_chunk = run(
        end_one_kernel,
        "end_one",
        [where, *placed(VMEM, ret, ret_oth, send, sums_one, sums_two, sums_out), (far, ANY), *placed(HBM, near, feat_t)],
        [((64, 128), F32, VMEM)] * 4 + [((chunk, units), F32, VMEM)],
        [
            vm((units, half // 2), F32),
            vm((units, half // 2), F32),
            vm((in_width, half // 2), BF16),
            vm((units, 128), F32),
            sems(3, steps),
        ],
        flops=work // 8,
    )
    pieces = [piece if k == 0 else swap(piece, k) for k, piece in enumerate(pieces)]
    gathered = run(
        gather_kernel,
        "gather",
        placed(VMEM, *pieces, second_chunk, last_chunk),
        [((parts, 64 + 4 * chunk, 128), F32, VMEM)],
    )[0]
    came = exchange(gathered)

    turn = lambda x: x.T
    same = lambda x: x
    row = lambda x: x.reshape(1, -1)
    forms = (turn, turn, turn, same, row)
    weights = (first_weight, second_weight, last_weight, hidden_bias, out_bias)
    moments = (moment_first, moment_second, moment_last, moment_hidden, moment_out)
    squares = (square_first, square_second, square_last, square_hidden, square_out)
    params = [form(x) for form, triple in zip(forms, zip(weights, moments, squares)) for x in triple]
    outs = run(
        update_kernel,
        "update",
        placed(VMEM, came, flags_t, *params),
        [(p.shape, F32, VMEM) for p in params] + [((1, 128), F32, VMEM)] * 2,
    )
    undo = (turn, turn, turn, same, lambda x: x.reshape(-1))
    results = [undo[k // 3](x) for k, x in enumerate(outs[0:15])]
    return (outs[15][0, 0], outs[16][0, 0], *results)


def solution(mesh):
    placed = (
        P("dom", None),
        P("dom"),
        P("dom"),
        P("dom", None),
        P("dom", None),
        P("dom", None, None),
        P(None, "dom"),
        P(None, "dom", "rep"),
        P("dom", None),
        P(None, "rep"),
        P(None, "rep"),
        P(),
        P(None, "rep"),
        P(),
        P(None, "rep"),
        P(None, "rep"),
        P(),
        P(None, "rep"),
        P(),
        P(None, "rep"),
        P(None, "rep"),
        P(),
        P(None, "rep"),
        P(),
    )
    return jax.shard_map(
        functools.partial(body, mesh.shape["dom"], mesh.shape["rep"]),
        mesh=mesh,
        in_specs=placed,
        out_specs=(P(), P()) + (P(None, "rep"),) * 6 + (P(),) * 3 + (P(None, "rep"),) * 3 + (P(),) * 3,
        check_vma=False,
    )
```

```python
import functools

import jax
import jax.numpy as jnp
from jax import lax
from jax.experimental import pallas as pl
from jax.experimental.pallas import tpu as pltpu
from jax.sharding import PartitionSpec as P

STEP = 5
beta_one = 0.5
beta_two = 0.5
rate_step = 0.03
decay_rate = 0.01
epsilon = 1e-08

BF16, F32, F8, I32 = jnp.bfloat16, jnp.float32, jnp.float8_e4m3fn, jnp.int32
REST_GAIN = 4096.0
TAIL_GAIN = 256.0
FLAG_LANE = 100
ROWS = 512
FINE = 256
AHEAD = 3
LIMIT = 52 << 20
RESIDENT_BYTES = 30 << 20

SMEM = pl.BlockSpec(memory_space=pltpu.SMEM)
VMEM = pl.BlockSpec(memory_space=pltpu.VMEM)
OWN = pl.BlockSpec(memory_space=pltpu.VMEM)
HBM = pl.BlockSpec(memory_space=pltpu.HBM)
ANY = pl.BlockSpec(memory_space=pl.ANY)


def whole_spec(shape):
    return pl.BlockSpec(shape, lambda *_: (0,) * len(shape))


def placed(spec, *arrays):
    return [(a, spec) for a in arrays]


def run(kernel, name, args, outs, scratch=(), flops=0, grid=()):
    pinned = [
        a if any(spec is s for s in (SMEM, VMEM, ANY)) else pltpu.with_memory_space_constraint(a, pltpu.HBM)
        for a, spec in args
    ]
    return pl.pallas_call(
        kernel,
        grid=grid,
        in_specs=[spec for _, spec in args],
        out_specs=[spec for _, _, spec in outs],
        out_shape=[
            jax.ShapeDtypeStruct(shape, kind) if spec is VMEM else pltpu.HBM(shape, kind)
            for shape, kind, spec in outs
        ],
        scratch_shapes=list(scratch),
        name=name,
        cost_estimate=pl.CostEstimate(flops=flops, bytes_accessed=1 << 20, transcendentals=0),
        compiler_params=pltpu.CompilerParams(vmem_limit_bytes=LIMIT),
    )(*pinned)


def dot_nn(left, right):
    return lax.dot_general(left, right, (((1,), (0,)), ((), ())), preferred_element_type=F32)


def dot_nt(left, right):
    return lax.dot_general(left, right, (((1,), (1,)), ((), ())), preferred_element_type=F32)


def dot_tn(left, right):
    return lax.dot_general(left, right, (((0,), (0,)), ((), ())), preferred_element_type=F32)


def scale_of(value):
    most = jnp.maximum(jnp.max(jnp.abs(value)), 1e-30)
    return 256.0 / most, most * (1.0 / 256.0)


def span(start, size):
    return pl.ds(pl.multiple_of(start, size), size)


def rows_at(size, cols=slice(None)):
    return lambda i: (span(i * size, size), cols)


def cols_at(size, base=0):
    return lambda i: (slice(None), span(base + i * size, size))


def all_of(i):
    return (slice(None), slice(None))


def loop(count, step):
    def one(i, carry):
        step(i)
        return carry

    lax.fori_loop(0, count, one, 0)


class Ring:
    def __init__(self, refs, bufs, sems, cut, first=0):
        self.refs, self.bufs, self.sems, self.cut = refs, bufs, sems, cut
        self.begins = pl.program_id(0) == 0
        self.step, self.steps = pl.program_id(0) - first, pl.num_programs(0) - first
        self.depth = bufs[0].shape[0]
        self.slot = lax.rem(self.step, self.depth)

    def copies(self, step, slot):
        return [
            pltpu.make_async_copy(ref.at[self.cut(step)], buf.at[slot], self.sems.at[k, slot])
            for k, (ref, buf) in enumerate(zip(self.refs, self.bufs))
        ]

    def begin(self):
        for step in range(self.depth):

            @pl.when(self.begins & (step < self.steps))
            def _():
                for copy in self.copies(step, step):
                    copy.start()

    def wait(self):
        for copy in self.copies(self.step, self.slot):
            copy.wait()
        return [buf.at[self.slot] for buf in self.bufs]

    def end(self):
        @pl.when(self.step + self.depth < self.steps)
        def _():
            for copy in self.copies(self.step + self.depth, self.slot):
                copy.start()


def ring_scratch(shape, depth=3):
    kinds = (BF16, F8)
    return [pltpu.VMEM((depth, *shape), kind) for kind in kinds] + [pltpu.SemaphoreType.DMA((len(kinds), depth))]


class Stream:
    def __init__(self, sems, *legs):
        self.sems, self.legs = sems, legs

    def copies(self, i):
        return [
            pltpu.make_async_copy(source.at[source_at(i)], target.at[target_at(i)], self.sems.at[k, i])
            for k, (source, source_at, target, target_at) in enumerate(self.legs)
        ]

    def start(self, i):
        for copy in self.copies(i):
            copy.start()

    def wait(self, i):
        for copy in self.copies(i):
            copy.wait()

    def wait_all(self, count):
        loop(count, self.wait)

    def start_first(self, count):
        for i in range(min(AHEAD, count)):
            self.start(i)

    def next(self, i, count):
        self.wait(i)

        @pl.when(i + AHEAD < count)
        def _():
            self.start(i + AHEAD)


def sems(legs, count):
    return pltpu.SemaphoreType.DMA((legs, count))


def pick_rows(send, first, count):
    nodes = lax.broadcasted_iota(I32, (send.shape[0], count), 1) + first
    return jnp.where(send == nodes, 1.0, 0.0).astype(BF16)


def pack_kernel(feat_t, send_list, changed, mask, first_t, second_t, cache_t, bias, rows_out, pack_out, send):
    nodes, halo = feat_t.shape[1], send.shape[0]
    parts, bound = send_list.shape
    turned = send_list[...].astype(F32)
    turned = jnp.concatenate([turned, jnp.zeros((parts, 128 - bound), F32)], axis=1)
    turned = turned.T.astype(I32)
    for q in range(parts):
        send[q * bound : (q + 1) * bound, :] = turned[0:bound, q : q + 1]
    width, cols = feat_t.shape[0], first_t.shape[0]

    def pick(i, total):
        return total + dot_nt(pick_rows(send[...], i * ROWS, ROWS), feat_t[:, span(i * ROWS, ROWS)])

    total = lax.fori_loop(0, nodes // ROWS, pick, jnp.zeros((halo, width), F32))
    count = jnp.sum(mask[...].astype(F32))
    many = jnp.floor(count * (1.0 / 64.0))
    lane = lax.broadcasted_iota(I32, (halo, 128), 1)
    row = jnp.concatenate([total, jnp.zeros((halo, 128 - width), F32)], axis=1)
    for layer in range(3):
        row = jnp.where(lane == FLAG_LANE + layer, changed[0:1, layer : layer + 1].astype(F32), row)
    row = jnp.where(lane == FLAG_LANE + 3, many, row)
    row = jnp.where(lane == FLAG_LANE + 4, count - 64.0 * many, row)
    rows_out[...] = row.astype(BF16).reshape(rows_out.shape)

    units = second_t.shape[1]
    pack_out[:, 0:128] = jnp.concatenate(
        [first_t[...], jnp.zeros((cols, 128 - width), F32)], axis=1
    ).astype(BF16)
    pack_out[:, 128 : 128 + units] = second_t[...].astype(BF16)
    left = jnp.concatenate([bias[...], jnp.zeros((2, 128 - cols), F32)], axis=1)
    terms = []
    for _ in range(3):
        term = left.astype(BF16).astype(F32)
        terms.append(term)
        left = left - term
    terms = jnp.concatenate(terms + [jnp.zeros((122, 128), F32)], axis=0).T
    pack_out[:, 128 + units : 256 + units] = terms[0:cols, :].astype(BF16)
    base = 256 + units
    for layer in range(2):
        pack_out[:, base + layer * halo : base + (layer + 1) * halo] = cache_t[layer]


def bias_column(packs, layer):
    units = packs.shape[0]
    terms = packs[:, 128 + units : 256 + units].astype(F32)
    return terms[:, layer : layer + 1] + terms[:, layer + 2 : layer + 3] + terms[:, layer + 4 : layer + 5]


def stale_columns(packs, layer, halo):
    base = 256 + packs.shape[0] + layer * halo
    return packs[:, base : base + halo].astype(F32)


def table_kernel(place, pack, pack_one, pack_two, pack_three, feat_hbm, packs, most_out, table_hbm, feat_t, table, in_sems, out_sems):
    width, nodes = feat_t.shape
    steps = nodes // ROWS
    blocks = Stream(in_sems, (feat_hbm, cols_at(ROWS), feat_t, cols_at(ROWS)))
    stores = Stream(out_sems, (table, cols_at(ROWS), table_hbm, cols_at(ROWS)))
    loop(steps, blocks.start)
    for k, ref in enumerate((pack, pack_one, pack_two, pack_three)):
        packs[span(jnp.bitwise_xor(place[0] + 2 * place[1], k) * 64, 64), :] = ref[...]
    weight = packs[:, 0:width]

    def step(i, most):
        blocks.wait(i)
        here = span(i * ROWS, ROWS)
        z = dot_nn(weight, feat_t[:, here])
        table[:, here] = z.astype(BF16)
        stores.start(i)
        return jnp.maximum(most, lane_most(z))

    most = lax.fori_loop(0, steps, step, jnp.zeros((packs.shape[0], 128), F32))
    most_out[...] = most
    stores.wait_all(steps)


def lane_most(value):
    most = jnp.abs(value[:, 0:128])
    for first in range(128, value.shape[1], 128):
        most = jnp.maximum(most, jnp.abs(value[:, first : first + 128]))
    return most


def gelu_both(u):
    square = u * u
    t = jnp.tanh(0.79788456 * (u + 0.044715 * u * square))
    half = 0.5 * (1.0 + t)
    slope = half + 0.5 * u * (1.0 - t * t) * (0.79788456 * (1.0 + 3.0 * 0.044715 * square))
    return u * half, slope


def layer_one_kernel(place, src_t, norm_t, rows, send, most, packs_hbm, table_hbm, z_send, flags_t, high_hbm, rest_hbm, hidden_hbm, slope_hbm, z_hbm, packs, table, table8, high, rest, hidden_t, slope_t, z_own, in_sems, edge_sems, out_sems):
    slots = src_t.shape[0]
    units, half = hidden_t.shape
    nodes = 2 * half
    halo = send.shape[0]
    blocks = high.shape[1] // 256
    per_group = 256 // slots
    steps = half // FINE
    fetch = Stream(in_sems, (packs_hbm, all_of, packs, all_of), (table_hbm, all_of, table, lambda i: (slice(None), slice(0, nodes))))
    fetch.start(0)
    depth = high.shape[0] // FINE
    around = lambda i, count: i if depth >= steps else lax.rem(i, count)
    slot_of = lambda i: span(around(i, depth) * FINE, FINE)
    slot_at = lambda i: (slot_of(i), slice(None))
    edge_stores = Stream(edge_sems, (high, slot_at, high_hbm, rows_at(FINE)), (rest, slot_at, rest_hbm, rows_at(FINE)))
    stores = Stream(
        out_sems,
        *[(a, cols_at(FINE), b, cols_at(FINE)) for a, b in ((hidden_t, hidden_hbm), (slope_t, slope_hbm), (z_own, z_hbm))],
    )
    in_slot = lax.broadcasted_iota(I32, (8, 128), 1) // per_group == lax.broadcasted_iota(I32, (8, 128), 0)
    node_row = lax.broadcasted_iota(I32, (per_group, 256), 0)
    mine = lax.rem(lax.broadcasted_iota(I32, (per_group, 256), 1), per_group) == node_row
    inner = lax.broadcasted_iota(I32, (256, 256), 0)

    def lean(tile):
        return [
            pltpu.roll(tile[first : first + 8, :], 0, 1, stride=per_group, stride_axis=0)
            for first in range(0, slots, 8)
        ]

    def flat(tiles, group):
        moved = [pltpu.roll(tile, (128 - per_group * group) % 128, 1) for tile in tiles]
        return jnp.concatenate(
            [jnp.sum(jnp.where(in_slot, tile, 0), axis=0, keepdims=True) for tile in moved], axis=1
        )

    def one(at, weight):
        weight_high = weight.astype(BF16).astype(F32)
        hit = inner == jnp.bitwise_and(at, 255)
        right = jnp.where(hit, weight_high, 0.0).astype(BF16)
        right_rest = jnp.where(hit, (weight - weight_high) * REST_GAIN, 0.0).astype(BF16)
        block = jnp.where(mine, jnp.right_shift(at, 8), -1)
        left = jnp.concatenate(
            [jnp.where(block == j, 1.0, 0.0).astype(BF16) for j in range(blocks)], axis=0
        )
        return dot_nt(left, right), dot_nt(left, right_rest)

    def build(i):
        here = span(place[0] * half + i * 128, 128)
        at, weight = src_t[:, here], norm_t[:, here]
        slot = lax.broadcasted_iota(I32, at.shape, 0)
        merged, repeat = weight, slot < 0
        for shift in range(1, slots):
            same = at == pltpu.roll(at, shift, 0)
            merged = merged + jnp.where(same, pltpu.roll(weight, shift, 0), 0.0)
            repeat = repeat | (same & (slot >= shift))
        source, weights = lean(at), lean(jnp.where(repeat, 0.0, merged))
        pairs = [one(flat(source, group), flat(weights, group)) for group in range(128 // per_group)]
        rows = span(around(i, high.shape[0] // 128) * 128, 128)
        for j in range(blocks):
            cols = slice(256 * j, 256 * (j + 1))
            for ref, parts in zip((high, rest), zip(*pairs)):
                piece = jnp.concatenate([p[per_group * j : per_group * (j + 1), :] for p in parts], axis=0)
                ref[rows, cols] = piece.astype(ref.dtype)

    def build_block(i):
        for k in range(FINE // 128):
            build(i * (FINE // 128) + k)
        edge_stores.start(i)

    flat_rows = rows[...].reshape(halo, 128)
    flags = flat_rows.astype(F32).T[FLAG_LANE : FLAG_LANE + 8, :]
    counts = jnp.sum(rows[...].astype(F32)[:, 0, :], axis=0, keepdims=True)
    count = 64.0 * counts[:, FLAG_LANE + 3 : FLAG_LANE + 4] + counts[:, FLAG_LANE + 4 : FLAG_LANE + 5]
    row = lax.broadcasted_iota(I32, flags.shape, 0)
    flags_t[...] = jnp.where(row == 3, count, flags)
    z_send[...] = jnp.zeros(z_send.shape, BF16)
    loop(FINE // 128, build)
    edge_stores.start(0)
    fetch.wait(0)
    border = dot_nt(packs[:, 0:FLAG_LANE], flat_rows[:, 0:FLAG_LANE]).astype(BF16).astype(F32)
    border = jnp.where(flags[0:1, :] == 1.0, border, stale_columns(packs, 0, halo))
    table[:, nodes : nodes + halo] = border.astype(BF16)
    scale, back = scale_of(jnp.maximum(jnp.max(most[...]), jnp.max(jnp.abs(border))))
    back = back * (1.0 / REST_GAIN)
    bias = bias_column(packs, 0)

    def small(i):
        here = span(i * 256, 256)
        table8[:, here] = (table[:, here].astype(F32) * scale).astype(F8)

    loop((nodes + halo) // 256, small)

    def sums(i):
        here = slot_of(i)
        return dot_nt(table[...], high[here, :]) + dot_nt(table8[...], rest[here, :]) * back

    def finish(i):
        here = span(i * FINE, FINE)
        value, slope = gelu_both(slope_t[:, here] + bias)
        value = value.astype(BF16)
        hidden_t[:, here] = value
        slope_t[:, here] = slope
        z = dot_nn(packs[:, 128 : 128 + units], value).astype(BF16)
        z_own[:, here] = z
        stores.start(i)
        chosen = dot_nt(pick_rows(send[...], place[0] * half + i * FINE, FINE), z)
        z_send[...] = (z_send[...].astype(F32) + chosen.reshape(z_send.shape)).astype(BF16)

    def step(i, carry):
        if depth < steps:

            @pl.when(i + 1 >= depth)
            def _():
                edge_stores.wait(i + 1 - depth)

        total = sums(i)
        finish(i - 1)
        build_block(i + 1)
        slope_t[:, span(i * FINE, FINE)] = total
        return carry

    slope_t[:, 0:FINE] = sums(0)
    build_block(1)
    lax.fori_loop(1, steps - 1, step, 0)
    slope_t[:, span((steps - 1) * FINE, FINE)] = sums(steps - 1)
    finish(steps - 2)
    finish(steps - 1)
    stores.wait_all(steps)
    for i in range(steps - depth, steps):
        edge_stores.wait(i)


def own_part_kernel(place, high, rest, z_own, z_oth, total, table, table8, back, hbuf, rbuf, sems):
    half = z_own.shape[1]
    nodes = 2 * half
    ring = Ring((high, rest), (hbuf, rbuf), sems, lambda i: (span(i * FINE, FINE), slice(0, nodes)))
    ring.begin()

    @pl.when(pl.program_id(0) == 0)
    def _():
        def larger(i, most):
            here = span(i * ROWS, ROWS)
            both = jnp.maximum(jnp.abs(z_own[:, here].astype(F32)), jnp.abs(z_oth[:, here].astype(F32)))
            return jnp.maximum(most, both)

        most = lax.fori_loop(0, half // ROWS, larger, jnp.zeros((z_own.shape[0], ROWS), F32))
        scale, inverse = scale_of(most)
        back[0] = inverse * (1.0 / REST_GAIN)
        for ref, first in ((z_own, place[0] * half), (z_oth, (1 - place[0]) * half)):

            def put(i, carry):
                value = ref[:, span(i * ROWS, ROWS)]
                cols = span(first + i * ROWS, ROWS)
                table[:, cols] = value
                table8[:, cols] = (value.astype(F32) * scale).astype(F8)
                return carry

            lax.fori_loop(0, half // ROWS, put, 0)

    top, low = ring.wait()
    total[...] = dot_nt(table[...], top[...]) + dot_nt(table8[...], low[...]) * back[0]
    ring.end()


def padded_rows(ref, count):
    value = ref[...]
    extra = jnp.zeros((count - value.shape[0], value.shape[1]), value.dtype)
    return jnp.concatenate([value, extra], axis=0).astype(BF16)


def border_cut(nodes, halo):
    return lambda i: (span(i * ROWS, ROWS), slice(nodes, nodes + halo))


def layer_two_end_kernel(place, flags_t, packs, send, high, rest, total, came, came_oth, last_t, hidden_t, slope_t, z_own, z_send, border, border8, back):
    halo = send.shape[0]
    width = hidden_t.shape[0]
    kinds = z_own.shape[0]
    step = pl.program_id(0)
    half = ROWS * pl.num_programs(0)

    @pl.when(step == 0)
    def _():
        both = came[...].reshape(halo, width).astype(F32) + came_oth[...].reshape(halo, width).astype(F32)
        value = jnp.where(flags_t[1:2, :] == 1.0, both.T, stale_columns(packs, 1, halo))
        scale, inverse = scale_of(value)
        border[...] = value.astype(BF16)
        border8[...] = (value * scale).astype(F8)
        back[0] = inverse * (1.0 / REST_GAIN)
        z_send[...] = jnp.zeros(z_send.shape, BF16)

    sums = total[...] + dot_nt(border[...], high[...]) + dot_nt(border8[...], rest[...]) * back[0]
    value, slope = gelu_both(sums + bias_column(packs, 1))
    value = value.astype(BF16)
    hidden_t[...] = value
    slope_t[...] = slope
    z = dot_nn(padded_rows(last_t, kinds), value).astype(BF16)
    z_own[...] = z
    chosen = dot_nt(pick_rows(send[...], place[0] * half + step * ROWS, ROWS), z)
    chosen = jnp.concatenate([chosen, jnp.zeros((halo, 128 - kinds), F32)], axis=1)
    z_send[...] = (z_send[...].astype(F32) + chosen.reshape(z_send.shape)).astype(BF16)


def put_border(border_grad, total, keep):
    value = (total * keep).T
    bound = value.shape[0] // border_grad.shape[0]
    border_grad[:, 0:bound, :] = value.reshape(border_grad.shape[0], bound, value.shape[1])


def loss_kernel(classes, place, flags_t, came, came_oth, stale_t, bias, labels, mask, total_hbm, high, rest, sums, back_out, border_grad, grads_hbm, grads8_hbm, far_hbm, border_sum, hrows, rrows, total, grads, grads8, far, hbuf, rbuf, in_sems, edge_sems, out_sems, far_sems):
    kinds, half = total.shape
    halo = stale_t.shape[1]
    steps = half // ROWS
    cut = border_cut(2 * half, halo)
    blocks = Stream(
        in_sems,
        (high, cut, hrows, rows_at(ROWS)),
        (rest, cut, rrows, rows_at(ROWS)),
        (total_hbm, cols_at(ROWS), total, cols_at(ROWS)),
    )
    others = rows_at(ROWS, span((1 - place[0]) * half, half))
    edges = Stream(edge_sems, (high, others, hbuf, rows_at(ROWS)), (rest, others, rbuf, rows_at(ROWS)))
    stores = Stream(
        out_sems, *[(a, cols_at(ROWS), b, cols_at(ROWS)) for a, b in ((grads, grads_hbm), (grads8, grads8_hbm))]
    )
    far_stores = Stream(far_sems, (far, all_of, far_hbm, all_of))
    blocks.start_first(steps)
    edges.start(0)
    both = came[...].reshape(halo, 128).astype(F32) + came_oth[...].reshape(halo, 128).astype(F32)
    old = jnp.concatenate([stale_t[...].astype(F32), jnp.zeros((kinds - classes, halo), F32)], axis=0)
    value = jnp.where(flags_t[2:3, :] == 1.0, both.T[0:kinds, :], old)
    scale, back = scale_of(value)
    back = back * (1.0 / REST_GAIN)
    border = value.astype(BF16)
    border8 = (value * scale).astype(F8)
    row = jnp.concatenate([bias[...], jnp.zeros((1, 128 - classes), F32)], axis=1)
    bias_col = jnp.broadcast_to(row, (8, 128)).T[0:kinds, 0:1]
    sums[...] = jnp.zeros(sums.shape, F32)
    border_sum[...] = jnp.zeros(border_sum.shape, F32)
    count = flags_t[3:4, 0:1]
    inverse = (1.0 / (256.0 * REST_GAIN)) / count
    back_out[...] = jnp.broadcast_to(inverse, back_out.shape)

    def far_step(i):
        edges.wait(i)
        here = span(i * ROWS, ROWS)
        both = dot_nn(grads[:, here], hbuf[here, :])
        low = dot_nn(grads8[:, here], rbuf[here, :]) * inverse
        far[...] += both[0:kinds] + both[kinds : 2 * kinds] + low

    def step(i):
        here = span(i * ROWS, ROWS)
        logits = total[:, here] + dot_nt(border, hrows[here, :]) + dot_nt(border8, rrows[here, :]) * back
        logits = logits + bias_col
        kind = lax.broadcasted_iota(I32, logits.shape, 0)
        real = kind < classes
        logits = jnp.where(real, logits, -jnp.inf)
        shifted = logits - jnp.max(logits, axis=0, keepdims=True)
        powers = jnp.exp(shifted)
        norm = jnp.sum(powers, axis=0, keepdims=True)
        logp = jnp.where(real, shifted - jnp.log(norm), 0.0)
        first = (place[0] * steps + i) * (ROWS // 128)
        row_of = lambda ref: jnp.concatenate([ref[pl.ds(first + k, 1), :] for k in range(ROWS // 128)], axis=1)
        target = jnp.where(kind == row_of(labels), 0.9, 0.0) + 0.1 / classes
        used = row_of(mask).astype(F32)
        loss = jnp.sum(target * logp, axis=0, keepdims=True) * used
        grad = jnp.where(real, (powers / norm - target) * (used / count), 0.0)
        sums[0:kinds, :] += lane_sums(grad)
        sums[kinds : kinds + 1, :] -= lane_sums(loss)
        top = grad.astype(BF16)
        tail = (grad - top.astype(F32)).astype(BF16)
        stacked = jnp.concatenate([top, tail], axis=0)
        small = (top.astype(F32) * (256.0 * count)).astype(F8)
        grads[:, here] = stacked
        grads8[:, here] = small
        stores.start(i)
        both = dot_nn(stacked, hrows[here, :])
        low = dot_nn(small, rrows[here, :]) * inverse
        border_sum[0:kinds, :] += both[0:kinds] + both[kinds : 2 * kinds] + low

    far[...] = jnp.zeros(far.shape, F32)
    blocks.next(0, steps)
    edges.start(1)
    step(0)

    def both_steps(i):
        blocks.next(i, steps)

        @pl.when(i + 1 < steps)
        def _():
            edges.start(i + 1)

        far_step(i - 1)
        step(i)

    lax.fori_loop(1, steps, lambda i, c: (both_steps(i), c)[1], 0)
    far_step(steps - 1)
    far_stores.start(0)
    put_border(border_grad, border_sum[...], flags_t[2:3, :])
    stores.wait_all(steps)
    far_stores.wait(0)


def lane_sums(value):
    total = value[:, 0:128]
    for first in range(128, value.shape[1], 128):
        total = total + value[:, first : first + 128]
    return total


def back_three_kernel(place, high, rest, grads, grads8, back, out, hbuf, rbuf, sems):
    kinds, size = out.shape
    base = place[0] * size * pl.num_programs(0)
    ring = Ring((high, rest), (hbuf, rbuf), sems, lambda i: (slice(None), span(base + i * size, size)))
    ring.begin()
    top, low = ring.wait()
    both = dot_nn(grads[...], top[...])
    out[...] = both[0:kinds] + both[kinds : 2 * kinds] + dot_nn(grads8[...], low[...]) * back[0:1, 0:1]
    ring.end()


def back_block(grads, grads8, tails8, back_rest, back_tail, top, low):
    total = dot_nn(grads, top) + dot_nn(grads8, low) * back_rest
    return total + dot_nn(tails8, top.astype(F8)) * back_tail


def back_kernel(halves, place, high, rest, grads, grads8, tails8, back, *refs):
    *outs, hbuf, rbuf, sems = refs
    size = outs[0].shape[1]
    steps = pl.num_programs(0) // len(outs)
    base = place[1] * size * steps if halves == 2 else 0

    def cut(i):
        owner = jnp.where(i < steps * (len(outs) - 1), 1 - place[0], place[0])
        return slice(None), span(owner * size * steps * halves + base + lax.rem(i, steps) * size, size)

    ring = Ring((high, rest), (hbuf, rbuf), sems, cut)
    ring.begin()
    top, low = ring.wait()
    total = back_block(grads[...], grads8[...], tails8[...], back[0:1, 0:1], back[0:1, 1:2], top[...], low[...])
    for k, out in enumerate(outs):

        @pl.when((ring.step >= k * steps) & (ring.step < (k + 1) * steps))
        def _():
            out[...] = total

    ring.end()


def returned_terms(ret, ret_oth, bound, kinds):
    value = ret[:, 0:bound, :] + ret_oth[:, 0:bound, :]
    value = value.reshape(value.shape[0] * bound, value.shape[2]).T[0:kinds, :]
    top = value.astype(BF16)
    return top, (value - top.astype(F32)).astype(BF16)


def round_gradient(own, came_part, terms, send, first_node):
    chosen = pick_rows(send, first_node, own.shape[1])
    total = own + came_part
    for term in terms:
        total = total + dot_nn(term, chosen)
    return total.astype(BF16)


def end_kernel(layer, place, flags_t, ret, ret_oth, weight_ref, send, far_in_any, near_hbm, hidden_hbm, slope_hbm, high, rest, sums, back_out, border_grad, grads_hbm, grads8_hbm, tails8_hbm, *more):
    if layer == 1:
        far_hbm, far, hbuf, rbuf, edge_sems, far_sems = more[0], *more[-5:]
        more = more[1:-5]
    near, far_in, hidden_t, slope_t, hrows, rrows, grad_rows, grad_weight, border_sum, grads, grads8, tails8, in_sems, row_sems, out_sems = more
    kinds, half = near.shape
    units = slope_t.shape[0]
    parts = ret.shape[0]
    bound = send.shape[0] // parts
    halo = send.shape[0]
    steps = half // ROWS
    size = 64 // parts
    cut = border_cut(2 * half, halo)
    blocks = Stream(
        in_sems,
        *[
            (a, cols_at(ROWS), b, cols_at(ROWS))
            for a, b in ((near_hbm, near), (far_in_any, far_in), (hidden_hbm, hidden_t), (slope_hbm, slope_t))
        ],
    )
    borders = Stream(row_sems, (high, cut, hrows, rows_at(ROWS)), (rest, cut, rrows, rows_at(ROWS)))
    stores = Stream(
        out_sems,
        *[
            (a, cols_at(ROWS), b, cols_at(ROWS))
            for a, b in ((grads, grads_hbm), (grads8, grads8_hbm), (tails8, tails8_hbm))
        ],
    )
    if layer == 1:
        others = cols_at(ROWS, (1 - place[0]) * half)
        edges = Stream(edge_sems, (high, others, hbuf, cols_at(ROWS)), (rest, others, rbuf, cols_at(ROWS)))
        far_stores = Stream(far_sems, (far, cols_at(ROWS), far_hbm, cols_at(ROWS)))
    loop(steps, blocks.start)
    loop(steps, borders.start)
    if layer == 1:
        loop(steps, edges.start)
    terms = returned_terms(ret, ret_oth, bound, kinds)
    if layer == 0:
        chunk = jnp.sum(ret[:, bound:, :] + ret_oth[:, bound:, :], axis=0)
        weight = weight_ref[:, 128 : 128 + units]
    else:
        weight = padded_rows(weight_ref, kinds)
    sums[...] = jnp.zeros(sums.shape, F32)
    grad_weight[...] = jnp.zeros(grad_weight.shape, F32)
    border_sum[...] = jnp.zeros(border_sum.shape, F32)

    def first_step(i, most):
        blocks.wait(i)
        here = span(i * ROWS, ROWS)
        d_z = round_gradient(near[:, here], far_in[:, here], terms, send[...], (place[0] * steps + i) * ROWS)
        grad_weight[0:kinds, :] += dot_nt(d_z, hidden_t[:, here])
        grad = dot_tn(weight, d_z) * slope_t[:, here]
        sums[...] += lane_sums(grad)
        grad_rows[:, here] = grad
        return jnp.maximum(most, jnp.max(jnp.abs(grad), axis=0, keepdims=True))

    most = lax.fori_loop(0, steps, first_step, jnp.zeros((1, ROWS), F32))
    scale, back = scale_of(most)
    back_rest, back_tail = back * (1.0 / REST_GAIN), back * (1.0 / TAIL_GAIN)
    lane = lax.broadcasted_iota(I32, back_out.shape, 1)
    back_out[...] = jnp.where(lane == 0, back_rest, back_tail)

    def second_step(i):
        borders.wait(i)
        here = span(i * ROWS, ROWS)
        grad = grad_rows[:, here]
        top = grad.astype(BF16)
        wide = top.astype(F32)
        small = (wide * scale).astype(F8)
        tail = ((grad - wide) * (scale * TAIL_GAIN)).astype(F8)
        grads[:, here] = top
        grads8[:, here] = small
        tails8[:, here] = tail
        stores.start(i)
        border_sum[...] += back_block(top, small, tail, back_rest, back_tail, hrows[here, :], rrows[here, :])

    loop(steps, second_step)
    put_border(border_grad, border_sum[...], flags_t[layer : layer + 1, :])
    if layer == 1:
        border_grad[:, bound:, :] = grad_weight[...].reshape(parts, size, units)
    else:
        for core in range(2):
            block = grad_weight[span(place[1] * 128 + core * 64, 64), :]
            first = bound + core * size
            border_grad[:, first : first + size, :] = block.reshape(parts, size, units)
        border_grad[:, bound + 2 * size :, :] = jnp.broadcast_to(chunk[None], (parts, size, units))

    def far_step(i):
        edges.wait(i)
        here = span(i * ROWS, ROWS)
        far[:, here] = back_block(
            grads[...], grads8[...], tails8[...], back_rest, back_tail, hbuf[:, here], rbuf[:, here]
        )
        far_stores.start(i)

    if layer == 1:
        loop(steps, far_step)
        far_stores.wait_all(steps)
    stores.wait_all(steps)


def end_one_kernel(place, ret, ret_oth, send, sums_one, sums_two, sums_out, far_any, near_hbm, feat_hbm, out, out_one, out_two, out_three, second_chunk, grad_last, near, far, feat_t, grad_first, in_sems):
    units, size = near.shape
    parts = ret.shape[0]
    bound = send.shape[0] // parts
    width = feat_t.shape[0]
    chunk = 64 // parts
    steps = size // ROWS
    base = place[0] * 2 * size + place[1] * size
    blocks = Stream(
        in_sems,
        (near_hbm, cols_at(ROWS), near, cols_at(ROWS)),
        (far_any, cols_at(ROWS), far, cols_at(ROWS)),
        (feat_hbm, cols_at(ROWS, base), feat_t, cols_at(ROWS)),
    )
    blocks.start_first(steps)
    terms = returned_terms(ret, ret_oth, bound, units)
    mine = pl.ds(bound + place[0] * chunk, chunk)
    second_chunk[...] = jnp.sum(ret[:, mine, :] + ret_oth[:, mine, :], axis=0)
    grad_last[...] = ret[:, bound + 2 * chunk :, :].reshape(64, units)
    grad_first[...] = jnp.zeros(grad_first.shape, F32)

    def step(i):
        blocks.next(i, steps)
        here = span(i * ROWS, ROWS)
        d_z = round_gradient(near[:, here], far[:, here], terms, send[...], base + i * ROWS)
        grad_first[:, 0:width] += dot_nt(d_z, feat_t[:, here])

    loop(steps, step)
    lead = jnp.where(place[1] == 0, 1.0, 0.0)
    lane = lax.broadcasted_iota(I32, (64, 128), 1)
    column = lambda value: jnp.sum(value, axis=1, keepdims=True) * lead
    for k, ref in enumerate((out, out_one, out_two, out_three)):
        rows = span(jnp.bitwise_xor(place[0] + 2 * place[1], k) * 64, 64)
        value = grad_first[rows, :]
        value = jnp.where(lane == FLAG_LANE, column(sums_one[rows, :]), value)
        value = jnp.where(lane == FLAG_LANE + 1, column(sums_two[rows, :]), value)
        ref[...] = jnp.where(lane == FLAG_LANE + 2, column(sums_out[...]), value)


def gather_kernel(mine, one, two, three, second_chunk, out):
    total = mine[...] + one[...] + two[...] + three[...]
    value = jnp.concatenate([total, second_chunk[:, 0:128], second_chunk[:, 128:256]], axis=0)
    for p in range(out.shape[0]):
        out[p] = value


def adamw(weight, moment, square, gradient):
    moment = beta_one * moment + (1.0 - beta_one) * gradient
    square = beta_two * square + (1.0 - beta_two) * gradient * gradient
    moment_hat = moment / (1.0 - beta_one**STEP)
    square_hat = square / (1.0 - beta_two**STEP)
    weight = weight - rate_step * (
        moment_hat / (jnp.sqrt(square_hat) + epsilon) + decay_rate * weight
    )
    return (weight, moment, square)


def update_kernel(came, grad_last, flags_t, *refs):
    params, outs = refs[0:15], refs[15:]
    parts = came.shape[0]
    size = 64 // parts
    width, kinds = params[0].shape[1], params[6].shape[0]
    total = jnp.sum(came[:, 0:64, :], axis=0)

    halves = [came[:, 64 + k * size : 64 + (k + 1) * size, :].reshape(64, 128) for k in range(2)]
    turned = jnp.concatenate([total, jnp.zeros((64, 128), F32)], axis=0).T
    gradients = (
        total[:, 0:width],
        jnp.concatenate(halves, axis=1),
        grad_last[0:kinds, :],
        turned[FLAG_LANE : FLAG_LANE + 2, 0:64],
        turned[FLAG_LANE + 2 : FLAG_LANE + 3, 0:kinds],
    )
    for k, gradient in enumerate(gradients):
        values = adamw(*[ref[...] for ref in params[3 * k : 3 * k + 3]], gradient)
        for ref, value in zip(outs[3 * k : 3 * k + 3], values):
            ref[...] = value
    padded = turned[FLAG_LANE + 2 : FLAG_LANE + 3, 48:49]
    outs[15][...] = jnp.broadcast_to(padded, (1, 128))
    outs[16][...] = jnp.broadcast_to(flags_t[3:4, 0:1], (1, 128))


def body(
    parts,
    reps,
    features,
    labels,
    train_mask,
    edge_src,
    edge_norm,
    send_rows,
    changed,
    cache_hidden,
    cache_out,
    first_weight,
    second_weight,
    last_weight,
    hidden_bias,
    out_bias,
    moment_first,
    moment_second,
    moment_last,
    moment_hidden,
    moment_out,
    square_first,
    square_second,
    square_last,
    square_hidden,
    square_out,
):
    nodes, in_width = features.shape
    half = nodes // 2
    bound = send_rows.shape[2]
    halo = parts * bound
    table = nodes + halo
    units, classes = last_weight.shape
    kinds = -(-classes // 16) * 16
    steps, fine = half // ROWS, half // FINE

    rep = lax.axis_index("rep")
    place = jnp.stack([lax.rem(rep, 2), lax.div(rep, 2)]).astype(I32)
    where = (place, SMEM)
    feat_t = features.T
    last_t = last_weight.T
    label_rows = labels.reshape(nodes // 128, 128)
    mask_rows = train_mask.reshape(nodes // 128, 128)

    def swap(x, k=1):
        return lax.ppermute(x, "rep", [(i, i ^ k) for i in range(reps)])

    def exchange(x):
        return lax.all_to_all(x, "dom", split_axis=0, concat_axis=0, tiled=True)

    def late(after, *arrays):
        return lax.optimization_barrier((*arrays, after))

    vm = pltpu.VMEM
    whole = lambda a: (a, whole_spec(a.shape))
    work = 2 * half * table * units
    pack_width = 256 + units + 2 * halo
    rows_out, pack, send = run(
        pack_kernel,
        "pack",
        [
            whole(feat_t),
            whole(send_rows.reshape(parts, bound)),
            whole(changed.T),
            *[whole(a) for a in (mask_rows, first_weight.T, second_weight.T)],
            *[whole(a) for a in (jnp.transpose(cache_hidden, (0, 2, 1)), hidden_bias)],
        ],
        [
            ((parts, bound, 128), BF16, VMEM),
            ((units // reps, pack_width), BF16, VMEM),
            ((halo, 1), I32, VMEM),
        ],
        flops=2 * halo * nodes * 128,
        grid=(1,),
    )
    packs = [pack if k == 0 else swap(pack, k) for k in range(reps)]
    rows = exchange(rows_out)
    node_block = lambda size, rows: pl.BlockSpec((rows, size), lambda i: (0, i))
    block, fine_block = node_block(ROWS, units), node_block(FINE, units)
    scalar = pltpu.SMEM((1,), F32)
    packs, most, first_table = run(
        table_kernel,
        "table",
        [where, *placed(VMEM, *packs), (feat_t, HBM)],
        [((units, pack_width), BF16, OWN), ((units, 128), F32, VMEM), ((units, nodes), BF16, HBM)],
        [
            vm((in_width, nodes), BF16),
            vm((units, nodes), BF16),
            sems(1, nodes // ROWS),
            sems(1, nodes // ROWS),
        ],
        flops=2 * units * nodes * in_width,
    )
    rows, most = late(most, rows)
    held = fine if half * table * 3 <= RESIDENT_BYTES else min(fine, 4)
    z_send, flags_t, high, rest, hidden_one, slope_one, z_own = run(
        layer_one_kernel,
        "layer_one",
        [where, *placed(OWN, edge_src.T, edge_norm.T), *placed(VMEM, rows, send, most), *placed(HBM, packs, first_table)],
        [
            ((parts, bound, units), BF16, VMEM),
            ((8, halo), F32, OWN),
            ((half, table), BF16, HBM),
            ((half, table), F8, HBM),
            ((units, half), BF16, HBM),
            ((units, half), F32, HBM),
            ((units, half), BF16, HBM),
        ],
        [
            vm((units, pack_width), BF16),
            vm((units, table), BF16),
            vm((units, table), F8),
            vm((held * FINE, table), BF16),
            vm((held * FINE, table), F8),
            vm((units, half), BF16),
            vm((units, half), F32),
            vm((units, half), BF16),
            sems(2, 1),
            sems(2, fine),
            sems(3, fine),
        ],
        flops=2 * work,
    )
    edge = placed(HBM, high, rest)

    def own_part(z_own, z_oth, name):
        n = z_own.shape[0]
        return run(
            own_part_kernel,
            name,
            [where, *edge, whole(z_own), (z_oth, VMEM)],
            [((n, half), F32, node_block(FINE, n))],
            [vm((n, nodes), BF16), vm((n, nodes), F8), scalar, *ring_scratch((FINE, nodes))],
            flops=work,
            grid=(fine,),
        )[0]

    z_oth = swap(z_own)
    came = exchange(z_send)
    total = own_part(z_own, z_oth, "layer_two_own")
    came, total = late(total, came)
    came_oth = swap(came)
    border_block = lambda array: (array, pl.BlockSpec((ROWS, halo), lambda i: (i, nodes // halo)))
    hidden_two, slope_two, z_own, z_send = run(
        layer_two_end_kernel,
        "layer_two_end",
        [where, whole(flags_t), whole(packs), (send, VMEM), border_block(high), border_block(rest), (total, block)]
        + placed(VMEM, came, came_oth)
        + [whole(last_t)],
        [
            ((units, half), BF16, block),
            ((units, half), F32, block),
            ((kinds, half), BF16, node_block(ROWS, kinds)),
            ((parts, bound, 128), BF16, whole_spec((parts, bound, 128))),
        ],
        [vm((units, halo), BF16), vm((units, halo), F8), scalar],
        flops=work // 4,
        grid=(steps,),
    )
    z_oth = swap(z_own)
    came = exchange(z_send)
    total = own_part(z_own, z_oth, "layer_three_own")
    came, total = late(total, came)
    came_oth = swap(came)
    border_rows = [vm((half, halo), BF16), vm((half, halo), F8)]
    sums_out, back, border_grad, grads, grads8, far = run(
        functools.partial(loss_kernel, classes),
        "loss",
        [
            where,
            *placed(VMEM, flags_t, came, came_oth, cache_out.T, out_bias.reshape(1, classes), label_rows, mask_rows),
            (total, HBM),
            *edge,
        ],
        [
            ((64, 128), F32, VMEM),
            ((8, 128), F32, VMEM),
            ((parts, bound, 128), F32, VMEM),
            ((2 * kinds, half), BF16, HBM),
            ((kinds, half), F8, HBM),
            ((kinds, half), F32, HBM),
        ],
        [
            vm((128, halo), F32),
            *border_rows,
            vm((kinds, half), F32),
            vm((2 * kinds, half), BF16),
            vm((kinds, half), F8),
            vm((kinds, half), F32),
            vm((half, half), BF16),
            vm((half, half), F8),
            sems(3, steps),
            sems(2, steps),
            sems(2, steps),
            sems(1, 1),
        ],
        flops=work,
    )
    far = swap(far)
    ret = exchange(border_grad)
    near = run(
        back_three_kernel,
        "back_three",
        [where, *edge, whole(grads), whole(grads8), (back, VMEM)],
        [((kinds, half), F32, node_block(FINE, kinds))],
        ring_scratch((half, FINE)),
        flops=work // 2,
        grid=(fine,),
    )[0]
    ret, far, near = late(near, ret, far)
    ret_oth = swap(ret)
    chunk = 64 // parts

    def end(layer, name, ret, ret_oth, weight, near, far, hidden, slope):
        n = near.shape[0]
        with_far = layer == 1
        return run(
            functools.partial(end_kernel, layer),
            name,
            [
                where,
                *placed(VMEM, flags_t, ret, ret_oth, weight, send),
                (far, ANY),
                *placed(HBM, near, hidden, slope),
                *edge,
            ],
            [
                ((units, 128), F32, VMEM),
                ((8, 128), F32, VMEM),
                ((parts, bound + (1 if with_far else 3) * chunk, units), F32, VMEM),
                ((units, half), BF16, HBM),
                ((units, half), F8, HBM),
                ((units, half), F8, HBM),
                *([((units, half), F32, HBM)] if with_far else []),
            ],
            [
                vm((n, half), F32),
                vm((n, half), F32),
                vm((units, half), BF16),
                vm((units, half), F32),
                *border_rows,
                vm((units, half), F32),
                vm((max(n, 64), units), F32),
                vm((units, halo), F32),
                vm((units, half), BF16),
                vm((units, half), F8),
                vm((units, half), F8),
                sems(4, steps),
                sems(2, steps),
                sems(3, steps),
            ]
            + (
                [vm((units, half), F32), vm((half, half), BF16), vm((half, half), F8), sems(2, steps), sems(1, steps)]
                if with_far
                else []
            ),
            flops=work,
        )

    def back_part(halves, back, grads, grads8, tails8):
        each = fine // halves
        out_block = lambda k: pl.BlockSpec((units, FINE), lambda i: (0, jnp.clip(i - k * each, 0, each - 1)))
        return run(
            functools.partial(back_kernel, halves),
            "back",
            [where, *edge, whole(grads), whole(grads8), whole(tails8), (back, VMEM)],
            [((units, half // halves), F32, out_block(k)) for k in range(halves)],
            ring_scratch((half, FINE)),
            flops=work // 2,
            grid=(fine,),
        )

    sums_two, back, border_grad, grads, grads8, tails8, far = end(
        1, "end_three", ret, ret_oth, last_t, near, far, hidden_two, slope_two
    )
    far = swap(far)
    ret = exchange(border_grad)
    near = back_part(1, back, grads, grads8, tails8)[0]
    ret, far, near = late(near, ret, far)
    ret_oth = swap(ret)
    sums_one, back, border_grad, grads, grads8, tails8 = end(
        0, "end_two", ret, ret_oth, packs, near, far, hidden_one, slope_one
    )
    ret = exchange(border_grad)
    far, near = back_part(2, back, grads, grads8, tails8)
    far = swap(far)
    ret, near = late(near, ret)
    ret_oth = swap(ret)
    *pieces, second_chunk, grad_last = run(
        end_one_kernel,
        "end_one",
        [where, *placed(VMEM, ret, ret_oth, send, sums_one, sums_two, sums_out), (far, ANY), *placed(HBM, near, feat_t)],
        [((64, 128), F32, VMEM)] * 4 + [((chunk, units), F32, VMEM), ((64, units), F32, VMEM)],
        [
            vm((units, half // 2), F32),
            vm((units, half // 2), F32),
            vm((in_width, half // 2), BF16),
            vm((units, 128), F32),
            sems(3, steps),
        ],
        flops=work // 8,
    )
    pieces = [piece if k == 0 else swap(piece, k) for k, piece in enumerate(pieces)]
    gathered = run(
        gather_kernel,
        "gather",
        placed(VMEM, *pieces, second_chunk),
        [((parts, 64 + 2 * chunk, 128), F32, VMEM)],
    )[0]
    came = exchange(gathered)

    turn = lambda x: x.T
    same = lambda x: x
    row = lambda x: x.reshape(1, -1)
    forms = (turn, turn, turn, same, row)
    weights = (first_weight, second_weight, last_weight, hidden_bias, out_bias)
    moments = (moment_first, moment_second, moment_last, moment_hidden, moment_out)
    squares = (square_first, square_second, square_last, square_hidden, square_out)
    params = [form(x) for form, triple in zip(forms, zip(weights, moments, squares)) for x in triple]
    outs = run(
        update_kernel,
        "update",
        placed(VMEM, came, grad_last, flags_t, *params),
        [(p.shape, F32, VMEM) for p in params] + [((1, 128), F32, VMEM)] * 2,
    )
    undo = (turn, turn, turn, same, lambda x: x.reshape(-1))
    results = [undo[k // 3](x) for k, x in enumerate(outs[0:15])]
    return (outs[15][0, 0], outs[16][0, 0], *results)


def solution(mesh):
    placed = (
        P("dom", None),
        P("dom"),
        P("dom"),
        P("dom", None),
        P("dom", None),
        P("dom", None, None),
        P(None, "dom"),
        P(None, "dom", "rep"),
        P("dom", None),
        P(None, "rep"),
        P(None, "rep"),
        P(),
        P(None, "rep"),
        P(),
        P(None, "rep"),
        P(None, "rep"),
        P(),
        P(None, "rep"),
        P(),
        P(None, "rep"),
        P(None, "rep"),
        P(),
        P(None, "rep"),
        P(),
    )
    return jax.shard_map(
        functools.partial(body, mesh.shape["dom"], mesh.shape["rep"]),
        mesh=mesh,
        in_specs=placed,
        out_specs=(P(), P()) + (P(None, "rep"),) * 6 + (P(),) * 3 + (P(None, "rep"),) * 3 + (P(),) * 3,
        check_vma=False,
    )
```

```python
import functools

import jax
import jax.numpy as jnp
from jax import lax
from jax.experimental import pallas as pl
from jax.experimental.pallas import tpu as pltpu
from jax.sharding import PartitionSpec as P

STEP = 5
beta_one = 0.5
beta_two = 0.5
rate_step = 0.03
decay_rate = 0.01
epsilon = 1e-08

BF16, F32, F8, I32 = jnp.bfloat16, jnp.float32, jnp.float8_e4m3fn, jnp.int32
REST_GAIN = 4096.0
TAIL_GAIN = 256.0
FLAG_LANE = 100
ROWS = 512
FINE = 256
AHEAD = 3
LIMIT = 52 << 20
RESIDENT_BYTES = 30 << 20
FEAT_SCALE = 32.0

SMEM = pl.BlockSpec(memory_space=pltpu.SMEM)
VMEM = pl.BlockSpec(memory_space=pltpu.VMEM)
OWN = pl.BlockSpec(memory_space=pltpu.VMEM)
HBM = pl.BlockSpec(memory_space=pltpu.HBM)
ANY = pl.BlockSpec(memory_space=pl.ANY)


def whole_spec(shape):
    return pl.BlockSpec(shape, lambda *_: (0,) * len(shape))


def placed(spec, *arrays):
    return [(a, spec) for a in arrays]


def run(kernel, name, args, outs, scratch=(), flops=0, grid=()):
    pinned = [
        a if any(spec is s for s in (SMEM, VMEM, ANY)) else pltpu.with_memory_space_constraint(a, pltpu.HBM)
        for a, spec in args
    ]
    return pl.pallas_call(
        kernel,
        grid=grid,
        in_specs=[spec for _, spec in args],
        out_specs=[spec for _, _, spec in outs],
        out_shape=[
            jax.ShapeDtypeStruct(shape, kind) if spec is VMEM else pltpu.HBM(shape, kind)
            for shape, kind, spec in outs
        ],
        scratch_shapes=list(scratch),
        name=name,
        cost_estimate=pl.CostEstimate(flops=flops, bytes_accessed=1 << 20, transcendentals=0),
        compiler_params=pltpu.CompilerParams(vmem_limit_bytes=LIMIT),
    )(*pinned)


def dot_nn(left, right):
    return lax.dot_general(left, right, (((1,), (0,)), ((), ())), preferred_element_type=F32)


def dot_nt(left, right):
    return lax.dot_general(left, right, (((1,), (1,)), ((), ())), preferred_element_type=F32)


def dot_tn(left, right):
    return lax.dot_general(left, right, (((0,), (0,)), ((), ())), preferred_element_type=F32)


def scale_of(value):
    most = jnp.maximum(jnp.max(jnp.abs(value)), 1e-30)
    return 256.0 / most, most * (1.0 / 256.0)


def span(start, size):
    return pl.ds(pl.multiple_of(start, size), size)


def rows_at(size, cols=slice(None)):
    return lambda i: (span(i * size, size), cols)


def cols_at(size, base=0):
    return lambda i: (slice(None), span(base + i * size, size))


def all_of(i):
    return (slice(None), slice(None))


def loop(count, step):
    def one(i, carry):
        step(i)
        return carry

    lax.fori_loop(0, count, one, 0)


class Ring:
    def __init__(self, refs, bufs, sems, cut, first=0):
        self.refs, self.bufs, self.sems, self.cut = refs, bufs, sems, cut
        self.begins = pl.program_id(0) == 0
        self.step, self.steps = pl.program_id(0) - first, pl.num_programs(0) - first
        self.depth = bufs[0].shape[0]
        self.slot = lax.rem(self.step, self.depth)

    def copies(self, step, slot):
        return [
            pltpu.make_async_copy(ref.at[self.cut(step)], buf.at[slot], self.sems.at[k, slot])
            for k, (ref, buf) in enumerate(zip(self.refs, self.bufs))
        ]

    def begin(self):
        for step in range(self.depth):

            @pl.when(self.begins & (step < self.steps))
            def _():
                for copy in self.copies(step, step):
                    copy.start()

    def wait(self):
        for copy in self.copies(self.step, self.slot):
            copy.wait()
        return [buf.at[self.slot] for buf in self.bufs]

    def end(self):
        @pl.when(self.step + self.depth < self.steps)
        def _():
            for copy in self.copies(self.step + self.depth, self.slot):
                copy.start()


def ring_scratch(shape, depth=3):
    kinds = (BF16, F8)
    return [pltpu.VMEM((depth, *shape), kind) for kind in kinds] + [pltpu.SemaphoreType.DMA((len(kinds), depth))]


class Stream:
    def __init__(self, sems, *legs):
        self.sems, self.legs = sems, legs

    def copies(self, i):
        return [
            pltpu.make_async_copy(source.at[source_at(i)], target.at[target_at(i)], self.sems.at[k, i])
            for k, (source, source_at, target, target_at) in enumerate(self.legs)
        ]

    def start(self, i):
        for copy in self.copies(i):
            copy.start()

    def wait(self, i):
        for copy in self.copies(i):
            copy.wait()

    def wait_all(self, count):
        loop(count, self.wait)

    def start_first(self, count):
        for i in range(min(AHEAD, count)):
            self.start(i)

    def next(self, i, count):
        self.wait(i)

        @pl.when(i + AHEAD < count)
        def _():
            self.start(i + AHEAD)


def sems(legs, count):
    return pltpu.SemaphoreType.DMA((legs, count))


def pick_rows(send, first, count):
    nodes = lax.broadcasted_iota(I32, (send.shape[0], count), 1) + first
    return jnp.where(send == nodes, 1.0, 0.0).astype(BF16)


def pack_kernel(feat_t, send_list, changed, mask, first_t, second_t, cache_t, bias, rows_out, pack_out, send):
    nodes, halo = feat_t.shape[1], send.shape[0]
    parts, bound = send_list.shape
    turned = send_list[...].astype(F32)
    turned = jnp.concatenate([turned, jnp.zeros((parts, 128 - bound), F32)], axis=1)
    turned = turned.T.astype(I32)
    for q in range(parts):
        send[q * bound : (q + 1) * bound, :] = turned[0:bound, q : q + 1]
    width, cols = feat_t.shape[0], first_t.shape[0]

    def pick(i, total):
        return total + dot_nt(pick_rows(send[...], i * ROWS, ROWS), feat_t[:, span(i * ROWS, ROWS)])

    total = lax.fori_loop(0, nodes // ROWS, pick, jnp.zeros((halo, width), F32))
    count = jnp.sum(mask[...].astype(F32))
    many = jnp.floor(count * (1.0 / 64.0))
    lane = lax.broadcasted_iota(I32, (halo, 128), 1)
    row = jnp.concatenate([total, jnp.zeros((halo, 128 - width), F32)], axis=1)
    for layer in range(3):
        row = jnp.where(lane == FLAG_LANE + layer, changed[0:1, layer : layer + 1].astype(F32), row)
    row = jnp.where(lane == FLAG_LANE + 3, many, row)
    row = jnp.where(lane == FLAG_LANE + 4, count - 64.0 * many, row)
    rows_out[...] = row.astype(BF16).reshape(rows_out.shape)

    units = second_t.shape[1]
    pack_out[:, 0:128] = jnp.concatenate(
        [first_t[...], jnp.zeros((cols, 128 - width), F32)], axis=1
    ).astype(BF16)
    pack_out[:, 128 : 128 + units] = second_t[...].astype(BF16)
    left = jnp.concatenate([bias[...], jnp.zeros((2, 128 - cols), F32)], axis=1)
    terms = []
    for _ in range(3):
        term = left.astype(BF16).astype(F32)
        terms.append(term)
        left = left - term
    terms = jnp.concatenate(terms + [jnp.zeros((122, 128), F32)], axis=0).T
    pack_out[:, 128 + units : 256 + units] = terms[0:cols, :].astype(BF16)
    base = 256 + units
    for layer in range(2):
        pack_out[:, base + layer * halo : base + (layer + 1) * halo] = cache_t[layer]


def bias_column(packs, layer):
    units = packs.shape[0]
    terms = packs[:, 128 + units : 256 + units].astype(F32)
    return terms[:, layer : layer + 1] + terms[:, layer + 2 : layer + 3] + terms[:, layer + 4 : layer + 5]


def stale_columns(packs, layer, halo):
    base = 256 + packs.shape[0] + layer * halo
    return packs[:, base : base + halo].astype(F32)


def table_kernel(place, pack, pack_one, pack_two, pack_three, feat_hbm, packs, most_out, table_hbm, feat_t, table, in_sems, out_sems):
    width, nodes = feat_t.shape
    units = packs.shape[0]
    extra = jnp.zeros((table.shape[0] - units - width, ROWS), BF16)
    steps = nodes // ROWS
    blocks = Stream(in_sems, (feat_hbm, cols_at(ROWS), feat_t, cols_at(ROWS)))
    stores = Stream(out_sems, (table, cols_at(ROWS), table_hbm, cols_at(ROWS)))
    loop(steps, blocks.start)
    for k, ref in enumerate((pack, pack_one, pack_two, pack_three)):
        packs[span(jnp.bitwise_xor(place[0] + 2 * place[1], k) * 64, 64), :] = ref[...]
    weight = packs[:, 0:width]

    def step(i, most):
        blocks.wait(i)
        here = span(i * ROWS, ROWS)
        z = dot_nn(weight, feat_t[:, here])
        table[0:units, here] = z.astype(BF16)
        table[units:, here] = jnp.concatenate([feat_t[:, here], extra], axis=0)
        stores.start(i)
        return jnp.maximum(most, lane_most(z))

    most = lax.fori_loop(0, steps, step, jnp.zeros((packs.shape[0], 128), F32))
    most_out[...] = most
    stores.wait_all(steps)


def lane_most(value):
    most = jnp.abs(value[:, 0:128])
    for first in range(128, value.shape[1], 128):
        most = jnp.maximum(most, jnp.abs(value[:, first : first + 128]))
    return most


def gelu_both(u):
    square = u * u
    t = jnp.tanh(0.79788456 * (u + 0.044715 * u * square))
    half = 0.5 * (1.0 + t)
    slope = half + 0.5 * u * (1.0 - t * t) * (0.79788456 * (1.0 + 3.0 * 0.044715 * square))
    return u * half, slope


def layer_one_kernel(place, src_t, norm_t, rows, send, most, packs_hbm, table_hbm, z_send, flags_t, high_hbm, rest_hbm, hidden_hbm, slope_hbm, z_hbm, near_hbm, packs, table, table8, high, rest, hidden_t, slope_t, z_own, near_feat, in_sems, edge_sems, out_sems):
    slots = src_t.shape[0]
    units, half = hidden_t.shape
    nodes = 2 * half
    halo = send.shape[0]
    blocks = high.shape[1] // 256
    per_group = 256 // slots
    steps = half // FINE
    fetch = Stream(in_sems, (packs_hbm, all_of, packs, all_of), (table_hbm, all_of, table, lambda i: (slice(None), slice(0, nodes))))
    fetch.start(0)
    depth = high.shape[0] // FINE
    around = lambda i, count: i if depth >= steps else lax.rem(i, count)
    slot_of = lambda i: span(around(i, depth) * FINE, FINE)
    slot_at = lambda i: (slot_of(i), slice(None))
    edge_stores = Stream(edge_sems, (high, slot_at, high_hbm, rows_at(FINE)), (rest, slot_at, rest_hbm, rows_at(FINE)))
    stores = Stream(
        out_sems,
        *[
            (a, cols_at(FINE), b, cols_at(FINE))
            for a, b in ((hidden_t, hidden_hbm), (slope_t, slope_hbm), (z_own, z_hbm), (near_feat, near_hbm))
        ],
    )
    in_slot = lax.broadcasted_iota(I32, (8, 128), 1) // per_group == lax.broadcasted_iota(I32, (8, 128), 0)
    node_row = lax.broadcasted_iota(I32, (per_group, 256), 0)
    mine = lax.rem(lax.broadcasted_iota(I32, (per_group, 256), 1), per_group) == node_row
    inner = lax.broadcasted_iota(I32, (256, 256), 0)

    def lean(tile):
        return [
            pltpu.roll(tile[first : first + 8, :], 0, 1, stride=per_group, stride_axis=0)
            for first in range(0, slots, 8)
        ]

    def flat(tiles, group):
        moved = [pltpu.roll(tile, (128 - per_group * group) % 128, 1) for tile in tiles]
        return jnp.concatenate(
            [jnp.sum(jnp.where(in_slot, tile, 0), axis=0, keepdims=True) for tile in moved], axis=1
        )

    def one(at, weight):
        weight_high = weight.astype(BF16).astype(F32)
        hit = inner == jnp.bitwise_and(at, 255)
        right = jnp.where(hit, weight_high, 0.0).astype(BF16)
        right_rest = jnp.where(hit, (weight - weight_high) * REST_GAIN, 0.0).astype(BF16)
        block = jnp.where(mine, jnp.right_shift(at, 8), -1)
        left = jnp.concatenate(
            [jnp.where(block == j, 1.0, 0.0).astype(BF16) for j in range(blocks)], axis=0
        )
        return dot_nt(left, right), dot_nt(left, right_rest)

    def build(i):
        here = span(place[0] * half + i * 128, 128)
        at, weight = src_t[:, here], norm_t[:, here]
        slot = lax.broadcasted_iota(I32, at.shape, 0)
        merged, repeat = weight, slot < 0
        for shift in range(1, slots):
            same = at == pltpu.roll(at, shift, 0)
            merged = merged + jnp.where(same, pltpu.roll(weight, shift, 0), 0.0)
            repeat = repeat | (same & (slot >= shift))
        source, weights = lean(at), lean(jnp.where(repeat, 0.0, merged))
        pairs = [one(flat(source, group), flat(weights, group)) for group in range(128 // per_group)]
        rows = span(around(i, high.shape[0] // 128) * 128, 128)
        for j in range(blocks):
            cols = slice(256 * j, 256 * (j + 1))
            for ref, parts in zip((high, rest), zip(*pairs)):
                piece = jnp.concatenate([p[per_group * j : per_group * (j + 1), :] for p in parts], axis=0)
                ref[rows, cols] = piece.astype(ref.dtype)

    def build_block(i):
        for k in range(FINE // 128):
            build(i * (FINE // 128) + k)
        edge_stores.start(i)

    flat_rows = rows[...].reshape(halo, 128)
    turned = flat_rows.astype(F32).T
    flags = turned[FLAG_LANE : FLAG_LANE + 8, :]
    counts = jnp.sum(rows[...].astype(F32)[:, 0, :], axis=0, keepdims=True)
    count = 64.0 * counts[:, FLAG_LANE + 3 : FLAG_LANE + 4] + counts[:, FLAG_LANE + 4 : FLAG_LANE + 5]
    row = lax.broadcasted_iota(I32, flags.shape, 0)
    flags_t[...] = jnp.where(row == 3, count, flags)
    z_send[...] = jnp.zeros(z_send.shape, BF16)
    loop(FINE // 128, build)
    edge_stores.start(0)
    fetch.wait(0)
    border = dot_nt(packs[:, 0:FLAG_LANE], flat_rows[:, 0:FLAG_LANE]).astype(BF16).astype(F32)
    border = jnp.where(flags[0:1, :] == 1.0, border, stale_columns(packs, 0, halo))
    table[0:units, nodes : nodes + halo] = border.astype(BF16)
    extra = table.shape[0] - units
    kept = lax.broadcasted_iota(I32, (extra, halo), 0) < FLAG_LANE
    kept = kept & (flags[0:1, :] == 1.0)
    table[units:, nodes : nodes + halo] = jnp.where(kept, turned[0:extra, :], 0.0).astype(BF16)
    scale, back = scale_of(jnp.maximum(jnp.max(most[...]), jnp.max(jnp.abs(border))))
    row = lax.broadcasted_iota(I32, (table.shape[0], 1), 0)
    scale = jnp.where(row < units, scale, FEAT_SCALE)
    back = jnp.where(row < units, back, 1.0 / FEAT_SCALE) * (1.0 / REST_GAIN)
    bias = bias_column(packs, 0)
    unused = jnp.zeros((table8.shape[0] - table.shape[0], 256), F32)

    def small(i):
        here = span(i * 256, 256)
        value = table[:, here].astype(F32) * scale
        table8[:, here] = jnp.concatenate([value, unused], axis=0).astype(F8)

    loop((nodes + halo) // 256, small)

    def sums(i):
        here = slot_of(i)
        low = dot_nt(table8[...], rest[here, :])[0 : table.shape[0]]
        return dot_nt(table[...], high[here, :]) + low * back

    def keep(i, total):
        here = span(i * FINE, FINE)
        slope_t[:, here] = total[0:units]
        value = total[units:]
        top = value.astype(BF16)
        near_feat[0:extra, here] = top
        near_feat[extra:, here] = (value - top.astype(F32)).astype(BF16)

    def finish(i):
        here = span(i * FINE, FINE)
        value, slope = gelu_both(slope_t[:, here] + bias)
        value = value.astype(BF16)
        hidden_t[:, here] = value
        slope_t[:, here] = slope
        z = dot_nn(packs[:, 128 : 128 + units], value).astype(BF16)
        z_own[:, here] = z
        stores.start(i)
        chosen = dot_nt(pick_rows(send[...], place[0] * half + i * FINE, FINE), z)
        z_send[...] = (z_send[...].astype(F32) + chosen.reshape(z_send.shape)).astype(BF16)

    def step(i, carry):
        if depth < steps:

            @pl.when(i + 1 >= depth)
            def _():
                edge_stores.wait(i + 1 - depth)

        total = sums(i)
        finish(i - 1)
        build_block(i + 1)
        keep(i, total)
        return carry

    keep(0, sums(0))
    build_block(1)
    lax.fori_loop(1, steps - 1, step, 0)
    keep(steps - 1, sums(steps - 1))
    finish(steps - 2)
    finish(steps - 1)
    stores.wait_all(steps)
    for i in range(steps - depth, steps):
        edge_stores.wait(i)


def own_part_kernel(place, high, rest, z_own, z_oth, total, table, table8, back, hbuf, rbuf, sems):
    half = z_own.shape[1]
    nodes = 2 * half
    ring = Ring((high, rest), (hbuf, rbuf), sems, lambda i: (span(i * FINE, FINE), slice(0, nodes)))
    ring.begin()

    @pl.when(pl.program_id(0) == 0)
    def _():
        def larger(i, most):
            here = span(i * ROWS, ROWS)
            both = jnp.maximum(jnp.abs(z_own[:, here].astype(F32)), jnp.abs(z_oth[:, here].astype(F32)))
            return jnp.maximum(most, both)

        most = lax.fori_loop(0, half // ROWS, larger, jnp.zeros((z_own.shape[0], ROWS), F32))
        scale, inverse = scale_of(most)
        back[0] = inverse * (1.0 / REST_GAIN)
        for ref, first in ((z_own, place[0] * half), (z_oth, (1 - place[0]) * half)):

            def put(i, carry):
                value = ref[:, span(i * ROWS, ROWS)]
                cols = span(first + i * ROWS, ROWS)
                table[:, cols] = value
                table8[:, cols] = (value.astype(F32) * scale).astype(F8)
                return carry

            lax.fori_loop(0, half // ROWS, put, 0)

    top, low = ring.wait()
    total[...] = dot_nt(table[...], top[...]) + dot_nt(table8[...], low[...]) * back[0]
    ring.end()


def padded_rows(ref, count):
    value = ref[...]
    extra = jnp.zeros((count - value.shape[0], value.shape[1]), value.dtype)
    return jnp.concatenate([value, extra], axis=0).astype(BF16)


def border_cut(nodes, halo):
    return lambda i: (span(i * ROWS, ROWS), slice(nodes, nodes + halo))


def layer_two_end_kernel(place, flags_t, packs, send, high, rest, total, came, came_oth, last_t, hidden_t, slope_t, z_own, z_send, border, border8, back):
    halo = send.shape[0]
    width = hidden_t.shape[0]
    kinds = z_own.shape[0]
    step = pl.program_id(0)
    half = ROWS * pl.num_programs(0)

    @pl.when(step == 0)
    def _():
        both = came[...].reshape(halo, width).astype(F32) + came_oth[...].reshape(halo, width).astype(F32)
        value = jnp.where(flags_t[1:2, :] == 1.0, both.T, stale_columns(packs, 1, halo))
        scale, inverse = scale_of(value)
        border[...] = value.astype(BF16)
        border8[...] = (value * scale).astype(F8)
        back[0] = inverse * (1.0 / REST_GAIN)
        z_send[...] = jnp.zeros(z_send.shape, BF16)

    sums = total[...] + dot_nt(border[...], high[...]) + dot_nt(border8[...], rest[...]) * back[0]
    value, slope = gelu_both(sums + bias_column(packs, 1))
    value = value.astype(BF16)
    hidden_t[...] = value
    slope_t[...] = slope
    z = dot_nn(padded_rows(last_t, kinds), value).astype(BF16)
    z_own[...] = z
    chosen = dot_nt(pick_rows(send[...], place[0] * half + step * ROWS, ROWS), z)
    chosen = jnp.concatenate([chosen, jnp.zeros((halo, 128 - kinds), F32)], axis=1)
    z_send[...] = (z_send[...].astype(F32) + chosen.reshape(z_send.shape)).astype(BF16)


def put_border(border_grad, total, keep):
    value = (total * keep).T
    bound = value.shape[0] // border_grad.shape[0]
    border_grad[:, 0:bound, :] = value.reshape(border_grad.shape[0], bound, value.shape[1])


def loss_kernel(classes, place, flags_t, came, came_oth, stale_t, bias, labels, mask, total_hbm, high, rest, sums, back_out, border_grad, grads_hbm, grads8_hbm, far_hbm, border_sum, hrows, rrows, total, grads, grads8, far, hbuf, rbuf, in_sems, edge_sems, out_sems, far_sems):
    kinds, half = total.shape
    halo = stale_t.shape[1]
    steps = half // ROWS
    cut = border_cut(2 * half, halo)
    blocks = Stream(
        in_sems,
        (high, cut, hrows, rows_at(ROWS)),
        (rest, cut, rrows, rows_at(ROWS)),
        (total_hbm, cols_at(ROWS), total, cols_at(ROWS)),
    )
    others = rows_at(ROWS, span((1 - place[0]) * half, half))
    edges = Stream(edge_sems, (high, others, hbuf, rows_at(ROWS)), (rest, others, rbuf, rows_at(ROWS)))
    stores = Stream(
        out_sems, *[(a, cols_at(ROWS), b, cols_at(ROWS)) for a, b in ((grads, grads_hbm), (grads8, grads8_hbm))]
    )
    far_stores = Stream(far_sems, (far, all_of, far_hbm, all_of))
    blocks.start_first(steps)
    edges.start(0)
    both = came[...].reshape(halo, 128).astype(F32) + came_oth[...].reshape(halo, 128).astype(F32)
    old = jnp.concatenate([stale_t[...].astype(F32), jnp.zeros((kinds - classes, halo), F32)], axis=0)
    value = jnp.where(flags_t[2:3, :] == 1.0, both.T[0:kinds, :], old)
    scale, back = scale_of(value)
    back = back * (1.0 / REST_GAIN)
    border = value.astype(BF16)
    border8 = (value * scale).astype(F8)
    row = jnp.concatenate([bias[...], jnp.zeros((1, 128 - classes), F32)], axis=1)
    bias_col = jnp.broadcast_to(row, (8, 128)).T[0:kinds, 0:1]
    sums[...] = jnp.zeros(sums.shape, F32)
    border_sum[...] = jnp.zeros(border_sum.shape, F32)
    count = flags_t[3:4, 0:1]
    inverse = (1.0 / (256.0 * REST_GAIN)) / count
    back_out[...] = jnp.broadcast_to(inverse, back_out.shape)

    def far_step(i):
        edges.wait(i)
        here = span(i * ROWS, ROWS)
        both = dot_nn(grads[:, here], hbuf[here, :])
        low = dot_nn(grads8[:, here], rbuf[here, :]) * inverse
        far[...] += both[0:kinds] + both[kinds : 2 * kinds] + low

    def step(i):
        here = span(i * ROWS, ROWS)
        logits = total[:, here] + dot_nt(border, hrows[here, :]) + dot_nt(border8, rrows[here, :]) * back
        logits = logits + bias_col
        kind = lax.broadcasted_iota(I32, logits.shape, 0)
        real = kind < classes
        logits = jnp.where(real, logits, -jnp.inf)
        shifted = logits - jnp.max(logits, axis=0, keepdims=True)
        powers = jnp.exp(shifted)
        norm = jnp.sum(powers, axis=0, keepdims=True)
        logp = jnp.where(real, shifted - jnp.log(norm), 0.0)
        first = (place[0] * steps + i) * (ROWS // 128)
        row_of = lambda ref: jnp.concatenate([ref[pl.ds(first + k, 1), :] for k in range(ROWS // 128)], axis=1)
        target = jnp.where(kind == row_of(labels), 0.9, 0.0) + 0.1 / classes
        used = row_of(mask).astype(F32)
        loss = jnp.sum(target * logp, axis=0, keepdims=True) * used
        grad = jnp.where(real, (powers / norm - target) * (used / count), 0.0)
        sums[0:kinds, :] += lane_sums(grad)
        sums[kinds : kinds + 1, :] -= lane_sums(loss)
        top = grad.astype(BF16)
        tail = (grad - top.astype(F32)).astype(BF16)
        stacked = jnp.concatenate([top, tail], axis=0)
        small = (top.astype(F32) * (256.0 * count)).astype(F8)
        grads[:, here] = stacked
        grads8[:, here] = small
        stores.start(i)
        both = dot_nn(stacked, hrows[here, :])
        low = dot_nn(small, rrows[here, :]) * inverse
        border_sum[0:kinds, :] += both[0:kinds] + both[kinds : 2 * kinds] + low

    far[...] = jnp.zeros(far.shape, F32)
    blocks.next(0, steps)
    edges.start(1)
    step(0)

    def both_steps(i):
        blocks.next(i, steps)

        @pl.when(i + 1 < steps)
        def _():
            edges.start(i + 1)

        far_step(i - 1)
        step(i)

    lax.fori_loop(1, steps, lambda i, c: (both_steps(i), c)[1], 0)
    far_step(steps - 1)
    far_stores.start(0)
    put_border(border_grad, border_sum[...], flags_t[2:3, :])
    stores.wait_all(steps)
    far_stores.wait(0)


def lane_sums(value):
    total = value[:, 0:128]
    for first in range(128, value.shape[1], 128):
        total = total + value[:, first : first + 128]
    return total


def back_three_kernel(place, high, rest, grads, grads8, back, out, hbuf, rbuf, sems):
    kinds, size = out.shape
    base = place[0] * size * pl.num_programs(0)
    ring = Ring((high, rest), (hbuf, rbuf), sems, lambda i: (slice(None), span(base + i * size, size)))
    ring.begin()
    top, low = ring.wait()
    both = dot_nn(grads[...], top[...])
    out[...] = both[0:kinds] + both[kinds : 2 * kinds] + dot_nn(grads8[...], low[...]) * back[0:1, 0:1]
    ring.end()


def back_block(grads, grads8, tails8, back_rest, back_tail, top, low):
    total = dot_nn(grads, top) + dot_nn(grads8, low) * back_rest
    return total + dot_nn(tails8, top.astype(F8)) * back_tail


def back_kernel(place, back, grads_hbm, grads8_hbm, tails8_hbm, high, rest, out_hbm, out, grads, grads8, tails8, hbuf, rbuf, in_sems, edge_sems, out_sems):
    half = out.shape[1]
    steps = half // ROWS
    mine = cols_at(ROWS, place[0] * half)
    fetch = Stream(
        in_sems,
        *[(a, all_of, b, all_of) for a, b in ((grads_hbm, grads), (grads8_hbm, grads8), (tails8_hbm, tails8))],
    )
    edges = Stream(edge_sems, (high, mine, hbuf, cols_at(ROWS)), (rest, mine, rbuf, cols_at(ROWS)))
    stores = Stream(out_sems, (out, cols_at(ROWS), out_hbm, cols_at(ROWS)))
    fetch.start(0)
    edges.start(0)
    fetch.wait(0)
    for i in range(1, min(AHEAD, steps)):
        edges.start(i)

    def step(i):
        edges.wait(i)
        here = span(i * ROWS, ROWS)
        out[:, here] = back_block(
            grads[...], grads8[...], tails8[...], back[0:1, 0:1], back[0:1, 1:2], hbuf[:, here], rbuf[:, here]
        )
        stores.start(i)

        @pl.when(i + AHEAD < steps)
        def _():
            edges.start(i + AHEAD)

    loop(steps, step)
    stores.wait_all(steps)


def returned_terms(ret, ret_oth, bound, kinds):
    value = ret[:, 0:bound, :] + ret_oth[:, 0:bound, :]
    value = value.reshape(value.shape[0] * bound, value.shape[2]).T[0:kinds, :]
    top = value.astype(BF16)
    return top, (value - top.astype(F32)).astype(BF16)


def round_gradient(own, came_part, terms, send, first_node):
    chosen = pick_rows(send, first_node, own.shape[1])
    total = own + came_part
    for term in terms:
        total = total + dot_nn(term, chosen)
    return total.astype(BF16)


def end_three_kernel(place, flags_t, ret, ret_oth, last_t, send, far_in_any, near_hbm, hidden_hbm, slope_hbm, high, rest, sums, back_out, border_grad, grads_hbm, grads8_hbm, tails8_hbm, far_hbm, near, far_in, hidden_t, slope_t, hrows, rrows, grad_rows, grad_last, border_sum, grads, grads8, tails8, far, hbuf, rbuf, in_sems, row_sems, out_sems, edge_sems, far_sems):
    kinds, half = near.shape
    units = slope_t.shape[0]
    parts = ret.shape[0]
    bound = send.shape[0] // parts
    halo = send.shape[0]
    steps = half // ROWS
    cut = border_cut(2 * half, halo)
    blocks = Stream(
        in_sems,
        *[
            (a, cols_at(ROWS), b, cols_at(ROWS))
            for a, b in ((near_hbm, near), (far_in_any, far_in), (hidden_hbm, hidden_t), (slope_hbm, slope_t))
        ],
    )
    borders = Stream(row_sems, (high, cut, hrows, rows_at(ROWS)), (rest, cut, rrows, rows_at(ROWS)))
    stores = Stream(
        out_sems,
        *[
            (a, cols_at(ROWS), b, cols_at(ROWS))
            for a, b in ((grads, grads_hbm), (grads8, grads8_hbm), (tails8, tails8_hbm))
        ],
    )
    others = cols_at(ROWS, (1 - place[0]) * half)
    edges = Stream(edge_sems, (high, others, hbuf, cols_at(ROWS)), (rest, others, rbuf, cols_at(ROWS)))
    far_stores = Stream(far_sems, (far, cols_at(ROWS), far_hbm, cols_at(ROWS)))
    for stream in (blocks, borders, edges):
        loop(steps, stream.start)
    terms = returned_terms(ret, ret_oth, bound, kinds)
    weight = padded_rows(last_t, kinds)
    sums[...] = jnp.zeros(sums.shape, F32)
    grad_last[...] = jnp.zeros(grad_last.shape, F32)
    border_sum[...] = jnp.zeros(border_sum.shape, F32)

    def first_step(i, most):
        blocks.wait(i)
        here = span(i * ROWS, ROWS)
        d_z = round_gradient(near[:, here], far_in[:, here], terms, send[...], (place[0] * steps + i) * ROWS)
        grad_last[0:kinds, :] += dot_nt(d_z, hidden_t[:, here])
        grad = dot_tn(weight, d_z) * slope_t[:, here]
        sums[...] += lane_sums(grad)
        grad_rows[:, here] = grad
        return jnp.maximum(most, jnp.max(jnp.abs(grad), axis=0, keepdims=True))

    most = lax.fori_loop(0, steps, first_step, jnp.zeros((1, ROWS), F32))
    scale, back = scale_of(most)
    back_rest, back_tail = back * (1.0 / REST_GAIN), back * (1.0 / TAIL_GAIN)
    lane = lax.broadcasted_iota(I32, back_out.shape, 1)
    back_out[...] = jnp.where(lane == 0, back_rest, back_tail)

    def second_step(i):
        borders.wait(i)
        here = span(i * ROWS, ROWS)
        grad = grad_rows[:, here]
        top = grad.astype(BF16)
        wide = top.astype(F32)
        small = (wide * scale).astype(F8)
        tail = ((grad - wide) * (scale * TAIL_GAIN)).astype(F8)
        grads[:, here] = top
        grads8[:, here] = small
        tails8[:, here] = tail
        stores.start(i)
        border_sum[...] += back_block(top, small, tail, back_rest, back_tail, hrows[here, :], rrows[here, :])

    loop(steps, second_step)
    put_border(border_grad, border_sum[...], flags_t[1:2, :])
    border_grad[:, bound:, :] = grad_last[...].reshape(parts, 64 // parts, units)

    def far_step(i):
        edges.wait(i)
        here = span(i * ROWS, ROWS)
        far[:, here] = back_block(
            grads[...], grads8[...], tails8[...], back_rest, back_tail, hbuf[:, here], rbuf[:, here]
        )
        far_stores.start(i)

    loop(steps, far_step)
    far_stores.wait_all(steps)
    stores.wait_all(steps)


def end_two_kernel(place, ret, ret_oth, packs, send, sums_two, sums_out, far_any, near_hbm, hidden_hbm, slope_hbm, feat_hbm, out, out_one, last_chunk, near, far, hidden_t, slope_t, near_feat, grad_first, grad_second, sums_one, in_sems):
    units, half = near.shape
    parts = ret.shape[0]
    bound = send.shape[0] // parts
    steps = half // ROWS
    extra = near_feat.shape[0] // 2
    blocks = Stream(
        in_sems,
        *[
            (a, cols_at(ROWS), b, cols_at(ROWS))
            for a, b in (
                (near_hbm, near),
                (far_any, far),
                (hidden_hbm, hidden_t),
                (slope_hbm, slope_t),
                (feat_hbm, near_feat),
            )
        ],
    )
    loop(steps, blocks.start)
    terms = returned_terms(ret, ret_oth, bound, units)
    last_chunk[...] = jnp.sum(ret[:, bound:, :] + ret_oth[:, bound:, :], axis=0)
    weight = packs[:, 128 : 128 + units]
    for ref in (grad_first, grad_second, sums_one):
        ref[...] = jnp.zeros(ref.shape, F32)

    def step(i):
        blocks.wait(i)
        here = span(i * ROWS, ROWS)
        d_z = round_gradient(near[:, here], far[:, here], terms, send[...], (place[0] * steps + i) * ROWS)
        grad_second[...] += dot_nt(d_z, hidden_t[:, here])
        grad = dot_tn(weight, d_z) * slope_t[:, here]
        sums_one[...] += lane_sums(grad)
        top = grad.astype(BF16)
        tail = (grad - top.astype(F32)).astype(BF16)
        high, low = near_feat[0:extra, here], near_feat[extra:, here]
        grad_first[:, 0:extra] += dot_nt(top, high) + (dot_nt(tail, high) + dot_nt(top, low))

    loop(steps, step)
    lane = lax.broadcasted_iota(I32, (64, 128), 1)
    column = lambda value: jnp.sum(value, axis=1, keepdims=True)
    for k, ref in enumerate((out, out_one)):
        rows = span(jnp.bitwise_xor(place[0] + 2 * place[1], k) * 64, 64)
        value = jnp.where(lane < FLAG_LANE, grad_first[rows, :], 0.0)
        value = jnp.where(lane == FLAG_LANE, column(sums_one[rows, :]), value)
        value = jnp.where(lane == FLAG_LANE + 1, column(sums_two[rows, :]), value)
        ref[0:64, :] = jnp.where(lane == FLAG_LANE + 2, column(sums_out[...]), value)
        ref[64:128, :] = grad_second[rows, 0:128]
        ref[128:192, :] = grad_second[rows, 128:256]


def scatter_kernel(mine, came, last_chunk, out):
    total = mine[...] + came[...]
    parts, size = out.shape[0], last_chunk.shape[0]
    for q in range(parts):
        pieces = [total[64 * k + q * size : 64 * k + (q + 1) * size, :] for k in range(3)]
        pieces += [last_chunk[:, 0:128], last_chunk[:, 128:256]]
        out[q] = jnp.concatenate(pieces, axis=0)


def joined(came, first, size):
    return came[:, first : first + size, :].reshape(64, 128)


def gather_kernel(came, out, grad_last):
    parts = came.shape[0]
    size = 64 // parts
    value = jnp.sum(came[:, 0 : 3 * size, :], axis=0)
    for p in range(parts):
        out[p] = value
    grad_last[...] = jnp.concatenate([joined(came, 3 * size, size), joined(came, 4 * size, size)], axis=1)


def adamw(weight, moment, square, gradient):
    moment = beta_one * moment + (1.0 - beta_one) * gradient
    square = beta_two * square + (1.0 - beta_two) * gradient * gradient
    moment_hat = moment / (1.0 - beta_one**STEP)
    square_hat = square / (1.0 - beta_two**STEP)
    weight = weight - rate_step * (
        moment_hat / (jnp.sqrt(square_hat) + epsilon) + decay_rate * weight
    )
    return (weight, moment, square)


def update_kernel(came, grad_last, flags_t, *refs):
    params, outs = refs[0:15], refs[15:]
    parts = came.shape[0]
    size = 64 // parts
    width, kinds = params[0].shape[1], params[6].shape[0]
    total = joined(came, 0, size)
    halves = [joined(came, size, size), joined(came, 2 * size, size)]
    turned = jnp.concatenate([total, jnp.zeros((64, 128), F32)], axis=0).T
    gradients = (
        total[:, 0:width],
        jnp.concatenate(halves, axis=1),
        grad_last[0:kinds, :],
        turned[FLAG_LANE : FLAG_LANE + 2, 0:64],
        turned[FLAG_LANE + 2 : FLAG_LANE + 3, 0:kinds],
    )
    for k, gradient in enumerate(gradients):
        values = adamw(*[ref[...] for ref in params[3 * k : 3 * k + 3]], gradient)
        for ref, value in zip(outs[3 * k : 3 * k + 3], values):
            ref[...] = value
    padded = turned[FLAG_LANE + 2 : FLAG_LANE + 3, 48:49]
    outs[15][...] = jnp.broadcast_to(padded, (1, 128))
    outs[16][...] = jnp.broadcast_to(flags_t[3:4, 0:1], (1, 128))


def body(
    parts,
    reps,
    features,
    labels,
    train_mask,
    edge_src,
    edge_norm,
    send_rows,
    changed,
    cache_hidden,
    cache_out,
    first_weight,
    second_weight,
    last_weight,
    hidden_bias,
    out_bias,
    moment_first,
    moment_second,
    moment_last,
    moment_hidden,
    moment_out,
    square_first,
    square_second,
    square_last,
    square_hidden,
    square_out,
):
    nodes, in_width = features.shape
    half = nodes // 2
    bound = send_rows.shape[2]
    halo = parts * bound
    table = nodes + halo
    units, classes = last_weight.shape
    kinds = -(-classes // 16) * 16
    steps, fine = half // ROWS, half // FINE

    rep = lax.axis_index("rep")
    place = jnp.stack([lax.rem(rep, 2), lax.div(rep, 2)]).astype(I32)
    where = (place, SMEM)
    feat_t = features.T
    last_t = last_weight.T
    label_rows = labels.reshape(nodes // 128, 128)
    mask_rows = train_mask.reshape(nodes // 128, 128)

    def swap(x, k=1):
        return lax.ppermute(x, "rep", [(i, i ^ k) for i in range(reps)])

    def exchange(x):
        return lax.all_to_all(x, "dom", split_axis=0, concat_axis=0, tiled=True)

    def late(after, *arrays):
        return lax.optimization_barrier((*arrays, after))

    vm = pltpu.VMEM
    whole = lambda a: (a, whole_spec(a.shape))
    work = 2 * half * table * units
    pack_width = 256 + units + 2 * halo
    extra = -(-in_width // 16) * 16
    both = units + extra
    rows_out, pack, send = run(
        pack_kernel,
        "pack",
        [
            whole(feat_t),
            whole(send_rows.reshape(parts, bound)),
            whole(changed.T),
            *[whole(a) for a in (mask_rows, first_weight.T, second_weight.T)],
            *[whole(a) for a in (jnp.transpose(cache_hidden, (0, 2, 1)), hidden_bias)],
        ],
        [
            ((parts, bound, 128), BF16, VMEM),
            ((units // reps, pack_width), BF16, VMEM),
            ((halo, 1), I32, VMEM),
        ],
        flops=2 * halo * nodes * 128,
        grid=(1,),
    )
    packs = [pack if k == 0 else swap(pack, k) for k in range(reps)]
    rows = exchange(rows_out)
    node_block = lambda size, rows: pl.BlockSpec((rows, size), lambda i: (0, i))
    block, fine_block = node_block(ROWS, units), node_block(FINE, units)
    scalar = pltpu.SMEM((1,), F32)
    packs, most, first_table = run(
        table_kernel,
        "table",
        [where, *placed(VMEM, *packs), (feat_t, HBM)],
        [((units, pack_width), BF16, OWN), ((units, 128), F32, VMEM), ((units + extra, nodes), BF16, HBM)],
        [
            vm((in_width, nodes), BF16),
            vm((units + extra, nodes), BF16),
            sems(1, nodes // ROWS),
            sems(1, nodes // ROWS),
        ],
        flops=2 * units * nodes * in_width,
    )
    rows, most = late(most, rows)
    held = fine if half * table * 3 <= RESIDENT_BYTES else min(fine, 4)
    z_send, flags_t, high, rest, hidden_one, slope_one, z_own, near_feat = run(
        layer_one_kernel,
        "layer_one",
        [where, *placed(OWN, edge_src.T, edge_norm.T), *placed(VMEM, rows, send, most), *placed(HBM, packs, first_table)],
        [
            ((parts, bound, units), BF16, VMEM),
            ((8, halo), F32, OWN),
            ((half, table), BF16, HBM),
            ((half, table), F8, HBM),
            ((units, half), BF16, HBM),
            ((units, half), F32, HBM),
            ((units, half), BF16, HBM),
            ((2 * extra, half), BF16, HBM),
        ],
        [
            vm((units, pack_width), BF16),
            vm((both, table), BF16),
            vm((-(-both // 32) * 32, table), F8),
            vm((held * FINE, table), BF16),
            vm((held * FINE, table), F8),
            vm((units, half), BF16),
            vm((units, half), F32),
            vm((units, half), BF16),
            vm((2 * extra, half), BF16),
            sems(2, 1),
            sems(2, fine),
            sems(4, fine),
        ],
        flops=2 * work,
    )
    edge = placed(HBM, high, rest)

    def own_part(z_own, z_oth, name):
        n = z_own.shape[0]
        return run(
            own_part_kernel,
            name,
            [where, *edge, whole(z_own), (z_oth, VMEM)],
            [((n, half), F32, node_block(FINE, n))],
            [vm((n, nodes), BF16), vm((n, nodes), F8), scalar, *ring_scratch((FINE, nodes))],
            flops=work,
            grid=(fine,),
        )[0]

    z_oth = swap(z_own)
    came = exchange(z_send)
    total = own_part(z_own, z_oth, "layer_two_own")
    came, total = late(total, came)
    came_oth = swap(came)
    border_block = lambda array: (array, pl.BlockSpec((ROWS, halo), lambda i: (i, nodes // halo)))
    hidden_two, slope_two, z_own, z_send = run(
        layer_two_end_kernel,
        "layer_two_end",
        [where, whole(flags_t), whole(packs), (send, VMEM), border_block(high), border_block(rest), (total, block)]
        + placed(VMEM, came, came_oth)
        + [whole(last_t)],
        [
            ((units, half), BF16, block),
            ((units, half), F32, block),
            ((kinds, half), BF16, node_block(ROWS, kinds)),
            ((parts, bound, 128), BF16, whole_spec((parts, bound, 128))),
        ],
        [vm((units, halo), BF16), vm((units, halo), F8), scalar],
        flops=work // 4,
        grid=(steps,),
    )
    z_oth = swap(z_own)
    came = exchange(z_send)
    total = own_part(z_own, z_oth, "layer_three_own")
    came, total = late(total, came)
    came_oth = swap(came)
    border_rows = [vm((half, halo), BF16), vm((half, halo), F8)]
    sums_out, back, border_grad, grads, grads8, far = run(
        functools.partial(loss_kernel, classes),
        "loss",
        [
            where,
            *placed(VMEM, flags_t, came, came_oth, cache_out.T, out_bias.reshape(1, classes), label_rows, mask_rows),
            (total, HBM),
            *edge,
        ],
        [
            ((64, 128), F32, VMEM),
            ((8, 128), F32, VMEM),
            ((parts, bound, 128), F32, VMEM),
            ((2 * kinds, half), BF16, HBM),
            ((kinds, half), F8, HBM),
            ((kinds, half), F32, HBM),
        ],
        [
            vm((128, halo), F32),
            *border_rows,
            vm((kinds, half), F32),
            vm((2 * kinds, half), BF16),
            vm((kinds, half), F8),
            vm((kinds, half), F32),
            vm((half, half), BF16),
            vm((half, half), F8),
            sems(3, steps),
            sems(2, steps),
            sems(2, steps),
            sems(1, 1),
        ],
        flops=work,
    )
    far = swap(far)
    ret = exchange(border_grad)
    near = run(
        back_three_kernel,
        "back_three",
        [where, *edge, whole(grads), whole(grads8), (back, VMEM)],
        [((kinds, half), F32, node_block(FINE, kinds))],
        ring_scratch((half, FINE)),
        flops=work // 2,
        grid=(fine,),
    )[0]
    ret, far, near = late(near, ret, far)
    ret_oth = swap(ret)
    chunk = 64 // parts

    sums_two, back, border_grad, grads, grads8, tails8, far = run(
        end_three_kernel,
        "end_three",
        [where, *placed(VMEM, flags_t, ret, ret_oth, last_t, send), (far, ANY)]
        + [*placed(HBM, near, hidden_two, slope_two), *edge],
        [
            ((units, 128), F32, VMEM),
            ((8, 128), F32, VMEM),
            ((parts, bound + chunk, units), F32, VMEM),
            ((units, half), BF16, HBM),
            ((units, half), F8, HBM),
            ((units, half), F8, HBM),
            ((units, half), F32, HBM),
        ],
        [
            vm((kinds, half), F32),
            vm((kinds, half), F32),
            vm((units, half), BF16),
            vm((units, half), F32),
            *border_rows,
            vm((units, half), F32),
            vm((64, units), F32),
            vm((units, halo), F32),
            vm((units, half), BF16),
            vm((units, half), F8),
            vm((units, half), F8),
            vm((units, half), F32),
            vm((half, half), BF16),
            vm((half, half), F8),
            sems(4, steps),
            sems(2, steps),
            sems(3, steps),
            sems(2, steps),
            sems(1, steps),
        ],
        flops=work,
    )
    far = swap(far)
    ret = exchange(border_grad)
    near = run(
        back_kernel,
        "back",
        [where, (back, VMEM), *placed(HBM, grads, grads8, tails8), *edge],
        [((units, half), F32, HBM)],
        [
            vm((units, half), F32),
            vm((units, half), BF16),
            vm((units, half), F8),
            vm((units, half), F8),
            vm((half, half), BF16),
            vm((half, half), F8),
            sems(3, 1),
            sems(2, steps),
            sems(1, steps),
        ],
        flops=work // 2,
    )[0]
    ret, far, near = late(near, ret, far)
    ret_oth = swap(ret)
    mine, theirs, last_chunk = run(
        end_two_kernel,
        "end_two",
        [where, *placed(VMEM, ret, ret_oth), (packs, OWN), *placed(VMEM, send, sums_two, sums_out), (far, ANY)]
        + placed(HBM, near, hidden_one, slope_one, near_feat),
        [((192, 128), F32, VMEM)] * 2 + [((chunk, units), F32, VMEM)],
        [
            vm((units, half), F32),
            vm((units, half), F32),
            vm((units, half), BF16),
            vm((units, half), F32),
            vm((2 * extra, half), BF16),
            vm((units, 128), F32),
            vm((units, units), F32),
            vm((units, 128), F32),
            sems(5, steps),
        ],
        flops=work // 4,
    )
    scattered = run(
        scatter_kernel,
        "scatter",
        placed(VMEM, mine, swap(theirs), last_chunk),
        [((parts, 5 * chunk, 128), F32, VMEM)],
    )[0]
    gathered, grad_last = run(
        gather_kernel,
        "gather",
        placed(VMEM, exchange(scattered)),
        [((parts, 3 * chunk, 128), F32, VMEM), ((64, units), F32, VMEM)],
    )
    came = exchange(gathered)

    turn = lambda x: x.T
    same = lambda x: x
    row = lambda x: x.reshape(1, -1)
    forms = (turn, turn, turn, same, row)
    weights = (first_weight, second_weight, last_weight, hidden_bias, out_bias)
    moments = (moment_first, moment_second, moment_last, moment_hidden, moment_out)
    squares = (square_first, square_second, square_last, square_hidden, square_out)
    params = [form(x) for form, triple in zip(forms, zip(weights, moments, squares)) for x in triple]
    outs = run(
        update_kernel,
        "update",
        placed(VMEM, came, grad_last, flags_t, *params),
        [(p.shape, F32, VMEM) for p in params] + [((1, 128), F32, VMEM)] * 2,
    )
    undo = (turn, turn, turn, same, lambda x: x.reshape(-1))
    results = [undo[k // 3](x) for k, x in enumerate(outs[0:15])]
    return (outs[15][0, 0], outs[16][0, 0], *results)


def solution(mesh):
    placed = (
        P("dom", None),
        P("dom"),
        P("dom"),
        P("dom", None),
        P("dom", None),
        P("dom", None, None),
        P(None, "dom"),
        P(None, "dom", "rep"),
        P("dom", None),
        P(None, "rep"),
        P(None, "rep"),
        P(),
        P(None, "rep"),
        P(),
        P(None, "rep"),
        P(None, "rep"),
        P(),
        P(None, "rep"),
        P(),
        P(None, "rep"),
        P(None, "rep"),
        P(),
        P(None, "rep"),
        P(),
    )
    return jax.shard_map(
        functools.partial(body, mesh.shape["dom"], mesh.shape["rep"]),
        mesh=mesh,
        in_specs=placed,
        out_specs=(P(), P()) + (P(None, "rep"),) * 6 + (P(),) * 3 + (P(None, "rep"),) * 3 + (P(),) * 3,
        check_vma=False,
    )
```

```python
import functools

import jax
import jax.numpy as jnp
from jax import lax
from jax.experimental import pallas as pl
from jax.experimental.pallas import tpu as pltpu
from jax.sharding import PartitionSpec as P

STEP = 5
beta_one = 0.5
beta_two = 0.5
rate_step = 0.03
decay_rate = 0.01
epsilon = 1e-08

BF16, F32, F8, I32 = jnp.bfloat16, jnp.float32, jnp.float8_e4m3fn, jnp.int32
REST_GAIN = 4096.0
TAIL_GAIN = 256.0
FLAG_LANE = 100
ROWS = 512
FINE = 256
AHEAD = 3
LIMIT = 52 << 20
LOW_LIMIT = 34 << 20
RESIDENT_BYTES = 30 << 20
FEAT_SCALE = 32.0

SMEM = pl.BlockSpec(memory_space=pltpu.SMEM)
VMEM = pl.BlockSpec(memory_space=pltpu.VMEM)
OWN = pl.BlockSpec(memory_space=pltpu.VMEM)
HBM = pl.BlockSpec(memory_space=pltpu.HBM)
ANY = pl.BlockSpec(memory_space=pl.ANY)


def whole_spec(shape):
    return pl.BlockSpec(shape, lambda *_: (0,) * len(shape))


def placed(spec, *arrays):
    return [(a, spec) for a in arrays]


def run(kernel, name, args, outs, scratch=(), flops=0, grid=(), limit=LIMIT):
    pinned = [
        a if any(spec is s for s in (SMEM, VMEM, ANY)) else pltpu.with_memory_space_constraint(a, pltpu.HBM)
        for a, spec in args
    ]
    return pl.pallas_call(
        kernel,
        grid=grid,
        in_specs=[spec for _, spec in args],
        out_specs=[spec for _, _, spec in outs],
        out_shape=[
            jax.ShapeDtypeStruct(shape, kind) if spec is VMEM else pltpu.HBM(shape, kind)
            for shape, kind, spec in outs
        ],
        scratch_shapes=list(scratch),
        name=name,
        cost_estimate=pl.CostEstimate(flops=flops, bytes_accessed=1 << 20, transcendentals=0),
        compiler_params=pltpu.CompilerParams(vmem_limit_bytes=limit),
    )(*pinned)


def dot_nn(left, right):
    return lax.dot_general(left, right, (((1,), (0,)), ((), ())), preferred_element_type=F32)


def dot_nt(left, right):
    return lax.dot_general(left, right, (((1,), (1,)), ((), ())), preferred_element_type=F32)


def dot_tn(left, right):
    return lax.dot_general(left, right, (((0,), (0,)), ((), ())), preferred_element_type=F32)


def scale_of(value):
    most = jnp.maximum(jnp.max(jnp.abs(value)), 1e-30)
    return 256.0 / most, most * (1.0 / 256.0)


def span(start, size):
    return pl.ds(pl.multiple_of(start, size), size)


def rows_at(size, cols=slice(None)):
    return lambda i: (span(i * size, size), cols)


def cols_at(size, base=0):
    return lambda i: (slice(None), span(base + i * size, size))


def all_of(i):
    return (slice(None), slice(None))


def loop(count, step):
    def one(i, carry):
        step(i)
        return carry

    lax.fori_loop(0, count, one, 0)


class Ring:
    def __init__(self, refs, bufs, sems, cut, first=0):
        self.refs, self.bufs, self.sems, self.cut = refs, bufs, sems, cut
        self.begins = pl.program_id(0) == 0
        self.step, self.steps = pl.program_id(0) - first, pl.num_programs(0) - first
        self.depth = bufs[0].shape[0]
        self.slot = lax.rem(self.step, self.depth)

    def copies(self, step, slot):
        return [
            pltpu.make_async_copy(ref.at[self.cut(step)], buf.at[slot], self.sems.at[k, slot])
            for k, (ref, buf) in enumerate(zip(self.refs, self.bufs))
        ]

    def begin(self):
        for step in range(self.depth):

            @pl.when(self.begins & (step < self.steps))
            def _():
                for copy in self.copies(step, step):
                    copy.start()

    def wait(self):
        for copy in self.copies(self.step, self.slot):
            copy.wait()
        return [buf.at[self.slot] for buf in self.bufs]

    def end(self):
        @pl.when(self.step + self.depth < self.steps)
        def _():
            for copy in self.copies(self.step + self.depth, self.slot):
                copy.start()


def ring_scratch(shape, depth=3):
    kinds = (BF16, F8)
    return [pltpu.VMEM((depth, *shape), kind) for kind in kinds] + [pltpu.SemaphoreType.DMA((len(kinds), depth))]


class Stream:
    def __init__(self, sems, *legs):
        self.sems, self.legs = sems, legs

    def copies(self, i):
        return [
            pltpu.make_async_copy(source.at[source_at(i)], target.at[target_at(i)], self.sems.at[k, i])
            for k, (source, source_at, target, target_at) in enumerate(self.legs)
        ]

    def start(self, i):
        for copy in self.copies(i):
            copy.start()

    def wait(self, i):
        for copy in self.copies(i):
            copy.wait()

    def wait_all(self, count):
        loop(count, self.wait)

    def start_first(self, count):
        for i in range(min(AHEAD, count)):
            self.start(i)

    def next(self, i, count):
        self.wait(i)

        @pl.when(i + AHEAD < count)
        def _():
            self.start(i + AHEAD)


def sems(legs, count):
    return pltpu.SemaphoreType.DMA((legs, count))


def pick_rows(send, first, count):
    nodes = lax.broadcasted_iota(I32, (send.shape[0], count), 1) + first
    return jnp.where(send == nodes, 1.0, 0.0).astype(BF16)


def pack_kernel(feat_t, send_list, changed, mask, first_t, second_t, cache_t, bias, rows_out, pack_out, send):
    nodes, halo = feat_t.shape[1], send.shape[0]
    parts, bound = send_list.shape
    turned = send_list[...].astype(F32)
    turned = jnp.concatenate([turned, jnp.zeros((parts, 128 - bound), F32)], axis=1)
    turned = turned.T.astype(I32)
    for q in range(parts):
        send[q * bound : (q + 1) * bound, :] = turned[0:bound, q : q + 1]
    width, cols = feat_t.shape[0], first_t.shape[0]

    def pick(i, total):
        return total + dot_nt(pick_rows(send[...], i * ROWS, ROWS), feat_t[:, span(i * ROWS, ROWS)])

    total = lax.fori_loop(0, nodes // ROWS, pick, jnp.zeros((halo, width), F32))
    count = jnp.sum(mask[...].astype(F32))
    many = jnp.floor(count * (1.0 / 64.0))
    lane = lax.broadcasted_iota(I32, (halo, 128), 1)
    row = jnp.concatenate([total, jnp.zeros((halo, 128 - width), F32)], axis=1)
    for layer in range(3):
        row = jnp.where(lane == FLAG_LANE + layer, changed[0:1, layer : layer + 1].astype(F32), row)
    row = jnp.where(lane == FLAG_LANE + 3, many, row)
    row = jnp.where(lane == FLAG_LANE + 4, count - 64.0 * many, row)
    rows_out[...] = row.astype(BF16).reshape(rows_out.shape)

    units = second_t.shape[1]
    pack_out[:, 0:128] = jnp.concatenate(
        [first_t[...], jnp.zeros((cols, 128 - width), F32)], axis=1
    ).astype(BF16)
    pack_out[:, 128 : 128 + units] = second_t[...].astype(BF16)
    left = jnp.concatenate([bias[...], jnp.zeros((2, 128 - cols), F32)], axis=1)
    terms = []
    for _ in range(3):
        term = left.astype(BF16).astype(F32)
        terms.append(term)
        left = left - term
    terms = jnp.concatenate(terms + [jnp.zeros((122, 128), F32)], axis=0).T
    pack_out[:, 128 + units : 256 + units] = terms[0:cols, :].astype(BF16)
    base = 256 + units
    for layer in range(2):
        pack_out[:, base + layer * halo : base + (layer + 1) * halo] = cache_t[layer]


def bias_column(packs, layer):
    units = packs.shape[0]
    terms = packs[:, 128 + units : 256 + units].astype(F32)
    return terms[:, layer : layer + 1] + terms[:, layer + 2 : layer + 3] + terms[:, layer + 4 : layer + 5]


def stale_columns(packs, layer, halo):
    base = 256 + packs.shape[0] + layer * halo
    return packs[:, base : base + halo].astype(F32)


def table_kernel(place, pack, pack_one, pack_two, pack_three, feat_hbm, packs, most_out, table_hbm, feat_t, table, in_sems, out_sems):
    width, nodes = feat_t.shape
    units = packs.shape[0]
    extra = jnp.zeros((table.shape[0] - units - width, ROWS), BF16)
    steps = nodes // ROWS
    blocks = Stream(in_sems, (feat_hbm, cols_at(ROWS), feat_t, cols_at(ROWS)))
    stores = Stream(out_sems, (table, cols_at(ROWS), table_hbm, cols_at(ROWS)))
    loop(steps, blocks.start)
    for k, ref in enumerate((pack, pack_one, pack_two, pack_three)):
        packs[span(jnp.bitwise_xor(place[0] + 2 * place[1], k) * 64, 64), :] = ref[...]
    weight = packs[:, 0:width]

    def step(i, most):
        blocks.wait(i)
        here = span(i * ROWS, ROWS)
        z = dot_nn(weight, feat_t[:, here])
        table[0:units, here] = z.astype(BF16)
        table[units:, here] = jnp.concatenate([feat_t[:, here], extra], axis=0)
        stores.start(i)
        return jnp.maximum(most, lane_most(z))

    most = lax.fori_loop(0, steps, step, jnp.zeros((packs.shape[0], 128), F32))
    most_out[...] = most
    stores.wait_all(steps)


def lane_most(value):
    most = jnp.abs(value[:, 0:128])
    for first in range(128, value.shape[1], 128):
        most = jnp.maximum(most, jnp.abs(value[:, first : first + 128]))
    return most


def gelu_both(u):
    square = u * u
    t = jnp.tanh(0.79788456 * (u + 0.044715 * u * square))
    half = 0.5 * (1.0 + t)
    slope = half + 0.5 * u * (1.0 - t * t) * (0.79788456 * (1.0 + 3.0 * 0.044715 * square))
    return u * half, slope


def layer_one_kernel(place, src_t, norm_t, rows, send, most, packs_hbm, table_hbm, z_send, later, flags_t, high_hbm, rest_hbm, hidden_hbm, slope_hbm, z_hbm, near_hbm, packs, table, table8, high, rest, hidden_t, slope_t, z_own, near_feat, in_sems, edge_sems, out_sems):
    slots = src_t.shape[0]
    units, half = hidden_t.shape
    nodes = 2 * half
    halo = send.shape[0]
    blocks = high.shape[1] // 256
    per_group = 256 // slots
    steps = half // FINE
    fetch = Stream(in_sems, (packs_hbm, all_of, packs, all_of), (table_hbm, all_of, table, lambda i: (slice(None), slice(0, nodes))))
    fetch.start(0)
    depth = high.shape[0] // FINE
    around = lambda i, count: i if depth >= steps else lax.rem(i, count)
    slot_of = lambda i: span(around(i, depth) * FINE, FINE)
    slot_at = lambda i: (slot_of(i), slice(None))
    edge_stores = Stream(edge_sems, (high, slot_at, high_hbm, rows_at(FINE)), (rest, slot_at, rest_hbm, rows_at(FINE)))
    stores = Stream(
        out_sems,
        *[
            (a, cols_at(FINE), b, cols_at(FINE))
            for a, b in ((hidden_t, hidden_hbm), (slope_t, slope_hbm), (z_own, z_hbm), (near_feat, near_hbm))
        ],
    )
    in_slot = lax.broadcasted_iota(I32, (8, 128), 1) // per_group == lax.broadcasted_iota(I32, (8, 128), 0)
    node_row = lax.broadcasted_iota(I32, (per_group, 256), 0)
    mine = lax.rem(lax.broadcasted_iota(I32, (per_group, 256), 1), per_group) == node_row
    inner = lax.broadcasted_iota(I32, (256, 256), 0)

    def lean(tile):
        return [
            pltpu.roll(tile[first : first + 8, :], 0, 1, stride=per_group, stride_axis=0)
            for first in range(0, slots, 8)
        ]

    def flat(tiles, group):
        moved = [pltpu.roll(tile, (128 - per_group * group) % 128, 1) for tile in tiles]
        return jnp.concatenate(
            [jnp.sum(jnp.where(in_slot, tile, 0), axis=0, keepdims=True) for tile in moved], axis=1
        )

    def one(at, weight):
        weight_high = weight.astype(BF16).astype(F32)
        hit = inner == jnp.bitwise_and(at, 255)
        right = jnp.where(hit, weight_high, 0.0).astype(BF16)
        right_rest = jnp.where(hit, (weight - weight_high) * REST_GAIN, 0.0).astype(BF16)
        block = jnp.where(mine, jnp.right_shift(at, 8), -1)
        left = jnp.concatenate(
            [jnp.where(block == j, 1.0, 0.0).astype(BF16) for j in range(blocks)], axis=0
        )
        return dot_nt(left, right), dot_nt(left, right_rest)

    def build(i):
        here = span(place[0] * half + i * 128, 128)
        at, weight = src_t[:, here], norm_t[:, here]
        slot = lax.broadcasted_iota(I32, at.shape, 0)
        merged, repeat = weight, slot < 0
        for shift in range(1, slots):
            same = at == pltpu.roll(at, shift, 0)
            merged = merged + jnp.where(same, pltpu.roll(weight, shift, 0), 0.0)
            repeat = repeat | (same & (slot >= shift))
        source, weights = lean(at), lean(jnp.where(repeat, 0.0, merged))
        pairs = [one(flat(source, group), flat(weights, group)) for group in range(128 // per_group)]
        rows = span(around(i, high.shape[0] // 128) * 128, 128)
        for j in range(blocks):
            cols = slice(256 * j, 256 * (j + 1))
            for ref, parts in zip((high, rest), zip(*pairs)):
                piece = jnp.concatenate([p[per_group * j : per_group * (j + 1), :] for p in parts], axis=0)
                ref[rows, cols] = piece.astype(ref.dtype)

    def build_block(i):
        for k in range(FINE // 128):
            build(i * (FINE // 128) + k)
        edge_stores.start(i)

    flat_rows = rows[...].reshape(halo, 128)
    turned = flat_rows.astype(F32).T
    flags = turned[FLAG_LANE : FLAG_LANE + 8, :]
    counts = jnp.sum(rows[...].astype(F32)[:, 0, :], axis=0, keepdims=True)
    count = 64.0 * counts[:, FLAG_LANE + 3 : FLAG_LANE + 4] + counts[:, FLAG_LANE + 4 : FLAG_LANE + 5]
    row = lax.broadcasted_iota(I32, flags.shape, 0)
    flags_t[...] = jnp.where(row == 3, count, flags)
    loop(FINE // 128, build)
    edge_stores.start(0)
    fetch.wait(0)
    border = dot_nt(packs[:, 0:FLAG_LANE], flat_rows[:, 0:FLAG_LANE]).astype(BF16).astype(F32)
    border = jnp.where(flags[0:1, :] == 1.0, border, stale_columns(packs, 0, halo))
    table[0:units, nodes : nodes + halo] = border.astype(BF16)
    extra = table.shape[0] - units
    kept = lax.broadcasted_iota(I32, (extra, halo), 0) < FLAG_LANE
    kept = kept & (flags[0:1, :] == 1.0)
    table[units:, nodes : nodes + halo] = jnp.where(kept, turned[0:extra, :], 0.0).astype(BF16)
    scale, back = scale_of(jnp.maximum(jnp.max(most[...]), jnp.max(jnp.abs(border))))
    row = lax.broadcasted_iota(I32, (table.shape[0], 1), 0)
    scale = jnp.where(row < units, scale, FEAT_SCALE)
    back = jnp.where(row < units, back, 1.0 / FEAT_SCALE) * (1.0 / REST_GAIN)
    bias = bias_column(packs, 0)
    unused = jnp.zeros((table8.shape[0] - table.shape[0], 256), F32)

    def small(i):
        here = span(i * 256, 256)
        value = table[:, here].astype(F32) * scale
        table8[:, here] = jnp.concatenate([value, unused], axis=0).astype(F8)

    loop((nodes + halo) // 256, small)

    def sums(i):
        here = slot_of(i)
        low = dot_nt(table8[...], rest[here, :])[0 : table.shape[0]]
        return dot_nt(table[...], high[here, :]) + low * back

    def keep(i, total):
        here = span(i * FINE, FINE)
        slope_t[:, here] = total[0:units]
        value = total[units:]
        top = value.astype(BF16)
        near_feat[0:extra, here] = top
        near_feat[extra:, here] = (value - top.astype(F32)).astype(BF16)

    def finish(i):
        here = span(i * FINE, FINE)
        value, slope = gelu_both(slope_t[:, here] + bias)
        value = value.astype(BF16)
        hidden_t[:, here] = value
        slope_t[:, here] = slope
        z = dot_nn(packs[:, 128 : 128 + units], value).astype(BF16)
        z_own[:, here] = z
        stores.start(i)

    def step(i, carry):
        if depth < steps:

            @pl.when(i + 1 >= depth)
            def _():
                edge_stores.wait(i + 1 - depth)

        total = sums(i)
        finish(i - 1)
        build_block(i + 1)
        keep(i, total)
        return carry

    keep(0, sums(0))
    build_block(1)
    lax.fori_loop(1, steps - 1, step, 0)
    keep(steps - 1, sums(steps - 1))
    finish(steps - 2)
    finish(steps - 1)

    bound = z_send.shape[1]
    group = 256 // bound

    def send_some(c):
        chosen = pick_rows(send[span(c * 256, 256), :], place[0] * half, half)
        to = pl.ds(c * group, group)

        def put(ref, first, rows):
            value = dot_nt(chosen, rows).astype(BF16)
            ref[to, :, first : first + value.shape[1]] = value.reshape(group, bound, value.shape[1])

        slope = slope_t[...]
        top = slope.astype(BF16)
        put(z_send, 0, z_own[...])
        put(z_send, units, hidden_t[...])
        put(z_send, 2 * units, top)
        put(later, 0, (slope - top.astype(F32)).astype(BF16))
        later[to, :, units:] = jnp.zeros((group, bound, 256), BF16)
        put(later, units, near_feat[0:extra, :])
        put(later, units + 128, near_feat[extra:, :])

    loop(halo // 256, send_some)
    stores.wait_all(steps)
    for i in range(steps - depth, steps):
        edge_stores.wait(i)


def own_part_kernel(place, high, rest, z_own, z_oth, total, table, table8, back, hbuf, rbuf, sems):
    half = z_own.shape[1]
    nodes = 2 * half
    ring = Ring((high, rest), (hbuf, rbuf), sems, lambda i: (span(i * FINE, FINE), slice(0, nodes)))
    ring.begin()

    @pl.when(pl.program_id(0) == 0)
    def _():
        def larger(i, most):
            here = span(i * ROWS, ROWS)
            both = jnp.maximum(jnp.abs(z_own[:, here].astype(F32)), jnp.abs(z_oth[:, here].astype(F32)))
            return jnp.maximum(most, both)

        most = lax.fori_loop(0, half // ROWS, larger, jnp.zeros((z_own.shape[0], ROWS), F32))
        scale, inverse = scale_of(most)
        back[0] = inverse * (1.0 / REST_GAIN)
        for ref, first in ((z_own, place[0] * half), (z_oth, (1 - place[0]) * half)):

            def put(i, carry):
                value = ref[:, span(i * ROWS, ROWS)]
                cols = span(first + i * ROWS, ROWS)
                table[:, cols] = value
                table8[:, cols] = (value.astype(F32) * scale).astype(F8)
                return carry

            lax.fori_loop(0, half // ROWS, put, 0)

    top, low = ring.wait()
    total[...] = dot_nt(table[...], top[...]) + dot_nt(table8[...], low[...]) * back[0]
    ring.end()


def padded_rows(ref, count):
    value = ref[...]
    extra = jnp.zeros((count - value.shape[0], value.shape[1]), value.dtype)
    return jnp.concatenate([value, extra], axis=0).astype(BF16)


def border_cut(nodes, halo):
    return lambda i: (span(i * ROWS, ROWS), slice(nodes, nodes + halo))


def layer_two_end_kernel(place, flags_t, packs, send, high, rest, total, came, came_oth, later, last_t, hidden_t, slope_t, z_own, z_send, border, border8, back):
    halo = send.shape[0]
    width = hidden_t.shape[0]
    kinds = z_own.shape[0]
    step = pl.program_id(0)
    half = ROWS * pl.num_programs(0)

    @pl.when(step == 0)
    def _():
        flat = lambda ref: ref[:, :, 0:width].reshape(halo, width).astype(F32)
        both = flat(came) + flat(came_oth)
        value = jnp.where(flags_t[1:2, :] == 1.0, both.T, stale_columns(packs, 1, halo))
        scale, inverse = scale_of(value)
        border[...] = value.astype(BF16)
        border8[...] = (value * scale).astype(F8)
        back[0] = inverse * (1.0 / REST_GAIN)
        z_send[:, :, 0:128] = jnp.zeros((*z_send.shape[0:2], 128), BF16)
        z_send[:, :, 128:] = later[...]

    sums = total[...] + dot_nt(border[...], high[...]) + dot_nt(border8[...], rest[...]) * back[0]
    value, slope = gelu_both(sums + bias_column(packs, 1))
    value = value.astype(BF16)
    hidden_t[...] = value
    slope_t[...] = slope
    z = dot_nn(padded_rows(last_t, kinds), value).astype(BF16)
    z_own[...] = z
    chosen = dot_nt(pick_rows(send[...], place[0] * half + step * ROWS, ROWS), z)
    chosen = jnp.concatenate([chosen, jnp.zeros((halo, 128 - kinds), F32)], axis=1)
    sent = z_send[:, :, 0:128]
    z_send[:, :, 0:128] = (sent.astype(F32) + chosen.reshape(sent.shape)).astype(BF16)


def put_border(border_grad, total, keep):
    value = (total * keep).T
    bound = value.shape[0] // border_grad.shape[0]
    border_grad[:, 0:bound, :] = value.reshape(border_grad.shape[0], bound, value.shape[1])


def loss_kernel(classes, place, flags_t, came, came_oth, stale_t, bias, labels, mask, total_hbm, high, rest, sums, back_out, border_grad, grads_hbm, grads8_hbm, far_hbm, border_sum, hrows, rrows, total, grads, grads8, far, hbuf, rbuf, in_sems, edge_sems, out_sems, far_sems):
    kinds, half = total.shape
    halo = stale_t.shape[1]
    steps = half // ROWS
    cut = border_cut(2 * half, halo)
    blocks = Stream(
        in_sems,
        (high, cut, hrows, rows_at(ROWS)),
        (rest, cut, rrows, rows_at(ROWS)),
        (total_hbm, cols_at(ROWS), total, cols_at(ROWS)),
    )
    others = rows_at(ROWS, span((1 - place[0]) * half, half))
    edges = Stream(edge_sems, (high, others, hbuf, rows_at(ROWS)), (rest, others, rbuf, rows_at(ROWS)))
    stores = Stream(
        out_sems, *[(a, cols_at(ROWS), b, cols_at(ROWS)) for a, b in ((grads, grads_hbm), (grads8, grads8_hbm))]
    )
    far_stores = Stream(far_sems, (far, all_of, far_hbm, all_of))
    blocks.start_first(steps)
    edges.start(0)
    flat = lambda ref: ref[:, :, 0:128].reshape(halo, 128).astype(F32)
    both = flat(came) + flat(came_oth)
    old = jnp.concatenate([stale_t[...].astype(F32), jnp.zeros((kinds - classes, halo), F32)], axis=0)
    value = jnp.where(flags_t[2:3, :] == 1.0, both.T[0:kinds, :], old)
    scale, back = scale_of(value)
    back = back * (1.0 / REST_GAIN)
    border = value.astype(BF16)
    border8 = (value * scale).astype(F8)
    row = jnp.concatenate([bias[...], jnp.zeros((1, 128 - classes), F32)], axis=1)
    bias_col = jnp.broadcast_to(row, (8, 128)).T[0:kinds, 0:1]
    sums[...] = jnp.zeros(sums.shape, F32)
    border_sum[...] = jnp.zeros(border_sum.shape, F32)
    count = flags_t[3:4, 0:1]
    inverse = (1.0 / (256.0 * REST_GAIN)) / count
    back_out[...] = jnp.broadcast_to(inverse, back_out.shape)

    def far_step(i):
        edges.wait(i)
        here = span(i * ROWS, ROWS)
        both = dot_nn(grads[:, here], hbuf[here, :])
        low = dot_nn(grads8[:, here], rbuf[here, :]) * inverse
        far[...] += both[0:kinds] + both[kinds : 2 * kinds] + low

    def step(i):
        here = span(i * ROWS, ROWS)
        logits = total[:, here] + dot_nt(border, hrows[here, :]) + dot_nt(border8, rrows[here, :]) * back
        logits = logits + bias_col
        kind = lax.broadcasted_iota(I32, logits.shape, 0)
        real = kind < classes
        logits = jnp.where(real, logits, -jnp.inf)
        shifted = logits - jnp.max(logits, axis=0, keepdims=True)
        powers = jnp.exp(shifted)
        norm = jnp.sum(powers, axis=0, keepdims=True)
        logp = jnp.where(real, shifted - jnp.log(norm), 0.0)
        first = (place[0] * steps + i) * (ROWS // 128)
        row_of = lambda ref: jnp.concatenate([ref[pl.ds(first + k, 1), :] for k in range(ROWS // 128)], axis=1)
        target = jnp.where(kind == row_of(labels), 0.9, 0.0) + 0.1 / classes
        used = row_of(mask).astype(F32)
        loss = jnp.sum(target * logp, axis=0, keepdims=True) * used
        grad = jnp.where(real, (powers / norm - target) * (used / count), 0.0)
        sums[0:kinds, :] += lane_sums(grad)
        sums[kinds : kinds + 1, :] -= lane_sums(loss)
        top = grad.astype(BF16)
        tail = (grad - top.astype(F32)).astype(BF16)
        stacked = jnp.concatenate([top, tail], axis=0)
        small = (top.astype(F32) * (256.0 * count)).astype(F8)
        grads[:, here] = stacked
        grads8[:, here] = small
        stores.start(i)
        both = dot_nn(stacked, hrows[here, :])
        low = dot_nn(small, rrows[here, :]) * inverse
        border_sum[0:kinds, :] += both[0:kinds] + both[kinds : 2 * kinds] + low

    far[...] = jnp.zeros(far.shape, F32)
    blocks.next(0, steps)
    edges.start(1)
    step(0)

    def both_steps(i):
        blocks.next(i, steps)

        @pl.when(i + 1 < steps)
        def _():
            edges.start(i + 1)

        far_step(i - 1)
        step(i)

    lax.fori_loop(1, steps, lambda i, c: (both_steps(i), c)[1], 0)
    far_step(steps - 1)
    far_stores.start(0)
    put_border(border_grad, border_sum[...], flags_t[2:3, :])
    stores.wait_all(steps)
    far_stores.wait(0)


def lane_sums(value):
    total = value[:, 0:128]
    for first in range(128, value.shape[1], 128):
        total = total + value[:, first : first + 128]
    return total


def back_three_kernel(place, high, rest, grads, grads8, back, out, hbuf, rbuf, sems):
    kinds, size = out.shape
    base = place[0] * size * pl.num_programs(0)
    ring = Ring((high, rest), (hbuf, rbuf), sems, lambda i: (slice(None), span(base + i * size, size)))
    ring.begin()
    top, low = ring.wait()
    both = dot_nn(grads[...], top[...])
    out[...] = both[0:kinds] + both[kinds : 2 * kinds] + dot_nn(grads8[...], low[...]) * back[0:1, 0:1]
    ring.end()


def back_block(grads, grads8, tails8, back_rest, back_tail, top, low):
    total = dot_nn(grads, top) + dot_nn(grads8, low) * back_rest
    return total + dot_nn(tails8, top.astype(F8)) * back_tail


def back_kernel(place, back, grads, grads8, tails8, high, rest, out, hbuf, rbuf, edge_sems):
    half = out.shape[1]
    steps = half // ROWS
    mine = cols_at(ROWS, place[0] * half)
    edges = Stream(edge_sems, (high, mine, hbuf, cols_at(ROWS)), (rest, mine, rbuf, cols_at(ROWS)))
    edges.start_first(steps)

    def step(i):
        edges.next(i, steps)
        here = span(i * ROWS, ROWS)
        out[:, here] = back_block(
            grads[...], grads8[...], tails8[...], back[0:1, 0:1], back[0:1, 1:2], hbuf[:, here], rbuf[:, here]
        )

    loop(steps, step)


def returned_terms(ret, ret_oth, bound, kinds):
    value = ret[:, 0:bound, :] + ret_oth[:, 0:bound, :]
    value = value.reshape(value.shape[0] * bound, value.shape[2]).T[0:kinds, :]
    top = value.astype(BF16)
    return top, (value - top.astype(F32)).astype(BF16)


def round_gradient(own, came_part, terms, send, first_node):
    chosen = pick_rows(send, first_node, own.shape[1])
    total = own + came_part
    for term in terms:
        total = total + dot_nn(term, chosen)
    return total.astype(BF16)


def end_three_kernel(place, flags_t, ret, ret_oth, last_t, send, far_in_any, near_hbm, hidden_hbm, slope_hbm, high, rest, sums, back_out, border_sum, grad_last, grads, grads8, tails8, far, near, far_in, hidden_t, slope_t, hrows, rrows, grad_rows, hbuf, rbuf, in_sems, row_sems, edge_sems):
    kinds, half = near.shape
    units = slope_t.shape[0]
    parts = ret.shape[0]
    bound = send.shape[0] // parts
    halo = send.shape[0]
    steps = half // ROWS
    cut = border_cut(2 * half, halo)
    blocks = Stream(
        in_sems,
        *[
            (a, cols_at(ROWS), b, cols_at(ROWS))
            for a, b in ((near_hbm, near), (far_in_any, far_in), (hidden_hbm, hidden_t), (slope_hbm, slope_t))
        ],
    )
    borders = Stream(row_sems, (high, cut, hrows, rows_at(ROWS)), (rest, cut, rrows, rows_at(ROWS)))
    others = cols_at(ROWS, (1 - place[0]) * half)
    edges = Stream(edge_sems, (high, others, hbuf, cols_at(ROWS)), (rest, others, rbuf, cols_at(ROWS)))
    for stream in (blocks, borders, edges):
        loop(steps, stream.start)
    terms = returned_terms(ret, ret_oth, bound, kinds)
    weight = padded_rows(last_t, kinds)
    sums[...] = jnp.zeros(sums.shape, F32)
    grad_last[...] = jnp.zeros(grad_last.shape, F32)
    border_sum[...] = jnp.zeros(border_sum.shape, F32)

    def first_step(i, most):
        blocks.wait(i)
        here = span(i * ROWS, ROWS)
        d_z = round_gradient(near[:, here], far_in[:, here], terms, send[...], (place[0] * steps + i) * ROWS)
        grad_last[0:kinds, :] += dot_nt(d_z, hidden_t[:, here])
        grad = dot_tn(weight, d_z) * slope_t[:, here]
        sums[...] += lane_sums(grad)
        grad_rows[:, here] = grad
        return jnp.maximum(most, jnp.max(jnp.abs(grad), axis=0, keepdims=True))

    most = lax.fori_loop(0, steps, first_step, jnp.zeros((1, ROWS), F32))
    scale, back = scale_of(most)
    back_rest, back_tail = back * (1.0 / REST_GAIN), back * (1.0 / TAIL_GAIN)
    lane = lax.broadcasted_iota(I32, back_out.shape, 1)
    back_out[...] = jnp.where(lane == 0, back_rest, back_tail)

    def second_step(i):
        borders.wait(i)
        here = span(i * ROWS, ROWS)
        grad = grad_rows[:, here]
        top = grad.astype(BF16)
        wide = top.astype(F32)
        small = (wide * scale).astype(F8)
        tail = ((grad - wide) * (scale * TAIL_GAIN)).astype(F8)
        grads[:, here] = top
        grads8[:, here] = small
        tails8[:, here] = tail
        border_sum[...] += back_block(top, small, tail, back_rest, back_tail, hrows[here, :], rrows[here, :])

    loop(steps, second_step)
    border_sum[...] = border_sum[...] * flags_t[1:2, :]

    def far_step(i):
        edges.wait(i)
        here = span(i * ROWS, ROWS)
        far[:, here] = back_block(
            grads[...], grads8[...], tails8[...], back_rest, back_tail, hbuf[:, here], rbuf[:, here]
        )

    loop(steps, far_step)


def end_two_kernel(place, border, border_oth, packs, sums_two, sums_out, near, far, came_hbm, late_hbm, hidden_hbm, slope_hbm, feat_hbm, out, out_one, came, came_late, hidden_t, slope_t, near_feat, grad_first, grad_second, sums_one, came_sems, in_sems):
    units, half = near.shape
    halo = border.shape[1]
    steps = half // ROWS
    extra = near_feat.shape[0] // 2
    every = lambda i: (slice(None), slice(None), slice(None))
    fetch = Stream(came_sems, (came_hbm, every, came, every), (late_hbm, every, came_late, every))
    blocks = Stream(
        in_sems,
        *[
            (a, cols_at(ROWS), b, cols_at(ROWS))
            for a, b in ((hidden_hbm, hidden_t), (slope_hbm, slope_t), (feat_hbm, near_feat))
        ],
    )
    loop(steps, blocks.start)
    fetch.start(0)
    weight = packs[:, 128 : 128 + units]
    for ref in (grad_first, grad_second, sums_one):
        ref[...] = jnp.zeros(ref.shape, F32)

    def through(d_z, slope):
        grad = dot_tn(weight, d_z) * slope
        sums_one[...] += lane_sums(grad)
        top = grad.astype(BF16)
        return top, (grad - top.astype(F32)).astype(BF16)

    def step(i):
        blocks.wait(i)
        here = span(i * ROWS, ROWS)
        d_z = (near[:, here] + far[:, here]).astype(BF16)
        grad_second[...] += dot_nt(d_z, hidden_t[:, here])
        top, tail = through(d_z, slope_t[:, here])
        high, low = near_feat[0:extra, here], near_feat[extra:, here]
        grad_first[:, 0:extra] += dot_nt(top, high) + (dot_nt(tail, high) + dot_nt(top, low))

    loop(steps, step)
    fetch.wait(0)
    lanes = lambda ref, first, size: ref[:, :, first : first + size].reshape(halo, size)
    d_z = (border[...] + border_oth[...]).astype(BF16)
    grad_second[...] += dot_nn(d_z, lanes(came, units, units))
    slope = lanes(came, 2 * units, units).astype(F32) + lanes(came_late, 128, units).astype(F32)
    top, tail = through(d_z, slope.T)
    high, low = lanes(came_late, 128 + units, 128), lanes(came_late, 256 + units, 128)
    grad_first[...] += dot_nn(top, high) + (dot_nn(tail, high) + dot_nn(top, low))
    lane = lax.broadcasted_iota(I32, (64, 128), 1)
    column = lambda value: jnp.sum(value, axis=1, keepdims=True)
    for k, ref in enumerate((out, out_one)):
        rows = span(jnp.bitwise_xor(place[0] + 2 * place[1], k) * 64, 64)
        value = jnp.where(lane < FLAG_LANE, grad_first[rows, :], 0.0)
        value = jnp.where(lane == FLAG_LANE, column(sums_one[rows, :]), value)
        value = jnp.where(lane == FLAG_LANE + 1, column(sums_two[rows, :]), value)
        ref[0:64, :] = jnp.where(lane == FLAG_LANE + 2, column(sums_out[...]), value)
        ref[64:128, :] = grad_second[rows, 0:128]
        ref[128:192, :] = grad_second[rows, 128:256]


def scatter_kernel(mine, came, last, last_came, out):
    total = mine[...] + came[...]
    last_total = last[...] + last_came[...]
    parts = out.shape[0]
    size = 64 // parts
    for q in range(parts):
        pieces = [total[64 * k + q * size : 64 * k + (q + 1) * size, :] for k in range(3)]
        chunk = last_total[q * size : (q + 1) * size, :]
        out[q] = jnp.concatenate(pieces + [chunk[:, 0:128], chunk[:, 128:256]], axis=0)


def joined(came, first, size):
    return came[:, first : first + size, :].reshape(64, 128)


def gather_kernel(came, out):
    value = jnp.sum(came[...], axis=0)
    for p in range(came.shape[0]):
        out[p] = value


def adamw(weight, moment, square, gradient):
    moment = beta_one * moment + (1.0 - beta_one) * gradient
    square = beta_two * square + (1.0 - beta_two) * gradient * gradient
    moment_hat = moment / (1.0 - beta_one**STEP)
    square_hat = square / (1.0 - beta_two**STEP)
    weight = weight - rate_step * (
        moment_hat / (jnp.sqrt(square_hat) + epsilon) + decay_rate * weight
    )
    return (weight, moment, square)


def update_kernel(came, flags_t, *refs):
    params, outs = refs[0:15], refs[15:]
    parts = came.shape[0]
    size = 64 // parts
    width, kinds = params[0].shape[1], params[6].shape[0]
    total = joined(came, 0, size)
    halves = [joined(came, size, size), joined(came, 2 * size, size)]
    turned = jnp.concatenate([total, jnp.zeros((64, 128), F32)], axis=0).T
    gradients = (
        total[:, 0:width],
        jnp.concatenate(halves, axis=1),
        jnp.concatenate([joined(came, 3 * size, size), joined(came, 4 * size, size)], axis=1)[0:kinds, :],
        turned[FLAG_LANE : FLAG_LANE + 2, 0:64],
        turned[FLAG_LANE + 2 : FLAG_LANE + 3, 0:kinds],
    )
    for k, gradient in enumerate(gradients):
        values = adamw(*[ref[...] for ref in params[3 * k : 3 * k + 3]], gradient)
        for ref, value in zip(outs[3 * k : 3 * k + 3], values):
            ref[...] = value
    padded = turned[FLAG_LANE + 2 : FLAG_LANE + 3, 48:49]
    outs[15][...] = jnp.broadcast_to(padded, (1, 128))
    outs[16][...] = jnp.broadcast_to(flags_t[3:4, 0:1], (1, 128))


def body(
    parts,
    reps,
    features,
    labels,
    train_mask,
    edge_src,
    edge_norm,
    send_rows,
    changed,
    cache_hidden,
    cache_out,
    first_weight,
    second_weight,
    last_weight,
    hidden_bias,
    out_bias,
    moment_first,
    moment_second,
    moment_last,
    moment_hidden,
    moment_out,
    square_first,
    square_second,
    square_last,
    square_hidden,
    square_out,
):
    nodes, in_width = features.shape
    half = nodes // 2
    bound = send_rows.shape[2]
    halo = parts * bound
    table = nodes + halo
    units, classes = last_weight.shape
    kinds = -(-classes // 16) * 16
    steps, fine = half // ROWS, half // FINE

    rep = lax.axis_index("rep")
    place = jnp.stack([lax.rem(rep, 2), lax.div(rep, 2)]).astype(I32)
    where = (place, SMEM)
    feat_t = features.T
    last_t = last_weight.T
    label_rows = labels.reshape(nodes // 128, 128)
    mask_rows = train_mask.reshape(nodes // 128, 128)

    def swap(x, k=1):
        return lax.ppermute(x, "rep", [(i, i ^ k) for i in range(reps)])

    def exchange(x):
        return lax.all_to_all(x, "dom", split_axis=0, concat_axis=0, tiled=True)

    def late(after, *arrays):
        return lax.optimization_barrier((*arrays, after))

    vm = pltpu.VMEM
    whole = lambda a: (a, whole_spec(a.shape))
    work = 2 * half * table * units
    pack_width = 256 + units + 2 * halo
    extra = -(-in_width // 16) * 16
    both = units + extra
    rows_out, pack, send = run(
        pack_kernel,
        "pack",
        [
            whole(feat_t),
            whole(send_rows.reshape(parts, bound)),
            whole(changed.T),
            *[whole(a) for a in (mask_rows, first_weight.T, second_weight.T)],
            *[whole(a) for a in (jnp.transpose(cache_hidden, (0, 2, 1)), hidden_bias)],
        ],
        [
            ((parts, bound, 128), BF16, VMEM),
            ((units // reps, pack_width), BF16, VMEM),
            ((halo, 1), I32, VMEM),
        ],
        flops=2 * halo * nodes * 128,
        grid=(1,),
    )
    packs = [pack if k == 0 else swap(pack, k) for k in range(reps)]
    rows = exchange(rows_out)
    node_block = lambda size, rows: pl.BlockSpec((rows, size), lambda i: (0, i))
    block, fine_block = node_block(ROWS, units), node_block(FINE, units)
    scalar = pltpu.SMEM((1,), F32)
    packs, most, first_table = run(
        table_kernel,
        "table",
        [where, *placed(VMEM, *packs), (feat_t, HBM)],
        [((units, pack_width), BF16, OWN), ((units, 128), F32, VMEM), ((units + extra, nodes), BF16, HBM)],
        [
            vm((in_width, nodes), BF16),
            vm((units + extra, nodes), BF16),
            sems(1, nodes // ROWS),
            sems(1, nodes // ROWS),
        ],
        flops=2 * units * nodes * in_width,
    )
    rows, most = late(most, rows)
    held = fine if half * table * 3 <= RESIDENT_BYTES else min(fine, 4)
    z_send, later, flags_t, high, rest, hidden_one, slope_one, z_own, near_feat = run(
        layer_one_kernel,
        "layer_one",
        [where, *placed(OWN, edge_src.T, edge_norm.T), *placed(VMEM, rows, send, most), *placed(HBM, packs, first_table)],
        [
            ((parts, bound, 3 * units), BF16, VMEM),
            ((parts, bound, units + 256), BF16, OWN),
            ((8, halo), F32, OWN),
            ((half, table), BF16, HBM),
            ((half, table), F8, HBM),
            ((units, half), BF16, HBM),
            ((units, half), F32, HBM),
            ((units, half), BF16, HBM),
            ((2 * extra, half), BF16, HBM),
        ],
        [
            vm((units, pack_width), BF16),
            vm((both, table), BF16),
            vm((-(-both // 32) * 32, table), F8),
            vm((held * FINE, table), BF16),
            vm((held * FINE, table), F8),
            vm((units, half), BF16),
            vm((units, half), F32),
            vm((units, half), BF16),
            vm((2 * extra, half), BF16),
            sems(2, 1),
            sems(2, fine),
            sems(4, fine),
        ],
        flops=2 * work,
    )
    edge = placed(HBM, high, rest)

    def own_part(z_own, z_oth, name):
        n = z_own.shape[0]
        return run(
            own_part_kernel,
            name,
            [where, *edge, whole(z_own), (z_oth, VMEM)],
            [((n, half), F32, node_block(FINE, n))],
            [vm((n, nodes), BF16), vm((n, nodes), F8), scalar, *ring_scratch((FINE, nodes))],
            flops=work,
            grid=(fine,),
        )[0]

    z_oth = swap(z_own)
    came = exchange(z_send)
    total = own_part(z_own, z_oth, "layer_two_own")
    came, total = late(total, came)
    came_one = came
    came_oth = swap(came)
    border_block = lambda array: (array, pl.BlockSpec((ROWS, halo), lambda i: (i, nodes // halo)))
    hidden_two, slope_two, z_own, z_send = run(
        layer_two_end_kernel,
        "layer_two_end",
        [where, whole(flags_t), whole(packs), (send, VMEM), border_block(high), border_block(rest), (total, block)]
        + placed(VMEM, came, came_oth)
        + [whole(later), whole(last_t)],
        [
            ((units, half), BF16, block),
            ((units, half), F32, block),
            ((kinds, half), BF16, node_block(ROWS, kinds)),
            ((parts, bound, 128 + units + 256), BF16, whole_spec((parts, bound, 128 + units + 256))),
        ],
        [vm((units, halo), BF16), vm((units, halo), F8), scalar],
        flops=work // 4,
        grid=(steps,),
    )
    z_oth = swap(z_own)
    came = exchange(z_send)
    total = own_part(z_own, z_oth, "layer_three_own")
    came, total = late(total, came)
    came_two = came
    came_oth = swap(came)
    border_rows = [vm((half, halo), BF16), vm((half, halo), F8)]
    sums_out, back, border_grad, grads, grads8, far = run(
        functools.partial(loss_kernel, classes),
        "loss",
        [
            where,
            *placed(VMEM, flags_t, came, came_oth, cache_out.T, out_bias.reshape(1, classes), label_rows, mask_rows),
            (total, HBM),
            *edge,
        ],
        [
            ((64, 128), F32, VMEM),
            ((8, 128), F32, VMEM),
            ((parts, bound, 128), F32, VMEM),
            ((2 * kinds, half), BF16, HBM),
            ((kinds, half), F8, HBM),
            ((kinds, half), F32, HBM),
        ],
        [
            vm((128, halo), F32),
            *border_rows,
            vm((kinds, half), F32),
            vm((2 * kinds, half), BF16),
            vm((kinds, half), F8),
            vm((kinds, half), F32),
            vm((half, half), BF16),
            vm((half, half), F8),
            sems(3, steps),
            sems(2, steps),
            sems(2, steps),
            sems(1, 1),
        ],
        flops=work,
    )
    far = swap(far)
    ret = exchange(border_grad)
    near = run(
        back_three_kernel,
        "back_three",
        [where, *edge, whole(grads), whole(grads8), (back, VMEM)],
        [((kinds, half), F32, node_block(FINE, kinds))],
        ring_scratch((half, FINE)),
        flops=work // 2,
        grid=(fine,),
    )[0]
    ret, far, near = late(near, ret, far)
    ret_oth = swap(ret)
    sums_two, back, border, last, grads, grads8, tails8, far = run(
        end_three_kernel,
        "end_three",
        [where, *placed(VMEM, flags_t, ret, ret_oth, last_t, send), (far, ANY)]
        + [*placed(HBM, near, hidden_two, slope_two), *edge],
        [
            ((units, 128), F32, VMEM),
            ((8, 128), F32, VMEM),
            ((units, halo), F32, VMEM),
            ((64, units), F32, VMEM),
            ((units, half), BF16, VMEM),
            ((units, half), F8, VMEM),
            ((units, half), F8, VMEM),
            ((units, half), F32, VMEM),
        ],
        [
            vm((kinds, half), F32),
            vm((kinds, half), F32),
            vm((units, half), BF16),
            vm((units, half), F32),
            *border_rows,
            vm((units, half), F32),
            vm((half, half), BF16),
            vm((half, half), F8),
            sems(4, steps),
            sems(2, steps),
            sems(2, steps),
        ],
        flops=work,
        limit=LOW_LIMIT,
    )
    far, border_oth, last_oth = swap(far), swap(border), swap(last)
    near = run(
        back_kernel,
        "back",
        [where, *placed(VMEM, back, grads, grads8, tails8), *edge],
        [((units, half), F32, VMEM)],
        [vm((half, half), BF16), vm((half, half), F8), sems(2, steps)],
        flops=work // 2,
        limit=LOW_LIMIT,
    )[0]
    mine, theirs = run(
        end_two_kernel,
        "end_two",
        [where, *placed(VMEM, border, border_oth), (packs, OWN), *placed(VMEM, sums_two, sums_out, near, far)]
        + [*placed(HBM, came_one, came_two, hidden_one, slope_one, near_feat)],
        [((192, 128), F32, VMEM)] * 2,
        [
            vm(came_one.shape, BF16),
            vm(came_two.shape, BF16),
            vm((units, half), BF16),
            vm((units, half), F32),
            vm((2 * extra, half), BF16),
            vm((units, 128), F32),
            vm((units, units), F32),
            vm((units, 128), F32),
            sems(2, 1),
            sems(3, steps),
        ],
        flops=work // 4,
        limit=LOW_LIMIT,
    )
    scattered = run(
        scatter_kernel,
        "scatter",
        placed(VMEM, mine, swap(theirs), last, last_oth),
        [((parts, 5 * 64 // parts, 128), F32, VMEM)],
    )[0]
    gathered = run(
        gather_kernel,
        "gather",
        placed(VMEM, exchange(scattered)),
        [(scattered.shape, F32, VMEM)],
    )[0]
    came = exchange(gathered)

    turn = lambda x: x.T
    same = lambda x: x
    row = lambda x: x.reshape(1, -1)
    forms = (turn, turn, turn, same, row)
    weights = (first_weight, second_weight, last_weight, hidden_bias, out_bias)
    moments = (moment_first, moment_second, moment_last, moment_hidden, moment_out)
    squares = (square_first, square_second, square_last, square_hidden, square_out)
    params = [form(x) for form, triple in zip(forms, zip(weights, moments, squares)) for x in triple]
    outs = run(
        update_kernel,
        "update",
        placed(VMEM, came, flags_t, *params),
        [(p.shape, F32, VMEM) for p in params] + [((1, 128), F32, VMEM)] * 2,
    )
    undo = (turn, turn, turn, same, lambda x: x.reshape(-1))
    results = [undo[k // 3](x) for k, x in enumerate(outs[0:15])]
    return (outs[15][0, 0], outs[16][0, 0], *results)


def solution(mesh):
    placed = (
        P("dom", None),
        P("dom"),
        P("dom"),
        P("dom", None),
        P("dom", None),
        P("dom", None, None),
        P(None, "dom"),
        P(None, "dom", "rep"),
        P("dom", None),
        P(None, "rep"),
        P(None, "rep"),
        P(),
        P(None, "rep"),
        P(),
        P(None, "rep"),
        P(None, "rep"),
        P(),
        P(None, "rep"),
        P(),
        P(None, "rep"),
        P(None, "rep"),
        P(),
        P(None, "rep"),
        P(),
    )
    return jax.shard_map(
        functools.partial(body, mesh.shape["dom"], mesh.shape["rep"]),
        mesh=mesh,
        in_specs=placed,
        out_specs=(P(), P()) + (P(None, "rep"),) * 6 + (P(),) * 3 + (P(None, "rep"),) * 3 + (P(),) * 3,
        check_vma=False,
    )
```

```python
import functools

import jax
import jax.numpy as jnp
from jax import lax
from jax.experimental import pallas as pl
from jax.experimental.pallas import tpu as pltpu
from jax.sharding import PartitionSpec as P

STEP = 5
beta_one = 0.5
beta_two = 0.5
rate_step = 0.03
decay_rate = 0.01
epsilon = 1e-08

BF16, F32, F8, I32 = jnp.bfloat16, jnp.float32, jnp.float8_e4m3fn, jnp.int32
REST_GAIN = 4096.0
TAIL_GAIN = 256.0
FLAG_LANE = 100
ROWS = 512
FINE = 256
AHEAD = 3
LIMIT = 52 << 20
LOW_LIMIT = 34 << 20
RESIDENT_BYTES = 30 << 20
FEAT_SCALE = 32.0

SMEM = pl.BlockSpec(memory_space=pltpu.SMEM)
VMEM = pl.BlockSpec(memory_space=pltpu.VMEM)
OWN = pl.BlockSpec(memory_space=pltpu.VMEM)
HBM = pl.BlockSpec(memory_space=pltpu.HBM)
ANY = pl.BlockSpec(memory_space=pl.ANY)


def whole_spec(shape):
    return pl.BlockSpec(shape, lambda *_: (0,) * len(shape))


def placed(spec, *arrays):
    return [(a, spec) for a in arrays]


def run(kernel, name, args, outs, scratch=(), flops=0, grid=(), limit=LIMIT):
    pinned = [
        a if any(spec is s for s in (SMEM, VMEM, ANY)) else pltpu.with_memory_space_constraint(a, pltpu.HBM)
        for a, spec in args
    ]
    return pl.pallas_call(
        kernel,
        grid=grid,
        in_specs=[spec for _, spec in args],
        out_specs=[spec for _, _, spec in outs],
        out_shape=[
            jax.ShapeDtypeStruct(shape, kind) if spec is VMEM else pltpu.HBM(shape, kind)
            for shape, kind, spec in outs
        ],
        scratch_shapes=list(scratch),
        name=name,
        cost_estimate=pl.CostEstimate(flops=flops, bytes_accessed=1 << 20, transcendentals=0),
        compiler_params=pltpu.CompilerParams(vmem_limit_bytes=limit),
    )(*pinned)


def dot_nn(left, right):
    return lax.dot_general(left, right, (((1,), (0,)), ((), ())), preferred_element_type=F32)


def dot_nt(left, right):
    return lax.dot_general(left, right, (((1,), (1,)), ((), ())), preferred_element_type=F32)


def dot_tn(left, right):
    return lax.dot_general(left, right, (((0,), (0,)), ((), ())), preferred_element_type=F32)


def scale_of(value):
    most = jnp.maximum(jnp.max(jnp.abs(value)), 1e-30)
    return 256.0 / most, most * (1.0 / 256.0)


def span(start, size):
    return pl.ds(pl.multiple_of(start, size), size)


def rows_at(size, cols=slice(None)):
    return lambda i: (span(i * size, size), cols)


def cols_at(size, base=0):
    return lambda i: (slice(None), span(base + i * size, size))


def all_of(i):
    return (slice(None), slice(None))


def loop(count, step):
    def one(i, carry):
        step(i)
        return carry

    lax.fori_loop(0, count, one, 0)


class Ring:
    def __init__(self, refs, bufs, sems, cut, first=0):
        self.refs, self.bufs, self.sems, self.cut = refs, bufs, sems, cut
        self.begins = pl.program_id(0) == 0
        self.step, self.steps = pl.program_id(0) - first, pl.num_programs(0) - first
        self.depth = bufs[0].shape[0]
        self.slot = lax.rem(self.step, self.depth)

    def copies(self, step, slot):
        return [
            pltpu.make_async_copy(ref.at[self.cut(step)], buf.at[slot], self.sems.at[k, slot])
            for k, (ref, buf) in enumerate(zip(self.refs, self.bufs))
        ]

    def begin(self):
        for step in range(self.depth):

            @pl.when(self.begins & (step < self.steps))
            def _():
                for copy in self.copies(step, step):
                    copy.start()

    def wait(self):
        for copy in self.copies(self.step, self.slot):
            copy.wait()
        return [buf.at[self.slot] for buf in self.bufs]

    def end(self):
        @pl.when(self.step + self.depth < self.steps)
        def _():
            for copy in self.copies(self.step + self.depth, self.slot):
                copy.start()


def ring_scratch(shape, depth=3):
    kinds = (BF16, F8)
    return [pltpu.VMEM((depth, *shape), kind) for kind in kinds] + [pltpu.SemaphoreType.DMA((len(kinds), depth))]


class Stream:
    def __init__(self, sems, *legs):
        self.sems, self.legs = sems, legs

    def copies(self, i):
        return [
            pltpu.make_async_copy(source.at[source_at(i)], target.at[target_at(i)], self.sems.at[k, i])
            for k, (source, source_at, target, target_at) in enumerate(self.legs)
        ]

    def start(self, i):
        for copy in self.copies(i):
            copy.start()

    def wait(self, i):
        for copy in self.copies(i):
            copy.wait()

    def wait_all(self, count):
        loop(count, self.wait)

    def start_first(self, count):
        for i in range(min(AHEAD, count)):
            self.start(i)

    def next(self, i, count):
        self.wait(i)

        @pl.when(i + AHEAD < count)
        def _():
            self.start(i + AHEAD)


def sems(legs, count):
    return pltpu.SemaphoreType.DMA((legs, count))


def pick_rows(send, first, count):
    nodes = lax.broadcasted_iota(I32, (send.shape[0], count), 1) + first
    return jnp.where(send == nodes, 1.0, 0.0).astype(BF16)


def pack_kernel(feat_t, send_list, changed, mask, first_t, second_t, cache_t, bias, rows_out, pack_out, send):
    nodes, halo = feat_t.shape[1], send.shape[0]
    parts, bound = send_list.shape
    turned = send_list[...].astype(F32)
    turned = jnp.concatenate([turned, jnp.zeros((parts, 128 - bound), F32)], axis=1)
    turned = turned.T.astype(I32)
    for q in range(parts):
        send[q * bound : (q + 1) * bound, :] = turned[0:bound, q : q + 1]
    width, cols = feat_t.shape[0], first_t.shape[0]

    def pick(i, total):
        return total + dot_nt(pick_rows(send[...], i * ROWS, ROWS), feat_t[:, span(i * ROWS, ROWS)])

    total = jnp.zeros((halo, width), F32)
    for i in range(nodes // ROWS):
        total = pick(i, total)
    count = jnp.sum(mask[...].astype(F32))
    many = jnp.floor(count * (1.0 / 64.0))
    lane = lax.broadcasted_iota(I32, (halo, 128), 1)
    row = jnp.concatenate([total, jnp.zeros((halo, 128 - width), F32)], axis=1)
    for layer in range(3):
        row = jnp.where(lane == FLAG_LANE + layer, changed[0:1, layer : layer + 1].astype(F32), row)
    row = jnp.where(lane == FLAG_LANE + 3, many, row)
    row = jnp.where(lane == FLAG_LANE + 4, count - 64.0 * many, row)
    rows_out[...] = row.astype(BF16).reshape(rows_out.shape)

    units = second_t.shape[1]
    pack_out[:, 0:128] = jnp.concatenate(
        [first_t[...], jnp.zeros((cols, 128 - width), F32)], axis=1
    ).astype(BF16)
    pack_out[:, 128 : 128 + units] = second_t[...].astype(BF16)
    left = jnp.concatenate([bias[...], jnp.zeros((2, 128 - cols), F32)], axis=1)
    terms = []
    for _ in range(3):
        term = left.astype(BF16).astype(F32)
        terms.append(term)
        left = left - term
    terms = jnp.concatenate(terms + [jnp.zeros((122, 128), F32)], axis=0).T
    pack_out[:, 128 + units : 256 + units] = terms[0:cols, :].astype(BF16)
    base = 256 + units
    for layer in range(2):
        pack_out[:, base + layer * halo : base + (layer + 1) * halo] = cache_t[layer]


def bias_column(packs, layer):
    units = packs.shape[0]
    terms = packs[:, 128 + units : 256 + units].astype(F32)
    return terms[:, layer : layer + 1] + terms[:, layer + 2 : layer + 3] + terms[:, layer + 4 : layer + 5]


def stale_columns(packs, layer, halo):
    base = 256 + packs.shape[0] + layer * halo
    return packs[:, base : base + halo].astype(F32)


def table_kernel(place, pack, pack_one, pack_two, pack_three, feat_hbm, packs, most_out, table_hbm, feat_t, table, in_sems, out_sems):
    width, nodes = feat_t.shape
    units = packs.shape[0]
    steps = 4
    size = nodes // steps
    extra = jnp.zeros((table.shape[0] - units - width, size), BF16)
    blocks = Stream(in_sems, (feat_hbm, cols_at(size), feat_t, cols_at(size)))
    stores = Stream(out_sems, (table, cols_at(size), table_hbm, cols_at(size)))
    loop(steps, blocks.start)
    for k, ref in enumerate((pack, pack_one, pack_two, pack_three)):
        packs[span(jnp.bitwise_xor(place[0] + 2 * place[1], k) * 64, 64), :] = ref[...]
    weight = packs[:, 0:width]

    def step(i, most):
        blocks.wait(i)
        here = span(i * size, size)
        z = dot_nn(weight, feat_t[:, here])
        table[0:units, here] = z.astype(BF16)
        table[units:, here] = jnp.concatenate([feat_t[:, here], extra], axis=0)
        stores.start(i)
        return jnp.maximum(most, lane_most(z))

    most = lax.fori_loop(0, steps, step, jnp.zeros((packs.shape[0], 128), F32))
    most_out[...] = most
    stores.wait_all(steps)


def lane_most(value):
    most = jnp.abs(value[:, 0:128])
    for first in range(128, value.shape[1], 128):
        most = jnp.maximum(most, jnp.abs(value[:, first : first + 128]))
    return most


def gelu_both(u):
    square = u * u
    t = jnp.tanh(0.79788456 * (u + 0.044715 * u * square))
    half = 0.5 * (1.0 + t)
    slope = half + 0.5 * u * (1.0 - t * t) * (0.79788456 * (1.0 + 3.0 * 0.044715 * square))
    return u * half, slope


def layer_one_kernel(place, src_t, norm_t, rows, send, most, packs_hbm, table_hbm, z_send, later, flags_t, high_hbm, rest_hbm, hidden_hbm, slope_hbm, z_hbm, near_hbm, packs, table, table8, high, rest, hidden_t, slope_t, z_own, near_feat, in_sems, edge_sems, out_sems):
    slots = src_t.shape[0]
    units, half = hidden_t.shape
    nodes = 2 * half
    halo = send.shape[0]
    blocks = high.shape[1] // 256
    per_group = 256 // slots
    steps = half // FINE
    fetch = Stream(in_sems, (packs_hbm, all_of, packs, all_of), (table_hbm, all_of, table, lambda i: (slice(None), slice(0, nodes))))
    fetch.start(0)
    depth = high.shape[0] // FINE
    around = lambda i, count: i if depth >= steps else lax.rem(i, count)
    slot_of = lambda i: span(around(i, depth) * FINE, FINE)
    slot_at = lambda i: (slot_of(i), slice(None))
    edge_stores = Stream(edge_sems, (high, slot_at, high_hbm, rows_at(FINE)), (rest, slot_at, rest_hbm, rows_at(FINE)))
    stores = Stream(
        out_sems,
        *[
            (a, cols_at(FINE), b, cols_at(FINE))
            for a, b in ((hidden_t, hidden_hbm), (slope_t, slope_hbm), (z_own, z_hbm), (near_feat, near_hbm))
        ],
    )
    in_slot = lax.broadcasted_iota(I32, (8, 128), 1) // per_group == lax.broadcasted_iota(I32, (8, 128), 0)
    node_row = lax.broadcasted_iota(I32, (per_group, 256), 0)
    mine = lax.rem(lax.broadcasted_iota(I32, (per_group, 256), 1), per_group) == node_row
    inner = lax.broadcasted_iota(I32, (256, 256), 0)

    def lean(tile):
        return [
            pltpu.roll(tile[first : first + 8, :], 0, 1, stride=per_group, stride_axis=0)
            for first in range(0, slots, 8)
        ]

    def flat(tiles, group):
        moved = [pltpu.roll(tile, (128 - per_group * group) % 128, 1) for tile in tiles]
        return jnp.concatenate(
            [jnp.sum(jnp.where(in_slot, tile, 0), axis=0, keepdims=True) for tile in moved], axis=1
        )

    def one(at, weight):
        weight_high = weight.astype(BF16).astype(F32)
        hit = inner == jnp.bitwise_and(at, 255)
        right = jnp.where(hit, weight_high, 0.0).astype(BF16)
        right_rest = jnp.where(hit, (weight - weight_high) * REST_GAIN, 0.0).astype(BF16)
        block = jnp.where(mine, jnp.right_shift(at, 8), -1)
        left = jnp.concatenate(
            [jnp.where(block == j, 1.0, 0.0).astype(BF16) for j in range(blocks)], axis=0
        )
        return dot_nt(left, right), dot_nt(left, right_rest)

    def build(i):
        here = span(place[0] * half + i * 128, 128)
        at, weight = src_t[:, here], norm_t[:, here]
        slot = lax.broadcasted_iota(I32, at.shape, 0)
        merged, repeat = weight, slot < 0
        for shift in range(1, slots):
            same = at == pltpu.roll(at, shift, 0)
            merged = merged + jnp.where(same, pltpu.roll(weight, shift, 0), 0.0)
            repeat = repeat | (same & (slot >= shift))
        source, weights = lean(at), lean(jnp.where(repeat, 0.0, merged))
        pairs = [one(flat(source, group), flat(weights, group)) for group in range(128 // per_group)]
        rows = span(around(i, high.shape[0] // 128) * 128, 128)
        for j in range(blocks):
            cols = slice(256 * j, 256 * (j + 1))
            for ref, parts in zip((high, rest), zip(*pairs)):
                piece = jnp.concatenate([p[per_group * j : per_group * (j + 1), :] for p in parts], axis=0)
                ref[rows, cols] = piece.astype(ref.dtype)

    def build_block(i):
        for k in range(FINE // 128):
            build(i * (FINE // 128) + k)
        edge_stores.start(i)

    flat_rows = rows[...].reshape(halo, 128)
    turned = flat_rows.astype(F32).T
    flags = turned[FLAG_LANE : FLAG_LANE + 8, :]
    counts = jnp.sum(rows[...].astype(F32)[:, 0, :], axis=0, keepdims=True)
    count = 64.0 * counts[:, FLAG_LANE + 3 : FLAG_LANE + 4] + counts[:, FLAG_LANE + 4 : FLAG_LANE + 5]
    row = lax.broadcasted_iota(I32, flags.shape, 0)
    flags_t[...] = jnp.where(row == 3, count, flags)
    loop(FINE // 128, build)
    edge_stores.start(0)
    fetch.wait(0)
    border = dot_nt(packs[:, 0:FLAG_LANE], flat_rows[:, 0:FLAG_LANE]).astype(BF16).astype(F32)
    border = jnp.where(flags[0:1, :] == 1.0, border, stale_columns(packs, 0, halo))
    table[0:units, nodes : nodes + halo] = border.astype(BF16)
    extra = table.shape[0] - units
    kept = lax.broadcasted_iota(I32, (extra, halo), 0) < FLAG_LANE
    kept = kept & (flags[0:1, :] == 1.0)
    table[units:, nodes : nodes + halo] = jnp.where(kept, turned[0:extra, :], 0.0).astype(BF16)
    scale, back = scale_of(jnp.maximum(jnp.max(most[...]), jnp.max(jnp.abs(border))))
    row = lax.broadcasted_iota(I32, (table.shape[0], 1), 0)
    scale = jnp.where(row < units, scale, FEAT_SCALE)
    back = jnp.where(row < units, back, 1.0 / FEAT_SCALE) * (1.0 / REST_GAIN)
    bias = bias_column(packs, 0)
    unused = jnp.zeros((table8.shape[0] - table.shape[0], 256), F32)

    def small(i):
        here = span(i * 256, 256)
        value = table[:, here].astype(F32) * scale
        table8[:, here] = jnp.concatenate([value, unused], axis=0).astype(F8)

    loop((nodes + halo) // 256, small)

    def sums(i):
        here = slot_of(i)
        low = dot_nt(table8[...], rest[here, :])[0 : table.shape[0]]
        return dot_nt(table[...], high[here, :]) + low * back

    def keep(i, total):
        here = span(i * FINE, FINE)
        slope_t[:, here] = total[0:units]
        value = total[units:]
        top = value.astype(BF16)
        near_feat[0:extra, here] = top
        near_feat[extra:, here] = (value - top.astype(F32)).astype(BF16)

    def finish(i):
        here = span(i * FINE, FINE)
        value, slope = gelu_both(slope_t[:, here] + bias)
        value = value.astype(BF16)
        hidden_t[:, here] = value
        slope_t[:, here] = slope
        z = dot_nn(packs[:, 128 : 128 + units], value).astype(BF16)
        z_own[:, here] = z
        stores.start(i)

    def step(i, carry):
        if depth < steps:

            @pl.when(i + 1 >= depth)
            def _():
                edge_stores.wait(i + 1 - depth)

        total = sums(i)
        finish(i - 1)
        build_block(i + 1)
        keep(i, total)
        return carry

    keep(0, sums(0))
    build_block(1)
    lax.fori_loop(1, steps - 1, step, 0)
    keep(steps - 1, sums(steps - 1))
    finish(steps - 2)
    finish(steps - 1)

    bound = z_send.shape[1]
    group = 256 // bound

    def send_some(c):
        chosen = pick_rows(send[span(c * 256, 256), :], place[0] * half, half)
        to = pl.ds(c * group, group)

        def put(ref, first, rows):
            value = dot_nt(chosen, rows).astype(BF16)
            ref[to, :, first : first + value.shape[1]] = value.reshape(group, bound, value.shape[1])

        slope = slope_t[...]
        top = slope.astype(BF16)
        put(z_send, 0, z_own[...])
        put(z_send, units, hidden_t[...])
        put(z_send, 2 * units, top)
        put(later, 0, (slope - top.astype(F32)).astype(BF16))
        later[to, :, units:] = jnp.zeros((group, bound, 256), BF16)
        put(later, units, near_feat[0:extra, :])
        put(later, units + 128, near_feat[extra:, :])

    loop(halo // 256, send_some)
    stores.wait_all(steps)
    for i in range(steps - depth, steps):
        edge_stores.wait(i)


def own_part_kernel(place, high, rest, z_own, z_oth, total, table, table8, back, hbuf, rbuf, sems):
    half = z_own.shape[1]
    nodes = 2 * half
    ring = Ring((high, rest), (hbuf, rbuf), sems, lambda i: (span(i * FINE, FINE), slice(0, nodes)))
    ring.begin()

    @pl.when(pl.program_id(0) == 0)
    def _():
        def larger(i, most):
            here = span(i * ROWS, ROWS)
            both = jnp.maximum(jnp.abs(z_own[:, here].astype(F32)), jnp.abs(z_oth[:, here].astype(F32)))
            return jnp.maximum(most, both)

        most = lax.fori_loop(0, half // ROWS, larger, jnp.zeros((z_own.shape[0], ROWS), F32))
        scale, inverse = scale_of(most)
        back[0] = inverse * (1.0 / REST_GAIN)
        for ref, first in ((z_own, place[0] * half), (z_oth, (1 - place[0]) * half)):

            def put(i, carry):
                value = ref[:, span(i * ROWS, ROWS)]
                cols = span(first + i * ROWS, ROWS)
                table[:, cols] = value
                table8[:, cols] = (value.astype(F32) * scale).astype(F8)
                return carry

            lax.fori_loop(0, half // ROWS, put, 0)

    top, low = ring.wait()
    total[...] = dot_nt(table[...], top[...]) + dot_nt(table8[...], low[...]) * back[0]
    ring.end()


def padded_rows(ref, count):
    value = ref[...]
    extra = jnp.zeros((count - value.shape[0], value.shape[1]), value.dtype)
    return jnp.concatenate([value, extra], axis=0).astype(BF16)


def border_cut(nodes, halo):
    return lambda i: (span(i * ROWS, ROWS), slice(nodes, nodes + halo))


def layer_two_end_kernel(place, flags_t, packs, send, high, rest, total, came, came_oth, later, last_t, hidden_t, slope_t, z_own, z_send, border, border8, back):
    halo = send.shape[0]
    width = hidden_t.shape[0]
    kinds = z_own.shape[0]
    step = pl.program_id(0)
    size = total.shape[1]
    half = size * pl.num_programs(0)

    @pl.when(step == 0)
    def _():
        flat = lambda ref: ref[:, :, 0:width].reshape(halo, width).astype(F32)
        both = flat(came) + flat(came_oth)
        value = jnp.where(flags_t[1:2, :] == 1.0, both.T, stale_columns(packs, 1, halo))
        scale, inverse = scale_of(value)
        border[...] = value.astype(BF16)
        border8[...] = (value * scale).astype(F8)
        back[0] = inverse * (1.0 / REST_GAIN)
        z_send[:, :, 0:128] = jnp.zeros((*z_send.shape[0:2], 128), BF16)
        z_send[:, :, 128:] = later[...]

    sums = total[...] + dot_nt(border[...], high[...]) + dot_nt(border8[...], rest[...]) * back[0]
    value, slope = gelu_both(sums + bias_column(packs, 1))
    value = value.astype(BF16)
    hidden_t[...] = value
    slope_t[...] = slope
    z = dot_nn(padded_rows(last_t, kinds), value).astype(BF16)
    z_own[...] = z
    chosen = dot_nt(pick_rows(send[...], place[0] * half + step * size, size), z)
    chosen = jnp.concatenate([chosen, jnp.zeros((halo, 128 - kinds), F32)], axis=1)
    sent = z_send[:, :, 0:128]
    z_send[:, :, 0:128] = (sent.astype(F32) + chosen.reshape(sent.shape)).astype(BF16)


def put_border(border_grad, total, keep):
    value = (total * keep).T
    bound = value.shape[0] // border_grad.shape[0]
    border_grad[:, 0:bound, :] = value.reshape(border_grad.shape[0], bound, value.shape[1])


def loss_kernel(classes, place, flags_t, came, came_oth, stale_t, bias, labels, mask, total_hbm, high, rest, sums, back_out, border_grad, grads_hbm, grads8_hbm, far_hbm, border_sum, hrows, rrows, total, grads, grads8, far, hbuf, rbuf, in_sems, edge_sems, out_sems, far_sems):
    kinds, half = total.shape
    halo = stale_t.shape[1]
    steps = half // ROWS
    cut = border_cut(2 * half, halo)
    blocks = Stream(
        in_sems,
        (high, cut, hrows, rows_at(ROWS)),
        (rest, cut, rrows, rows_at(ROWS)),
        (total_hbm, cols_at(ROWS), total, cols_at(ROWS)),
    )
    others = rows_at(ROWS, span((1 - place[0]) * half, half))
    edges = Stream(edge_sems, (high, others, hbuf, rows_at(ROWS)), (rest, others, rbuf, rows_at(ROWS)))
    stores = Stream(
        out_sems, *[(a, cols_at(ROWS), b, cols_at(ROWS)) for a, b in ((grads, grads_hbm), (grads8, grads8_hbm))]
    )
    far_stores = Stream(far_sems, (far, all_of, far_hbm, all_of))
    blocks.start_first(steps)
    edges.start(0)
    flat = lambda ref: ref[:, :, 0:128].reshape(halo, 128).astype(F32)
    both = flat(came) + flat(came_oth)
    old = jnp.concatenate([stale_t[...].astype(F32), jnp.zeros((kinds - classes, halo), F32)], axis=0)
    value = jnp.where(flags_t[2:3, :] == 1.0, both.T[0:kinds, :], old)
    scale, back = scale_of(value)
    back = back * (1.0 / REST_GAIN)
    border = value.astype(BF16)
    border8 = (value * scale).astype(F8)
    row = jnp.concatenate([bias[...], jnp.zeros((1, 128 - classes), F32)], axis=1)
    bias_col = jnp.broadcast_to(row, (8, 128)).T[0:kinds, 0:1]
    sums[...] = jnp.zeros(sums.shape, F32)
    border_sum[...] = jnp.zeros(border_sum.shape, F32)
    count = flags_t[3:4, 0:1]
    inverse = (1.0 / (256.0 * REST_GAIN)) / count
    back_out[...] = jnp.broadcast_to(inverse, back_out.shape)

    def far_step(i):
        edges.wait(i)
        here = span(i * ROWS, ROWS)
        both = dot_nn(grads[:, here], hbuf[here, :])
        low = dot_nn(grads8[:, here], rbuf[here, :]) * inverse
        far[...] += both[0:kinds] + both[kinds : 2 * kinds] + low

    def step(i):
        here = span(i * ROWS, ROWS)
        logits = total[:, here] + dot_nt(border, hrows[here, :]) + dot_nt(border8, rrows[here, :]) * back
        logits = logits + bias_col
        kind = lax.broadcasted_iota(I32, logits.shape, 0)
        real = kind < classes
        logits = jnp.where(real, logits, -jnp.inf)
        shifted = logits - jnp.max(logits, axis=0, keepdims=True)
        powers = jnp.exp(shifted)
        norm = jnp.sum(powers, axis=0, keepdims=True)
        logp = jnp.where(real, shifted - jnp.log(norm), 0.0)
        first = (place[0] * steps + i) * (ROWS // 128)
        row_of = lambda ref: jnp.concatenate([ref[pl.ds(first + k, 1), :] for k in range(ROWS // 128)], axis=1)
        target = jnp.where(kind == row_of(labels), 0.9, 0.0) + 0.1 / classes
        used = row_of(mask).astype(F32)
        loss = jnp.sum(target * logp, axis=0, keepdims=True) * used
        grad = jnp.where(real, (powers / norm - target) * (used / count), 0.0)
        sums[0:kinds, :] += lane_sums(grad)
        sums[kinds : kinds + 1, :] -= lane_sums(loss)
        top = grad.astype(BF16)
        tail = (grad - top.astype(F32)).astype(BF16)
        stacked = jnp.concatenate([top, tail], axis=0)
        small = (top.astype(F32) * (256.0 * count)).astype(F8)
        grads[:, here] = stacked
        grads8[:, here] = small
        stores.start(i)
        both = dot_nn(stacked, hrows[here, :])
        low = dot_nn(small, rrows[here, :]) * inverse
        border_sum[0:kinds, :] += both[0:kinds] + both[kinds : 2 * kinds] + low

    far[...] = jnp.zeros(far.shape, F32)
    blocks.next(0, steps)
    edges.start(1)
    step(0)

    def both_steps(i):
        blocks.next(i, steps)

        @pl.when(i + 1 < steps)
        def _():
            edges.start(i + 1)

        far_step(i - 1)
        step(i)

    lax.fori_loop(1, steps, lambda i, c: (both_steps(i), c)[1], 0)
    far_step(steps - 1)
    far_stores.start(0)
    put_border(border_grad, border_sum[...], flags_t[2:3, :])
    stores.wait_all(steps)
    far_stores.wait(0)


def lane_sums(value):
    total = value[:, 0:128]
    for first in range(128, value.shape[1], 128):
        total = total + value[:, first : first + 128]
    return total


def back_three_kernel(place, high, rest, grads, grads8, back, out, hbuf, rbuf, sems):
    kinds, size = out.shape
    base = place[0] * size * pl.num_programs(0)
    ring = Ring((high, rest), (hbuf, rbuf), sems, lambda i: (slice(None), span(base + i * size, size)))
    ring.begin()
    top, low = ring.wait()
    both = dot_nn(grads[...], top[...])
    out[...] = both[0:kinds] + both[kinds : 2 * kinds] + dot_nn(grads8[...], low[...]) * back[0:1, 0:1]
    ring.end()


def back_block(grads, grads8, tails8, back_rest, back_tail, top, low):
    total = dot_nn(grads, top) + dot_nn(grads8, low) * back_rest
    return total + dot_nn(tails8, top.astype(F8)) * back_tail


def back_kernel(place, back, grads, grads8, tails8, high, rest, out, hbuf, rbuf, edge_sems):
    half = out.shape[1]
    steps = half // ROWS
    mine = cols_at(ROWS, place[0] * half)
    edges = Stream(edge_sems, (high, mine, hbuf, cols_at(ROWS)), (rest, mine, rbuf, cols_at(ROWS)))
    edges.start_first(steps)

    def step(i):
        edges.next(i, steps)
        here = span(i * ROWS, ROWS)
        out[:, here] = back_block(
            grads[...], grads8[...], tails8[...], back[0:1, 0:1], back[0:1, 1:2], hbuf[:, here], rbuf[:, here]
        )

    loop(steps, step)


def returned_terms(ret, ret_oth, bound, kinds):
    value = ret[:, 0:bound, :] + ret_oth[:, 0:bound, :]
    value = value.reshape(value.shape[0] * bound, value.shape[2]).T[0:kinds, :]
    top = value.astype(BF16)
    return top, (value - top.astype(F32)).astype(BF16)


def round_gradient(own, came_part, terms, send, first_node):
    chosen = pick_rows(send, first_node, own.shape[1])
    total = own + came_part
    for term in terms:
        total = total + dot_nn(term, chosen)
    return total.astype(BF16)


def end_three_kernel(place, flags_t, ret, ret_oth, last_t, send, far_in_any, near_hbm, hidden_hbm, slope_hbm, high, rest, sums, back_out, border_sum, grad_last, grads, grads8, tails8, far, near, far_in, hidden_t, slope_t, hrows, rrows, grad_rows, hbuf, rbuf, in_sems, row_sems, edge_sems):
    kinds, half = near.shape
    units = slope_t.shape[0]
    parts = ret.shape[0]
    bound = send.shape[0] // parts
    halo = send.shape[0]
    steps = half // ROWS
    cut = border_cut(2 * half, halo)
    blocks = Stream(
        in_sems,
        *[
            (a, cols_at(ROWS), b, cols_at(ROWS))
            for a, b in ((near_hbm, near), (far_in_any, far_in), (hidden_hbm, hidden_t), (slope_hbm, slope_t))
        ],
    )
    borders = Stream(row_sems, (high, cut, hrows, rows_at(ROWS)), (rest, cut, rrows, rows_at(ROWS)))
    others = cols_at(ROWS, (1 - place[0]) * half)
    edges = Stream(edge_sems, (high, others, hbuf, cols_at(ROWS)), (rest, others, rbuf, cols_at(ROWS)))
    for stream in (blocks, borders, edges):
        loop(steps, stream.start)
    terms = returned_terms(ret, ret_oth, bound, kinds)
    weight = padded_rows(last_t, kinds)
    sums[...] = jnp.zeros(sums.shape, F32)
    grad_last[...] = jnp.zeros(grad_last.shape, F32)
    border_sum[...] = jnp.zeros(border_sum.shape, F32)

    def first_step(i, most):
        blocks.wait(i)
        here = span(i * ROWS, ROWS)
        d_z = round_gradient(near[:, here], far_in[:, here], terms, send[...], (place[0] * steps + i) * ROWS)
        grad_last[0:kinds, :] += dot_nt(d_z, hidden_t[:, here])
        grad = dot_tn(weight, d_z) * slope_t[:, here]
        sums[...] += lane_sums(grad)
        grad_rows[:, here] = grad
        return jnp.maximum(most, jnp.max(jnp.abs(grad), axis=0, keepdims=True))

    most = lax.fori_loop(0, steps, first_step, jnp.zeros((1, ROWS), F32))
    scale, back = scale_of(most)
    back_rest, back_tail = back * (1.0 / REST_GAIN), back * (1.0 / TAIL_GAIN)
    lane = lax.broadcasted_iota(I32, back_out.shape, 1)
    back_out[...] = jnp.where(lane == 0, back_rest, back_tail)

    def second_step(i):
        borders.wait(i)
        here = span(i * ROWS, ROWS)
        grad = grad_rows[:, here]
        top = grad.astype(BF16)
        wide = top.astype(F32)
        small = (wide * scale).astype(F8)
        tail = ((grad - wide) * (scale * TAIL_GAIN)).astype(F8)
        grads[:, here] = top
        grads8[:, here] = small
        tails8[:, here] = tail
        border_sum[...] += back_block(top, small, tail, back_rest, back_tail, hrows[here, :], rrows[here, :])

    loop(steps, second_step)
    border_sum[...] = border_sum[...] * flags_t[1:2, :]

    def far_step(i):
        edges.wait(i)
        here = span(i * ROWS, ROWS)
        far[:, here] = back_block(
            grads[...], grads8[...], tails8[...], back_rest, back_tail, hbuf[:, here], rbuf[:, here]
        )

    loop(steps, far_step)


def end_two_kernel(place, border, border_oth, packs, sums_two, sums_out, near, far, came_hbm, late_hbm, hidden_hbm, slope_hbm, feat_hbm, out, out_one, came, came_late, hidden_t, slope_t, near_feat, grad_first, grad_second, sums_one, came_sems, in_sems):
    units, half = near.shape
    halo = border.shape[1]
    steps = half // ROWS
    extra = near_feat.shape[0] // 2
    every = lambda i: (slice(None), slice(None), slice(None))
    fetch = Stream(came_sems, (came_hbm, every, came, every), (late_hbm, every, came_late, every))
    blocks = Stream(
        in_sems,
        *[
            (a, cols_at(ROWS), b, cols_at(ROWS))
            for a, b in ((hidden_hbm, hidden_t), (slope_hbm, slope_t), (feat_hbm, near_feat))
        ],
    )
    loop(steps, blocks.start)
    fetch.start(0)
    weight = packs[:, 128 : 128 + units]
    for ref in (grad_first, grad_second, sums_one):
        ref[...] = jnp.zeros(ref.shape, F32)

    def through(d_z, slope):
        grad = dot_tn(weight, d_z) * slope
        sums_one[...] += lane_sums(grad)
        top = grad.astype(BF16)
        return top, (grad - top.astype(F32)).astype(BF16)

    def step(i):
        blocks.wait(i)
        here = span(i * ROWS, ROWS)
        d_z = (near[:, here] + far[:, here]).astype(BF16)
        grad_second[...] += dot_nt(d_z, hidden_t[:, here])
        top, tail = through(d_z, slope_t[:, here])
        high, low = near_feat[0:extra, here], near_feat[extra:, here]
        grad_first[:, 0:extra] += dot_nt(top, high) + (dot_nt(tail, high) + dot_nt(top, low))

    loop(steps, step)
    fetch.wait(0)
    lanes = lambda ref, first, size: ref[:, :, first : first + size].reshape(halo, size)
    d_z = (border[...] + border_oth[...]).astype(BF16)
    grad_second[...] += dot_nn(d_z, lanes(came, units, units))
    slope = lanes(came, 2 * units, units).astype(F32) + lanes(came_late, 128, units).astype(F32)
    top, tail = through(d_z, slope.T)
    high, low = lanes(came_late, 128 + units, 128), lanes(came_late, 256 + units, 128)
    grad_first[...] += dot_nn(top, high) + (dot_nn(tail, high) + dot_nn(top, low))
    lane = lax.broadcasted_iota(I32, (64, 128), 1)
    column = lambda value: jnp.sum(value, axis=1, keepdims=True)
    for k, ref in enumerate((out, out_one)):
        rows = span(jnp.bitwise_xor(place[0] + 2 * place[1], k) * 64, 64)
        value = jnp.where(lane < FLAG_LANE, grad_first[rows, :], 0.0)
        value = jnp.where(lane == FLAG_LANE, column(sums_one[rows, :]), value)
        value = jnp.where(lane == FLAG_LANE + 1, column(sums_two[rows, :]), value)
        ref[0:64, :] = jnp.where(lane == FLAG_LANE + 2, column(sums_out[...]), value)
        ref[64:128, :] = grad_second[rows, 0:128]
        ref[128:192, :] = grad_second[rows, 128:256]


def scatter_kernel(mine, came, last, last_came, out):
    total = mine[...] + came[...]
    last_total = last[...] + last_came[...]
    parts = out.shape[0]
    size = 64 // parts
    for q in range(parts):
        pieces = [total[64 * k + q * size : 64 * k + (q + 1) * size, :] for k in range(3)]
        chunk = last_total[q * size : (q + 1) * size, :]
        out[q] = jnp.concatenate(pieces + [chunk[:, 0:128], chunk[:, 128:256]], axis=0)


def joined(came, first, size):
    return came[:, first : first + size, :].reshape(64, 128)


def gather_kernel(came, out):
    value = jnp.sum(came[...], axis=0)
    for p in range(came.shape[0]):
        out[p] = value


def adamw(weight, moment, square, gradient):
    moment = beta_one * moment + (1.0 - beta_one) * gradient
    square = beta_two * square + (1.0 - beta_two) * gradient * gradient
    moment_hat = moment / (1.0 - beta_one**STEP)
    square_hat = square / (1.0 - beta_two**STEP)
    weight = weight - rate_step * (
        moment_hat / (jnp.sqrt(square_hat) + epsilon) + decay_rate * weight
    )
    return (weight, moment, square)


def update_kernel(came, flags_t, *refs):
    params, outs = refs[0:15], refs[15:]
    parts = came.shape[0]
    size = 64 // parts
    width, kinds = params[0].shape[1], params[6].shape[0]
    total = joined(came, 0, size)
    halves = [joined(came, size, size), joined(came, 2 * size, size)]
    turned = jnp.concatenate([total, jnp.zeros((64, 128), F32)], axis=0).T
    gradients = (
        total[:, 0:width],
        jnp.concatenate(halves, axis=1),
        jnp.concatenate([joined(came, 3 * size, size), joined(came, 4 * size, size)], axis=1)[0:kinds, :],
        turned[FLAG_LANE : FLAG_LANE + 2, 0:64],
        turned[FLAG_LANE + 2 : FLAG_LANE + 3, 0:kinds],
    )
    for k, gradient in enumerate(gradients):
        values = adamw(*[ref[...] for ref in params[3 * k : 3 * k + 3]], gradient)
        for ref, value in zip(outs[3 * k : 3 * k + 3], values):
            ref[...] = value
    padded = turned[FLAG_LANE + 2 : FLAG_LANE + 3, 48:49]
    outs[15][...] = jnp.broadcast_to(padded, (1, 128))
    outs[16][...] = jnp.broadcast_to(flags_t[3:4, 0:1], (1, 128))


def body(
    parts,
    reps,
    features,
    labels,
    train_mask,
    edge_src,
    edge_norm,
    send_rows,
    changed,
    cache_hidden,
    cache_out,
    first_weight,
    second_weight,
    last_weight,
    hidden_bias,
    out_bias,
    moment_first,
    moment_second,
    moment_last,
    moment_hidden,
    moment_out,
    square_first,
    square_second,
    square_last,
    square_hidden,
    square_out,
):
    nodes, in_width = features.shape
    half = nodes // 2
    bound = send_rows.shape[2]
    halo = parts * bound
    table = nodes + halo
    units, classes = last_weight.shape
    kinds = -(-classes // 16) * 16
    steps, fine = half // ROWS, half // FINE

    rep = lax.axis_index("rep")
    place = jnp.stack([lax.rem(rep, 2), lax.div(rep, 2)]).astype(I32)
    where = (place, SMEM)
    feat_t = features.T
    last_t = last_weight.T
    label_rows = labels.reshape(nodes // 128, 128)
    mask_rows = train_mask.reshape(nodes // 128, 128)

    def swap(x, k=1):
        return lax.ppermute(x, "rep", [(i, i ^ k) for i in range(reps)])

    def exchange(x):
        return lax.all_to_all(x, "dom", split_axis=0, concat_axis=0, tiled=True)

    def late(after, *arrays):
        return lax.optimization_barrier((*arrays, after))

    vm = pltpu.VMEM
    whole = lambda a: (a, whole_spec(a.shape))
    work = 2 * half * table * units
    pack_width = 256 + units + 2 * halo
    extra = -(-in_width // 16) * 16
    both = units + extra
    rows_out, pack, send = run(
        pack_kernel,
        "pack",
        [
            whole(feat_t),
            whole(send_rows.reshape(parts, bound)),
            whole(changed.T),
            *[whole(a) for a in (mask_rows, first_weight.T, second_weight.T)],
            *[whole(a) for a in (jnp.transpose(cache_hidden, (0, 2, 1)), hidden_bias)],
        ],
        [
            ((parts, bound, 128), BF16, VMEM),
            ((units // reps, pack_width), BF16, VMEM),
            ((halo, 1), I32, VMEM),
        ],
        flops=2 * halo * nodes * 128,
        grid=(1,),
    )
    packs = [pack if k == 0 else swap(pack, k) for k in range(reps)]
    rows = exchange(rows_out)
    node_block = lambda size, rows: pl.BlockSpec((rows, size), lambda i: (0, i))
    block, fine_block = node_block(ROWS, units), node_block(FINE, units)
    scalar = pltpu.SMEM((1,), F32)
    packs, most, first_table = run(
        table_kernel,
        "table",
        [where, *placed(VMEM, *packs), (feat_t, HBM)],
        [((units, pack_width), BF16, OWN), ((units, 128), F32, VMEM), ((units + extra, nodes), BF16, HBM)],
        [
            vm((in_width, nodes), BF16),
            vm((units + extra, nodes), BF16),
            sems(1, 4),
            sems(1, 4),
        ],
        flops=2 * units * nodes * in_width,
    )
    rows, most = late(most, rows)
    held = fine if half * table * 3 <= RESIDENT_BYTES else min(fine, 4)
    z_send, later, flags_t, high, rest, hidden_one, slope_one, z_own, near_feat = run(
        layer_one_kernel,
        "layer_one",
        [where, *placed(OWN, edge_src.T, edge_norm.T), *placed(VMEM, rows, send, most), *placed(HBM, packs, first_table)],
        [
            ((parts, bound, 3 * units), BF16, VMEM),
            ((parts, bound, units + 256), BF16, OWN),
            ((8, halo), F32, OWN),
            ((half, table), BF16, HBM),
            ((half, table), F8, HBM),
            ((units, half), BF16, HBM),
            ((units, half), F32, HBM),
            ((units, half), BF16, HBM),
            ((2 * extra, half), BF16, HBM),
        ],
        [
            vm((units, pack_width), BF16),
            vm((both, table), BF16),
            vm((-(-both // 32) * 32, table), F8),
            vm((held * FINE, table), BF16),
            vm((held * FINE, table), F8),
            vm((units, half), BF16),
            vm((units, half), F32),
            vm((units, half), BF16),
            vm((2 * extra, half), BF16),
            sems(2, 1),
            sems(2, fine),
            sems(4, fine),
        ],
        flops=2 * work,
    )
    edge = placed(HBM, high, rest)

    def own_part(z_own, z_oth, name):
        n = z_own.shape[0]
        return run(
            own_part_kernel,
            name,
            [where, *edge, whole(z_own), (z_oth, VMEM)],
            [((n, half), F32, node_block(FINE, n))],
            [vm((n, nodes), BF16), vm((n, nodes), F8), scalar, *ring_scratch((FINE, nodes))],
            flops=work,
            grid=(fine,),
        )[0]

    z_oth = swap(z_own)
    came = exchange(z_send)
    total = own_part(z_own, z_oth, "layer_two_own")
    came, total = late(total, came)
    came_one = came
    came_oth = swap(came)
    wide = half // 2
    wide_block = node_block(wide, units)
    border_block = lambda array: (array, pl.BlockSpec((wide, halo), lambda i: (i, nodes // halo)))
    hidden_two, slope_two, z_own, z_send = run(
        layer_two_end_kernel,
        "layer_two_end",
        [where, whole(flags_t), whole(packs), (send, VMEM), border_block(high), border_block(rest), (total, wide_block)]
        + placed(VMEM, came, came_oth)
        + [whole(later), whole(last_t)],
        [
            ((units, half), BF16, wide_block),
            ((units, half), F32, wide_block),
            ((kinds, half), BF16, node_block(wide, kinds)),
            ((parts, bound, 128 + units + 256), BF16, whole_spec((parts, bound, 128 + units + 256))),
        ],
        [vm((units, halo), BF16), vm((units, halo), F8), scalar],
        flops=work // 4,
        grid=(half // wide,),
    )
    z_oth = swap(z_own)
    came = exchange(z_send)
    total = own_part(z_own, z_oth, "layer_three_own")
    came, total = late(total, came)
    came_two = came
    came_oth = swap(came)
    border_rows = [vm((half, halo), BF16), vm((half, halo), F8)]
    sums_out, back, border_grad, grads, grads8, far = run(
        functools.partial(loss_kernel, classes),
        "loss",
        [
            where,
            *placed(VMEM, flags_t, came, came_oth, cache_out.T, out_bias.reshape(1, classes), label_rows, mask_rows),
            (total, HBM),
            *edge,
        ],
        [
            ((64, 128), F32, VMEM),
            ((8, 128), F32, VMEM),
            ((parts, bound, 128), F32, VMEM),
            ((2 * kinds, half), BF16, HBM),
            ((kinds, half), F8, HBM),
            ((kinds, half), F32, HBM),
        ],
        [
            vm((128, halo), F32),
            *border_rows,
            vm((kinds, half), F32),
            vm((2 * kinds, half), BF16),
            vm((kinds, half), F8),
            vm((kinds, half), F32),
            vm((half, half), BF16),
            vm((half, half), F8),
            sems(3, steps),
            sems(2, steps),
            sems(2, steps),
            sems(1, 1),
        ],
        flops=work,
    )
    far = swap(far)
    ret = exchange(border_grad)
    near = run(
        back_three_kernel,
        "back_three",
        [where, *edge, whole(grads), whole(grads8), (back, VMEM)],
        [((kinds, half), F32, node_block(ROWS, kinds))],
        ring_scratch((half, ROWS)),
        flops=work // 2,
        grid=(steps,),
    )[0]
    ret, far, near = late(near, ret, far)
    ret_oth = swap(ret)
    sums_two, back, border, last, grads, grads8, tails8, far = run(
        end_three_kernel,
        "end_three",
        [where, *placed(VMEM, flags_t, ret, ret_oth, last_t, send), (far, ANY)]
        + [*placed(HBM, near, hidden_two, slope_two), *edge],
        [
            ((units, 128), F32, VMEM),
            ((8, 128), F32, VMEM),
            ((units, halo), F32, VMEM),
            ((64, units), F32, VMEM),
            ((units, half), BF16, VMEM),
            ((units, half), F8, VMEM),
            ((units, half), F8, VMEM),
            ((units, half), F32, VMEM),
        ],
        [
            vm((kinds, half), F32),
            vm((kinds, half), F32),
            vm((units, half), BF16),
            vm((units, half), F32),
            *border_rows,
            vm((units, half), F32),
            vm((half, half), BF16),
            vm((half, half), F8),
            sems(4, steps),
            sems(2, steps),
            sems(2, steps),
        ],
        flops=work,
        limit=LOW_LIMIT,
    )
    far, border_oth, last_oth = swap(far), swap(border), swap(last)
    near = run(
        back_kernel,
        "back",
        [where, *placed(VMEM, back, grads, grads8, tails8), *edge],
        [((units, half), F32, VMEM)],
        [vm((half, half), BF16), vm((half, half), F8), sems(2, steps)],
        flops=work // 2,
        limit=LOW_LIMIT,
    )[0]
    mine, theirs = run(
        end_two_kernel,
        "end_two",
        [where, *placed(VMEM, border, border_oth), (packs, OWN), *placed(VMEM, sums_two, sums_out, near, far)]
        + [*placed(HBM, came_one, came_two, hidden_one, slope_one, near_feat)],
        [((192, 128), F32, VMEM)] * 2,
        [
            vm(came_one.shape, BF16),
            vm(came_two.shape, BF16),
            vm((units, half), BF16),
            vm((units, half), F32),
            vm((2 * extra, half), BF16),
            vm((units, 128), F32),
            vm((units, units), F32),
            vm((units, 128), F32),
            sems(2, 1),
            sems(3, steps),
        ],
        flops=work // 4,
        limit=LOW_LIMIT,
    )
    scattered = run(
        scatter_kernel,
        "scatter",
        placed(VMEM, mine, swap(theirs), last, last_oth),
        [((parts, 5 * 64 // parts, 128), F32, VMEM)],
    )[0]
    gathered = run(
        gather_kernel,
        "gather",
        placed(VMEM, exchange(scattered)),
        [(scattered.shape, F32, VMEM)],
    )[0]
    came = exchange(gathered)

    turn = lambda x: x.T
    same = lambda x: x
    row = lambda x: x.reshape(1, -1)
    forms = (turn, turn, turn, same, row)
    weights = (first_weight, second_weight, last_weight, hidden_bias, out_bias)
    moments = (moment_first, moment_second, moment_last, moment_hidden, moment_out)
    squares = (square_first, square_second, square_last, square_hidden, square_out)
    params = [form(x) for form, triple in zip(forms, zip(weights, moments, squares)) for x in triple]
    outs = run(
        update_kernel,
        "update",
        placed(VMEM, came, flags_t, *params),
        [(p.shape, F32, VMEM) for p in params] + [((1, 128), F32, VMEM)] * 2,
    )
    undo = (turn, turn, turn, same, lambda x: x.reshape(-1))
    results = [undo[k // 3](x) for k, x in enumerate(outs[0:15])]
    return (outs[15][0, 0], outs[16][0, 0], *results)


def solution(mesh):
    placed = (
        P("dom", None),
        P("dom"),
        P("dom"),
        P("dom", None),
        P("dom", None),
        P("dom", None, None),
        P(None, "dom"),
        P(None, "dom", "rep"),
        P("dom", None),
        P(None, "rep"),
        P(None, "rep"),
        P(),
        P(None, "rep"),
        P(),
        P(None, "rep"),
        P(None, "rep"),
        P(),
        P(None, "rep"),
        P(),
        P(None, "rep"),
        P(None, "rep"),
        P(),
        P(None, "rep"),
        P(),
    )
    return jax.shard_map(
        functools.partial(body, mesh.shape["dom"], mesh.shape["rep"]),
        mesh=mesh,
        in_specs=placed,
        out_specs=(P(), P()) + (P(None, "rep"),) * 6 + (P(),) * 3 + (P(None, "rep"),) * 3 + (P(),) * 3,
        check_vma=False,
    )
```

```python
import functools

import jax
import jax.numpy as jnp
from jax import lax
from jax.experimental import pallas as pl
from jax.experimental.pallas import tpu as pltpu
from jax.sharding import PartitionSpec as P

STEP = 5
beta_one = 0.5
beta_two = 0.5
rate_step = 0.03
decay_rate = 0.01
epsilon = 1e-08

BF16, F32, F8, I32 = jnp.bfloat16, jnp.float32, jnp.float8_e4m3fn, jnp.int32
REST_GAIN = 4096.0
TAIL_GAIN = 256.0
FLAG_LANE = 100
ROWS = 512
FINE = 256
AHEAD = 3
LIMIT = 52 << 20
LOW_LIMIT = 34 << 20
RESIDENT_BYTES = 30 << 20

SMEM = pl.BlockSpec(memory_space=pltpu.SMEM)
VMEM = pl.BlockSpec(memory_space=pltpu.VMEM)
OWN = pl.BlockSpec(memory_space=pltpu.VMEM)
HBM = pl.BlockSpec(memory_space=pltpu.HBM)
ANY = pl.BlockSpec(memory_space=pl.ANY)


def whole_spec(shape):
    return pl.BlockSpec(shape, lambda *_: (0,) * len(shape))


def placed(spec, *arrays):
    return [(a, spec) for a in arrays]


def run(kernel, name, args, outs, scratch=(), flops=0, grid=(), limit=LIMIT):
    pinned = [
        a if any(spec is s for s in (SMEM, VMEM, ANY)) else pltpu.with_memory_space_constraint(a, pltpu.HBM)
        for a, spec in args
    ]
    return pl.pallas_call(
        kernel,
        grid=grid,
        in_specs=[spec for _, spec in args],
        out_specs=[spec for _, _, spec in outs],
        out_shape=[
            jax.ShapeDtypeStruct(shape, kind) if spec is VMEM else pltpu.HBM(shape, kind)
            for shape, kind, spec in outs
        ],
        scratch_shapes=list(scratch),
        name=name,
        cost_estimate=pl.CostEstimate(flops=flops, bytes_accessed=1 << 20, transcendentals=0),
        compiler_params=pltpu.CompilerParams(vmem_limit_bytes=limit),
    )(*pinned)


def dot_nn(left, right):
    return lax.dot_general(left, right, (((1,), (0,)), ((), ())), preferred_element_type=F32)


def dot_nt(left, right):
    return lax.dot_general(left, right, (((1,), (1,)), ((), ())), preferred_element_type=F32)


def dot_tn(left, right):
    return lax.dot_general(left, right, (((0,), (0,)), ((), ())), preferred_element_type=F32)


def scale_of(value):
    most = jnp.maximum(jnp.max(jnp.abs(value)), 1e-30)
    return 256.0 / most, most * (1.0 / 256.0)


def span(start, size):
    return pl.ds(pl.multiple_of(start, size), size)


def rows_at(size, cols=slice(None)):
    return lambda i: (span(i * size, size), cols)


def cols_at(size, base=0):
    return lambda i: (slice(None), span(base + i * size, size))


def all_of(i):
    return (slice(None), slice(None))


def loop(count, step):
    def one(i, carry):
        step(i)
        return carry

    lax.fori_loop(0, count, one, 0)


class Ring:
    def __init__(self, refs, bufs, sems, cut, first=0):
        self.refs, self.bufs, self.sems, self.cut = refs, bufs, sems, cut
        self.begins = pl.program_id(0) == 0
        self.step, self.steps = pl.program_id(0) - first, pl.num_programs(0) - first
        self.depth = bufs[0].shape[0]
        self.slot = lax.rem(self.step, self.depth)

    def copies(self, step, slot):
        return [
            pltpu.make_async_copy(ref.at[self.cut(step)], buf.at[slot], self.sems.at[k, slot])
            for k, (ref, buf) in enumerate(zip(self.refs, self.bufs))
        ]

    def begin(self):
        for step in range(self.depth):

            @pl.when(self.begins & (step < self.steps))
            def _():
                for copy in self.copies(step, step):
                    copy.start()

    def wait(self):
        for copy in self.copies(self.step, self.slot):
            copy.wait()
        return [buf.at[self.slot] for buf in self.bufs]

    def end(self):
        @pl.when(self.step + self.depth < self.steps)
        def _():
            for copy in self.copies(self.step + self.depth, self.slot):
                copy.start()


def ring_scratch(shape, depth=3):
    kinds = (BF16, F8)
    return [pltpu.VMEM((depth, *shape), kind) for kind in kinds] + [pltpu.SemaphoreType.DMA((len(kinds), depth))]


class Stream:
    def __init__(self, sems, *legs):
        self.sems, self.legs = sems, legs

    def copies(self, i):
        return [
            pltpu.make_async_copy(source.at[source_at(i)], target.at[target_at(i)], self.sems.at[k, i])
            for k, (source, source_at, target, target_at) in enumerate(self.legs)
        ]

    def start(self, i):
        for copy in self.copies(i):
            copy.start()

    def wait(self, i):
        for copy in self.copies(i):
            copy.wait()

    def wait_all(self, count):
        loop(count, self.wait)

    def start_first(self, count):
        for i in range(min(AHEAD, count)):
            self.start(i)

    def next(self, i, count):
        self.wait(i)

        @pl.when(i + AHEAD < count)
        def _():
            self.start(i + AHEAD)


def sems(legs, count):
    return pltpu.SemaphoreType.DMA((legs, count))


def pick_rows(send, first, count):
    nodes = lax.broadcasted_iota(I32, (send.shape[0], count), 1) + first
    return jnp.where(send == nodes, 1.0, 0.0).astype(BF16)


def pack_kernel(feat_t, send_list, changed, mask, first_t, second_t, cache_t, bias, rows_out, pack_out, send):
    nodes, halo = feat_t.shape[1], send.shape[0]
    parts, bound = send_list.shape
    turned = send_list[...].astype(F32)
    turned = jnp.concatenate([turned, jnp.zeros((parts, 128 - bound), F32)], axis=1)
    turned = turned.T.astype(I32)
    for q in range(parts):
        send[q * bound : (q + 1) * bound, :] = turned[0:bound, q : q + 1]
    width, cols = feat_t.shape[0], first_t.shape[0]

    def pick(i, total):
        return total + dot_nt(pick_rows(send[...], i * ROWS, ROWS), feat_t[:, span(i * ROWS, ROWS)])

    total = jnp.zeros((halo, width), F32)
    for i in range(nodes // ROWS):
        total = pick(i, total)
    count = jnp.sum(mask[...].astype(F32))
    many = jnp.floor(count * (1.0 / 64.0))
    lane = lax.broadcasted_iota(I32, (halo, 128), 1)
    row = jnp.concatenate([total, jnp.zeros((halo, 128 - width), F32)], axis=1)
    for layer in range(3):
        row = jnp.where(lane == FLAG_LANE + layer, changed[0:1, layer : layer + 1].astype(F32), row)
    row = jnp.where(lane == FLAG_LANE + 3, many, row)
    row = jnp.where(lane == FLAG_LANE + 4, count - 64.0 * many, row)
    rows_out[...] = row.astype(BF16).reshape(rows_out.shape)

    units = second_t.shape[1]
    pack_out[:, 0:128] = jnp.concatenate(
        [first_t[...], jnp.zeros((cols, 128 - width), F32)], axis=1
    ).astype(BF16)
    pack_out[:, 128 : 128 + units] = second_t[...].astype(BF16)
    left = jnp.concatenate([bias[...], jnp.zeros((2, 128 - cols), F32)], axis=1)
    terms = []
    for _ in range(3):
        term = left.astype(BF16).astype(F32)
        terms.append(term)
        left = left - term
    terms = jnp.concatenate(terms + [jnp.zeros((122, 128), F32)], axis=0).T
    pack_out[:, 128 + units : 256 + units] = terms[0:cols, :].astype(BF16)
    base = 256 + units
    for layer in range(2):
        pack_out[:, base + layer * halo : base + (layer + 1) * halo] = cache_t[layer]


def bias_column(packs, layer):
    units = packs.shape[0]
    terms = packs[:, 128 + units : 256 + units].astype(F32)
    return terms[:, layer : layer + 1] + terms[:, layer + 2 : layer + 3] + terms[:, layer + 4 : layer + 5]


def stale_columns(packs, layer, halo):
    base = 256 + packs.shape[0] + layer * halo
    return packs[:, base : base + halo].astype(F32)


def table_kernel(place, pack, pack_one, pack_two, pack_three, feat_hbm, packs, most_out, table_hbm, feat_t, table, in_sems, out_sems):
    width, nodes = feat_t.shape
    units = packs.shape[0]
    steps = 4
    size = nodes // steps
    extra = jnp.zeros((table.shape[0] - units - width, size), BF16)
    blocks = Stream(in_sems, (feat_hbm, cols_at(size), feat_t, cols_at(size)))
    stores = Stream(out_sems, (table, cols_at(size), table_hbm, cols_at(size)))
    loop(steps, blocks.start)
    for k, ref in enumerate((pack, pack_one, pack_two, pack_three)):
        packs[span(jnp.bitwise_xor(place[0] + 2 * place[1], k) * 64, 64), :] = ref[...]
    weight = packs[:, 0:width]

    def step(i, most):
        blocks.wait(i)
        here = span(i * size, size)
        z = dot_nn(weight, feat_t[:, here])
        table[0:units, here] = z.astype(BF16)
        table[units:, here] = jnp.concatenate([feat_t[:, here], extra], axis=0)
        stores.start(i)
        return jnp.maximum(most, lane_most(z))

    most = lax.fori_loop(0, steps, step, jnp.zeros((packs.shape[0], 128), F32))
    most_out[...] = most
    stores.wait_all(steps)


def lane_most(value):
    most = jnp.abs(value[:, 0:128])
    for first in range(128, value.shape[1], 128):
        most = jnp.maximum(most, jnp.abs(value[:, first : first + 128]))
    return most


def gelu_both(u):
    square = u * u
    t = jnp.tanh(0.79788456 * (u + 0.044715 * u * square))
    half = 0.5 * (1.0 + t)
    slope = half + 0.5 * u * (1.0 - t * t) * (0.79788456 * (1.0 + 3.0 * 0.044715 * square))
    return u * half, slope


def layer_one_kernel(place, src_t, norm_t, rows, send, most, packs_hbm, table_hbm, z_send, later, flags_t, high_hbm, rest_hbm, hidden_hbm, slope_hbm, z_hbm, near_hbm, packs, table, table8, high, rest, hidden_t, slope_t, z_own, near_feat, in_sems, edge_sems, out_sems):
    slots = src_t.shape[0]
    units, half = hidden_t.shape
    nodes = 2 * half
    halo = send.shape[0]
    blocks = high.shape[1] // 256
    per_group = 256 // slots
    steps = half // FINE
    fetch = Stream(in_sems, (packs_hbm, all_of, packs, all_of), (table_hbm, all_of, table, lambda i: (slice(None), slice(0, nodes))))
    fetch.start(0)
    depth = high.shape[0] // FINE
    around = lambda i, count: i if depth >= steps else lax.rem(i, count)
    slot_of = lambda i: span(around(i, depth) * FINE, FINE)
    slot_at = lambda i: (slot_of(i), slice(None))
    edge_stores = Stream(edge_sems, (high, slot_at, high_hbm, rows_at(FINE)), (rest, slot_at, rest_hbm, rows_at(FINE)))
    stores = Stream(
        out_sems,
        *[
            (a, cols_at(FINE), b, cols_at(FINE))
            for a, b in ((hidden_t, hidden_hbm), (slope_t, slope_hbm), (z_own, z_hbm), (near_feat, near_hbm))
        ],
    )
    in_slot = lax.broadcasted_iota(I32, (8, 128), 1) // per_group == lax.broadcasted_iota(I32, (8, 128), 0)
    node_row = lax.broadcasted_iota(I32, (per_group, 256), 0)
    mine = lax.rem(lax.broadcasted_iota(I32, (per_group, 256), 1), per_group) == node_row
    inner = lax.broadcasted_iota(I32, (256, 256), 0)

    def lean(tile):
        return [
            pltpu.roll(tile[first : first + 8, :], 0, 1, stride=per_group, stride_axis=0)
            for first in range(0, slots, 8)
        ]

    def flat(tiles, group):
        moved = [pltpu.roll(tile, (128 - per_group * group) % 128, 1) for tile in tiles]
        return jnp.concatenate(
            [jnp.sum(jnp.where(in_slot, tile, 0), axis=0, keepdims=True) for tile in moved], axis=1
        )

    def one(at, weight):
        weight_high = weight.astype(BF16).astype(F32)
        hit = inner == jnp.bitwise_and(at, 255)
        right = jnp.where(hit, weight_high, 0.0).astype(BF16)
        right_rest = jnp.where(hit, (weight - weight_high) * REST_GAIN, 0.0).astype(BF16)
        block = jnp.where(mine, jnp.right_shift(at, 8), -1)
        left = jnp.concatenate(
            [jnp.where(block == j, 1.0, 0.0).astype(BF16) for j in range(blocks)], axis=0
        )
        return dot_nt(left, right), dot_nt(left, right_rest)

    def build(i):
        here = span(place[0] * half + i * 128, 128)
        at, weight = src_t[:, here], norm_t[:, here]
        slot = lax.broadcasted_iota(I32, at.shape, 0)
        merged, repeat = weight, slot < 0
        for shift in range(1, slots):
            same = at == pltpu.roll(at, shift, 0)
            merged = merged + jnp.where(same, pltpu.roll(weight, shift, 0), 0.0)
            repeat = repeat | (same & (slot >= shift))
        source, weights = lean(at), lean(jnp.where(repeat, 0.0, merged))
        pairs = [one(flat(source, group), flat(weights, group)) for group in range(128 // per_group)]
        rows = span(around(i, high.shape[0] // 128) * 128, 128)
        for j in range(blocks):
            cols = slice(256 * j, 256 * (j + 1))
            for ref, parts in zip((high, rest), zip(*pairs)):
                piece = jnp.concatenate([p[per_group * j : per_group * (j + 1), :] for p in parts], axis=0)
                ref[rows, cols] = piece.astype(ref.dtype)

    def build_block(i):
        for k in range(FINE // 128):
            build(i * (FINE // 128) + k)
        edge_stores.start(i)

    flat_rows = rows[...].reshape(halo, 128)
    turned = flat_rows.astype(F32).T
    flags = turned[FLAG_LANE : FLAG_LANE + 8, :]
    counts = jnp.sum(rows[...].astype(F32)[:, 0, :], axis=0, keepdims=True)
    count = 64.0 * counts[:, FLAG_LANE + 3 : FLAG_LANE + 4] + counts[:, FLAG_LANE + 4 : FLAG_LANE + 5]
    row = lax.broadcasted_iota(I32, flags.shape, 0)
    flags_t[...] = jnp.where(row == 3, count, flags)
    loop(FINE // 128, build)
    edge_stores.start(0)
    fetch.wait(0)
    border = dot_nt(packs[:, 0:FLAG_LANE], flat_rows[:, 0:FLAG_LANE]).astype(BF16).astype(F32)
    border = jnp.where(flags[0:1, :] == 1.0, border, stale_columns(packs, 0, halo))
    table[0:units, nodes : nodes + halo] = border.astype(BF16)
    extra = table.shape[0] - units
    kept = lax.broadcasted_iota(I32, (extra, halo), 0) < FLAG_LANE
    kept = kept & (flags[0:1, :] == 1.0)
    table[units:, nodes : nodes + halo] = jnp.where(kept, turned[0:extra, :], 0.0).astype(BF16)
    scale, back = scale_of(jnp.maximum(jnp.max(most[...]), jnp.max(jnp.abs(border))))
    back = back * (1.0 / REST_GAIN)
    bias = bias_column(packs, 0)

    def small(i):
        here = span(i * 256, 256)
        table8[:, here] = (table[0:units, here].astype(F32) * scale).astype(F8)

    for i in range((nodes + halo) // 256):
        small(i)

    def sums(i):
        here = slot_of(i)
        low = dot_nt(table8[...], rest[here, :]) * back
        top = dot_nt(table[...], high[here, :])
        return jnp.concatenate([top[0:units] + low, top[units:]], axis=0)

    def keep(i, total):
        here = span(i * FINE, FINE)
        slope_t[:, here] = total[0:units]
        value = total[units:]
        top = value.astype(BF16)
        near_feat[0:extra, here] = top
        near_feat[extra:, here] = (value - top.astype(F32)).astype(BF16)

    def finish(i):
        here = span(i * FINE, FINE)
        value, slope = gelu_both(slope_t[:, here] + bias)
        value = value.astype(BF16)
        hidden_t[:, here] = value
        slope_t[:, here] = slope
        z = dot_nn(packs[:, 128 : 128 + units], value).astype(BF16)
        z_own[:, here] = z
        stores.start(i)

    def step(i, carry):
        if depth < steps:

            @pl.when(i + 1 >= depth)
            def _():
                edge_stores.wait(i + 1 - depth)

        total = sums(i)
        finish(i - 1)
        build_block(i + 1)
        keep(i, total)
        return carry

    keep(0, sums(0))
    build_block(1)
    lax.fori_loop(1, steps - 1, step, 0)
    keep(steps - 1, sums(steps - 1))
    finish(steps - 2)
    finish(steps - 1)

    bound = z_send.shape[1]
    group = 256 // bound

    def send_some(c):
        chosen = pick_rows(send[span(c * 256, 256), :], place[0] * half, half)
        to = pl.ds(c * group, group)

        def put(ref, first, rows):
            value = dot_nt(chosen, rows).astype(BF16)
            ref[to, :, first : first + value.shape[1]] = value.reshape(group, bound, value.shape[1])

        slope = slope_t[...]
        top = slope.astype(BF16)
        put(z_send, 0, z_own[...])
        put(z_send, units, hidden_t[...])
        put(z_send, 2 * units, top)
        put(later, 0, (slope - top.astype(F32)).astype(BF16))
        later[to, :, units:] = jnp.zeros((group, bound, 256), BF16)
        put(later, units, near_feat[0:extra, :])
        put(later, units + 128, near_feat[extra:, :])

    loop(halo // 256, send_some)
    stores.wait_all(steps)
    for i in range(steps - depth, steps):
        edge_stores.wait(i)


def own_part_kernel(place, high, rest, z_own, z_oth, total, table, table8, back, hbuf, rbuf, sems):
    half = z_own.shape[1]
    nodes = 2 * half
    ring = Ring((high, rest), (hbuf, rbuf), sems, lambda i: (span(i * FINE, FINE), slice(0, nodes)))
    ring.begin()

    @pl.when(pl.program_id(0) == 0)
    def _():
        def larger(i, most):
            here = span(i * ROWS, ROWS)
            both = jnp.maximum(lane_most(z_own[:, here].astype(F32)), lane_most(z_oth[:, here].astype(F32)))
            return jnp.maximum(most, both)

        most = lax.fori_loop(0, half // ROWS, larger, jnp.zeros((z_own.shape[0], 128), F32))
        scale, inverse = scale_of(most)
        back[0] = inverse * (1.0 / REST_GAIN)
        for ref, first in ((z_own, place[0] * half), (z_oth, (1 - place[0]) * half)):

            def put(i, carry):
                value = ref[:, span(i * ROWS, ROWS)]
                cols = span(first + i * ROWS, ROWS)
                table[:, cols] = value
                table8[:, cols] = (value.astype(F32) * scale).astype(F8)
                return carry

            lax.fori_loop(0, half // ROWS, put, 0)

    top, low = ring.wait()
    total[...] = dot_nt(table[...], top[...]) + dot_nt(table8[...], low[...]) * back[0]
    ring.end()


def padded_rows(ref, count):
    value = ref[...]
    extra = jnp.zeros((count - value.shape[0], value.shape[1]), value.dtype)
    return jnp.concatenate([value, extra], axis=0).astype(BF16)


def border_cut(nodes, halo):
    return lambda i: (span(i * ROWS, ROWS), slice(nodes, nodes + halo))


def layer_two_end_kernel(place, flags_t, packs, send, high, rest, total, came, came_oth, later, last_t, hidden_t, slope_t, z_own, z_send, border, border8, back):
    halo = send.shape[0]
    width = hidden_t.shape[0]
    kinds = z_own.shape[0]
    step = pl.program_id(0)
    size = total.shape[1]
    half = size * pl.num_programs(0)

    @pl.when(step == 0)
    def _():
        flat = lambda ref: ref[:, :, 0:width].reshape(halo, width).astype(F32)
        both = flat(came) + flat(came_oth)
        value = jnp.where(flags_t[1:2, :] == 1.0, both.T, stale_columns(packs, 1, halo))
        scale, inverse = scale_of(value)
        border[...] = value.astype(BF16)
        border8[...] = (value * scale).astype(F8)
        back[0] = inverse * (1.0 / REST_GAIN)
        z_send[:, :, 0:128] = jnp.zeros((*z_send.shape[0:2], 128), BF16)
        z_send[:, :, 128:] = later[...]

    sums = total[...] + dot_nt(border[...], high[...]) + dot_nt(border8[...], rest[...]) * back[0]
    value, slope = gelu_both(sums + bias_column(packs, 1))
    value = value.astype(BF16)
    hidden_t[...] = value
    slope_t[...] = slope
    z = dot_nn(padded_rows(last_t, kinds), value).astype(BF16)
    z_own[...] = z
    chosen = dot_nt(pick_rows(send[...], place[0] * half + step * size, size), z)
    chosen = jnp.concatenate([chosen, jnp.zeros((halo, 128 - kinds), F32)], axis=1)
    sent = z_send[:, :, 0:128]
    z_send[:, :, 0:128] = (sent.astype(F32) + chosen.reshape(sent.shape)).astype(BF16)


def put_border(border_grad, total, keep):
    value = (total * keep).T
    bound = value.shape[0] // border_grad.shape[0]
    border_grad[:, 0:bound, :] = value.reshape(border_grad.shape[0], bound, value.shape[1])


def loss_kernel(classes, place, flags_t, came, came_oth, stale_t, bias, labels, mask, total_hbm, high, rest, sums, back_out, border_grad, grads_hbm, grads8_hbm, far_hbm, border_sum, hrows, rrows, total, grads, grads8, far, hbuf, rbuf, in_sems, edge_sems, out_sems, far_sems):
    kinds, half = total.shape
    halo = stale_t.shape[1]
    steps = half // ROWS
    cut = border_cut(2 * half, halo)
    blocks = Stream(
        in_sems,
        (high, cut, hrows, rows_at(ROWS)),
        (rest, cut, rrows, rows_at(ROWS)),
        (total_hbm, cols_at(ROWS), total, cols_at(ROWS)),
    )
    others = rows_at(ROWS, span((1 - place[0]) * half, half))
    edges = Stream(edge_sems, (high, others, hbuf, rows_at(ROWS)), (rest, others, rbuf, rows_at(ROWS)))
    stores = Stream(
        out_sems, *[(a, cols_at(ROWS), b, cols_at(ROWS)) for a, b in ((grads, grads_hbm), (grads8, grads8_hbm))]
    )
    far_stores = Stream(far_sems, (far, all_of, far_hbm, all_of))
    blocks.start_first(steps)
    edges.start(0)
    flat = lambda ref: ref[:, :, 0:128].reshape(halo, 128).astype(F32)
    both = flat(came) + flat(came_oth)
    old = jnp.concatenate([stale_t[...].astype(F32), jnp.zeros((kinds - classes, halo), F32)], axis=0)
    value = jnp.where(flags_t[2:3, :] == 1.0, both.T[0:kinds, :], old)
    scale, back = scale_of(value)
    back = back * (1.0 / REST_GAIN)
    border = value.astype(BF16)
    border8 = (value * scale).astype(F8)
    row = jnp.concatenate([bias[...], jnp.zeros((1, 128 - classes), F32)], axis=1)
    bias_col = jnp.broadcast_to(row, (8, 128)).T[0:kinds, 0:1]
    sums[...] = jnp.zeros(sums.shape, F32)
    border_sum[...] = jnp.zeros(border_sum.shape, F32)
    count = flags_t[3:4, 0:1]
    inverse = (1.0 / (256.0 * REST_GAIN)) / count
    back_out[...] = jnp.broadcast_to(inverse, back_out.shape)

    def far_step(i):
        edges.wait(i)
        here = span(i * ROWS, ROWS)
        both = dot_nn(grads[:, here], hbuf[here, :])
        low = dot_nn(grads8[:, here], rbuf[here, :]) * inverse
        far[...] += both[0:kinds] + both[kinds : 2 * kinds] + low

    def step(i):
        here = span(i * ROWS, ROWS)
        logits = total[:, here] + dot_nt(border, hrows[here, :]) + dot_nt(border8, rrows[here, :]) * back
        logits = logits + bias_col
        kind = lax.broadcasted_iota(I32, logits.shape, 0)
        real = kind < classes
        logits = jnp.where(real, logits, -jnp.inf)
        shifted = logits - jnp.max(logits, axis=0, keepdims=True)
        powers = jnp.exp(shifted)
        norm = jnp.sum(powers, axis=0, keepdims=True)
        logp = jnp.where(real, shifted - jnp.log(norm), 0.0)
        first = (place[0] * steps + i) * (ROWS // 128)
        row_of = lambda ref: jnp.concatenate([ref[pl.ds(first + k, 1), :] for k in range(ROWS // 128)], axis=1)
        target = jnp.where(kind == row_of(labels), 0.9, 0.0) + 0.1 / classes
        used = row_of(mask).astype(F32)
        loss = jnp.sum(target * logp, axis=0, keepdims=True) * used
        grad = jnp.where(real, (powers / norm - target) * (used / count), 0.0)
        sums[0:kinds, :] += lane_sums(grad)
        sums[kinds : kinds + 1, :] -= lane_sums(loss)
        top = grad.astype(BF16)
        tail = (grad - top.astype(F32)).astype(BF16)
        stacked = jnp.concatenate([top, tail], axis=0)
        small = (top.astype(F32) * (256.0 * count)).astype(F8)
        grads[:, here] = stacked
        grads8[:, here] = small
        stores.start(i)
        both = dot_nn(stacked, hrows[here, :])
        low = dot_nn(small, rrows[here, :]) * inverse
        border_sum[0:kinds, :] += both[0:kinds] + both[kinds : 2 * kinds] + low

    far[...] = jnp.zeros(far.shape, F32)
    blocks.next(0, steps)
    edges.start(1)
    step(0)

    def both_steps(i):
        blocks.next(i, steps)

        @pl.when(i + 1 < steps)
        def _():
            edges.start(i + 1)

        far_step(i - 1)
        step(i)

    lax.fori_loop(1, steps, lambda i, c: (both_steps(i), c)[1], 0)
    far_step(steps - 1)
    far_stores.start(0)
    put_border(border_grad, border_sum[...], flags_t[2:3, :])
    stores.wait_all(steps)
    far_stores.wait(0)


def lane_sums(value):
    total = value[:, 0:128]
    for first in range(128, value.shape[1], 128):
        total = total + value[:, first : first + 128]
    return total


def back_three_kernel(place, high, rest, grads, grads8, back, out, hbuf, rbuf, sems):
    kinds, size = out.shape
    base = place[0] * size * pl.num_programs(0)
    ring = Ring((high, rest), (hbuf, rbuf), sems, lambda i: (slice(None), span(base + i * size, size)))
    ring.begin()
    top, low = ring.wait()
    both = dot_nn(grads[...], top[...])
    out[...] = both[0:kinds] + both[kinds : 2 * kinds] + dot_nn(grads8[...], low[...]) * back[0:1, 0:1]
    ring.end()


def back_block(grads, grads8, tails8, back_rest, back_tail, top, low):
    total = dot_nn(grads, top) + dot_nn(grads8, low) * back_rest
    return total + dot_nn(tails8, top.astype(F8)) * back_tail


def back_kernel(place, back, grads, grads8, tails8, high, rest, out, hbuf, rbuf, edge_sems):
    half = out.shape[1]
    steps = half // ROWS
    mine = cols_at(ROWS, place[0] * half)
    edges = Stream(edge_sems, (high, mine, hbuf, cols_at(ROWS)), (rest, mine, rbuf, cols_at(ROWS)))
    edges.start_first(steps)

    def step(i):
        edges.next(i, steps)
        here = span(i * ROWS, ROWS)
        out[:, here] = back_block(
            grads[...], grads8[...], tails8[...], back[0:1, 0:1], back[0:1, 1:2], hbuf[:, here], rbuf[:, here]
        )

    loop(steps, step)


def returned_terms(ret, ret_oth, bound, kinds):
    value = ret[:, 0:bound, :] + ret_oth[:, 0:bound, :]
    value = value.reshape(value.shape[0] * bound, value.shape[2]).T[0:kinds, :]
    top = value.astype(BF16)
    return top, (value - top.astype(F32)).astype(BF16)


def round_gradient(own, came_part, terms, send, first_node):
    chosen = pick_rows(send, first_node, own.shape[1])
    total = own + came_part
    for term in terms:
        total = total + dot_nn(term, chosen)
    return total.astype(BF16)


def end_three_kernel(place, flags_t, ret, ret_oth, last_t, send, far_in_any, near_hbm, hidden_hbm, slope_hbm, high, rest, sums, back_out, border_sum, grad_last, grads, grads8, tails8, far, near, far_in, hidden_t, slope_t, hrows, rrows, grad_rows, hbuf, rbuf, in_sems, row_sems, edge_sems):
    kinds, half = near.shape
    units = slope_t.shape[0]
    parts = ret.shape[0]
    bound = send.shape[0] // parts
    halo = send.shape[0]
    steps = half // ROWS
    cut = border_cut(2 * half, halo)
    blocks = Stream(
        in_sems,
        *[
            (a, cols_at(ROWS), b, cols_at(ROWS))
            for a, b in ((near_hbm, near), (far_in_any, far_in), (hidden_hbm, hidden_t), (slope_hbm, slope_t))
        ],
    )
    borders = Stream(row_sems, (high, cut, hrows, rows_at(ROWS)), (rest, cut, rrows, rows_at(ROWS)))
    others = cols_at(ROWS, (1 - place[0]) * half)
    edges = Stream(edge_sems, (high, others, hbuf, cols_at(ROWS)), (rest, others, rbuf, cols_at(ROWS)))
    for stream in (blocks, borders, edges):
        loop(steps, stream.start)
    terms = returned_terms(ret, ret_oth, bound, kinds)
    weight = padded_rows(last_t, kinds)
    sums[...] = jnp.zeros(sums.shape, F32)
    grad_last[...] = jnp.zeros(grad_last.shape, F32)
    border_sum[...] = jnp.zeros(border_sum.shape, F32)

    def first_step(i, most):
        blocks.wait(i)
        here = span(i * ROWS, ROWS)
        d_z = round_gradient(near[:, here], far_in[:, here], terms, send[...], (place[0] * steps + i) * ROWS)
        grad_last[0:kinds, :] += dot_nt(d_z, hidden_t[:, here])
        grad = dot_tn(weight, d_z) * slope_t[:, here]
        sums[...] += lane_sums(grad)
        grad_rows[:, here] = grad
        return jnp.maximum(most, jnp.max(jnp.abs(grad), axis=0, keepdims=True))

    most = lax.fori_loop(0, steps, first_step, jnp.zeros((1, ROWS), F32))
    scale, back = scale_of(most)
    back_rest, back_tail = back * (1.0 / REST_GAIN), back * (1.0 / TAIL_GAIN)
    lane = lax.broadcasted_iota(I32, back_out.shape, 1)
    back_out[...] = jnp.where(lane == 0, back_rest, back_tail)

    def second_step(i):
        borders.wait(i)
        here = span(i * ROWS, ROWS)
        grad = grad_rows[:, here]
        top = grad.astype(BF16)
        wide = top.astype(F32)
        small = (wide * scale).astype(F8)
        tail = ((grad - wide) * (scale * TAIL_GAIN)).astype(F8)
        grads[:, here] = top
        grads8[:, here] = small
        tails8[:, here] = tail
        border_sum[...] += back_block(top, small, tail, back_rest, back_tail, hrows[here, :], rrows[here, :])

    loop(steps, second_step)
    border_sum[...] = border_sum[...] * flags_t[1:2, :]

    def far_step(i):
        edges.wait(i)
        here = span(i * ROWS, ROWS)
        far[:, here] = back_block(
            grads[...], grads8[...], tails8[...], back_rest, back_tail, hbuf[:, here], rbuf[:, here]
        )

    loop(steps, far_step)


def end_two_kernel(place, border, border_oth, packs, sums_two, sums_out, near, far, came_hbm, late_hbm, hidden_hbm, slope_hbm, feat_hbm, out, out_one, came, came_late, hidden_t, slope_t, near_feat, grad_first, grad_second, sums_one, came_sems, in_sems):
    units, half = near.shape
    halo = border.shape[1]
    steps = half // ROWS
    extra = near_feat.shape[0] // 2
    every = lambda i: (slice(None), slice(None), slice(None))
    fetch = Stream(came_sems, (came_hbm, every, came, every), (late_hbm, every, came_late, every))
    blocks = Stream(
        in_sems,
        *[
            (a, cols_at(ROWS), b, cols_at(ROWS))
            for a, b in ((hidden_hbm, hidden_t), (slope_hbm, slope_t), (feat_hbm, near_feat))
        ],
    )
    loop(steps, blocks.start)
    fetch.start(0)
    weight = packs[:, 128 : 128 + units]
    for ref in (grad_first, grad_second, sums_one):
        ref[...] = jnp.zeros(ref.shape, F32)

    def through(d_z, slope):
        grad = dot_tn(weight, d_z) * slope
        sums_one[...] += lane_sums(grad)
        top = grad.astype(BF16)
        return top, (grad - top.astype(F32)).astype(BF16)

    def step(i):
        blocks.wait(i)
        here = span(i * ROWS, ROWS)
        d_z = (near[:, here] + far[:, here]).astype(BF16)
        grad_second[...] += dot_nt(d_z, hidden_t[:, here])
        top, tail = through(d_z, slope_t[:, here])
        high, low = near_feat[0:extra, here], near_feat[extra:, here]
        grad_first[:, 0:extra] += dot_nt(top, high) + (dot_nt(tail, high) + dot_nt(top, low))

    loop(steps, step)
    fetch.wait(0)
    lanes = lambda ref, first, size: ref[:, :, first : first + size].reshape(halo, size)
    d_z = (border[...] + border_oth[...]).astype(BF16)
    grad_second[...] += dot_nn(d_z, lanes(came, units, units))
    slope = lanes(came, 2 * units, units).astype(F32) + lanes(came_late, 128, units).astype(F32)
    top, tail = through(d_z, slope.T)
    high, low = lanes(came_late, 128 + units, 128), lanes(came_late, 256 + units, 128)
    grad_first[...] += dot_nn(top, high) + (dot_nn(tail, high) + dot_nn(top, low))
    lane = lax.broadcasted_iota(I32, (64, 128), 1)
    column = lambda value: jnp.sum(value, axis=1, keepdims=True)
    for k, ref in enumerate((out, out_one)):
        rows = span(jnp.bitwise_xor(place[0] + 2 * place[1], k) * 64, 64)
        value = jnp.where(lane < FLAG_LANE, grad_first[rows, :], 0.0)
        value = jnp.where(lane == FLAG_LANE, column(sums_one[rows, :]), value)
        value = jnp.where(lane == FLAG_LANE + 1, column(sums_two[rows, :]), value)
        ref[0:64, :] = jnp.where(lane == FLAG_LANE + 2, column(sums_out[...]), value)
        ref[64:128, :] = grad_second[rows, 0:128]
        ref[128:192, :] = grad_second[rows, 128:256]


def scatter_kernel(mine, came, last, last_came, out):
    total = mine[...] + came[...]
    last_total = last[...] + last_came[...]
    parts = out.shape[0]
    size = 64 // parts
    for q in range(parts):
        pieces = [total[64 * k + q * size : 64 * k + (q + 1) * size, :] for k in range(3)]
        chunk = last_total[q * size : (q + 1) * size, :]
        out[q] = jnp.concatenate(pieces + [chunk[:, 0:128], chunk[:, 128:256]], axis=0)


def joined(came, first, size):
    return came[:, first : first + size, :].reshape(64, 128)


def gather_kernel(came, out):
    value = jnp.sum(came[...], axis=0)
    for p in range(came.shape[0]):
        out[p] = value


def adamw(weight, moment, square, gradient):
    moment = beta_one * moment + (1.0 - beta_one) * gradient
    square = beta_two * square + (1.0 - beta_two) * gradient * gradient
    moment_hat = moment / (1.0 - beta_one**STEP)
    square_hat = square / (1.0 - beta_two**STEP)
    weight = weight - rate_step * (
        moment_hat / (jnp.sqrt(square_hat) + epsilon) + decay_rate * weight
    )
    return (weight, moment, square)


def update_kernel(came, flags_t, *refs):
    params, outs = refs[0:15], refs[15:]
    parts = came.shape[0]
    size = 64 // parts
    width, kinds = params[0].shape[1], params[6].shape[0]
    total = joined(came, 0, size)
    halves = [joined(came, size, size), joined(came, 2 * size, size)]
    turned = jnp.concatenate([total, jnp.zeros((64, 128), F32)], axis=0).T
    gradients = (
        total[:, 0:width],
        jnp.concatenate(halves, axis=1),
        jnp.concatenate([joined(came, 3 * size, size), joined(came, 4 * size, size)], axis=1)[0:kinds, :],
        turned[FLAG_LANE : FLAG_LANE + 2, 0:64],
        turned[FLAG_LANE + 2 : FLAG_LANE + 3, 0:kinds],
    )
    for k, gradient in enumerate(gradients):
        values = adamw(*[ref[...] for ref in params[3 * k : 3 * k + 3]], gradient)
        for ref, value in zip(outs[3 * k : 3 * k + 3], values):
            ref[...] = value
    padded = turned[FLAG_LANE + 2 : FLAG_LANE + 3, 48:49]
    outs[15][...] = jnp.broadcast_to(padded, (1, 128))
    outs[16][...] = jnp.broadcast_to(flags_t[3:4, 0:1], (1, 128))


def body(
    parts,
    reps,
    features,
    labels,
    train_mask,
    edge_src,
    edge_norm,
    send_rows,
    changed,
    cache_hidden,
    cache_out,
    first_weight,
    second_weight,
    last_weight,
    hidden_bias,
    out_bias,
    moment_first,
    moment_second,
    moment_last,
    moment_hidden,
    moment_out,
    square_first,
    square_second,
    square_last,
    square_hidden,
    square_out,
):
    nodes, in_width = features.shape
    half = nodes // 2
    bound = send_rows.shape[2]
    halo = parts * bound
    table = nodes + halo
    units, classes = last_weight.shape
    kinds = -(-classes // 16) * 16
    steps, fine = half // ROWS, half // FINE

    rep = lax.axis_index("rep")
    place = jnp.stack([lax.rem(rep, 2), lax.div(rep, 2)]).astype(I32)
    where = (place, SMEM)
    feat_t = features.T
    last_t = last_weight.T
    label_rows = labels.reshape(nodes // 128, 128)
    mask_rows = train_mask.reshape(nodes // 128, 128)

    def swap(x, k=1):
        return lax.ppermute(x, "rep", [(i, i ^ k) for i in range(reps)])

    def exchange(x):
        return lax.all_to_all(x, "dom", split_axis=0, concat_axis=0, tiled=True)

    def late(after, *arrays):
        return lax.optimization_barrier((*arrays, after))

    vm = pltpu.VMEM
    whole = lambda a: (a, whole_spec(a.shape))
    work = 2 * half * table * units
    pack_width = 256 + units + 2 * halo
    extra = -(-in_width // 16) * 16
    both = units + extra
    rows_out, pack, send = run(
        pack_kernel,
        "pack",
        [
            whole(feat_t),
            whole(send_rows.reshape(parts, bound)),
            whole(changed.T),
            *[whole(a) for a in (mask_rows, first_weight.T, second_weight.T)],
            *[whole(a) for a in (jnp.transpose(cache_hidden, (0, 2, 1)), hidden_bias)],
        ],
        [
            ((parts, bound, 128), BF16, VMEM),
            ((units // reps, pack_width), BF16, VMEM),
            ((halo, 1), I32, VMEM),
        ],
        flops=2 * halo * nodes * 128,
        grid=(1,),
    )
    packs = [pack if k == 0 else swap(pack, k) for k in range(reps)]
    rows = exchange(rows_out)
    node_block = lambda size, rows: pl.BlockSpec((rows, size), lambda i: (0, i))
    block, fine_block = node_block(ROWS, units), node_block(FINE, units)
    scalar = pltpu.SMEM((1,), F32)
    packs, most, first_table = run(
        table_kernel,
        "table",
        [where, *placed(VMEM, *packs), (feat_t, HBM)],
        [((units, pack_width), BF16, OWN), ((units, 128), F32, VMEM), ((units + extra, nodes), BF16, HBM)],
        [
            vm((in_width, nodes), BF16),
            vm((units + extra, nodes), BF16),
            sems(1, 4),
            sems(1, 4),
        ],
        flops=2 * units * nodes * in_width,
    )
    rows, most = late(most, rows)
    held = fine if half * table * 3 <= RESIDENT_BYTES else min(fine, 4)
    z_send, later, flags_t, high, rest, hidden_one, slope_one, z_own, near_feat = run(
        layer_one_kernel,
        "layer_one",
        [where, *placed(OWN, edge_src.T, edge_norm.T), *placed(VMEM, rows, send, most), *placed(HBM, packs, first_table)],
        [
            ((parts, bound, 3 * units), BF16, VMEM),
            ((parts, bound, units + 256), BF16, OWN),
            ((8, halo), F32, OWN),
            ((half, table), BF16, HBM),
            ((half, table), F8, HBM),
            ((units, half), BF16, HBM),
            ((units, half), F32, HBM),
            ((units, half), BF16, HBM),
            ((2 * extra, half), BF16, HBM),
        ],
        [
            vm((units, pack_width), BF16),
            vm((both, table), BF16),
            vm((units, table), F8),
            vm((held * FINE, table), BF16),
            vm((held * FINE, table), F8),
            vm((units, half), BF16),
            vm((units, half), F32),
            vm((units, half), BF16),
            vm((2 * extra, half), BF16),
            sems(2, 1),
            sems(2, fine),
            sems(4, fine),
        ],
        flops=2 * work,
    )
    edge = placed(HBM, high, rest)

    def own_part(z_own, z_oth, name):
        n = z_own.shape[0]
        return run(
            own_part_kernel,
            name,
            [where, *edge, whole(z_own), (z_oth, VMEM)],
            [((n, half), F32, node_block(FINE, n))],
            [vm((n, nodes), BF16), vm((n, nodes), F8), scalar, *ring_scratch((FINE, nodes))],
            flops=work,
            grid=(fine,),
        )[0]

    z_oth = swap(z_own)
    came = exchange(z_send)
    total = own_part(z_own, z_oth, "layer_two_own")
    came, total = late(total, came)
    came_one = came
    came_oth = swap(came)
    wide = half // 2
    wide_block = node_block(wide, units)
    border_block = lambda array: (array, pl.BlockSpec((wide, halo), lambda i: (i, nodes // halo)))
    hidden_two, slope_two, z_own, z_send = run(
        layer_two_end_kernel,
        "layer_two_end",
        [where, whole(flags_t), whole(packs), (send, VMEM), border_block(high), border_block(rest), (total, wide_block)]
        + placed(VMEM, came, came_oth)
        + [whole(later), whole(last_t)],
        [
            ((units, half), BF16, wide_block),
            ((units, half), F32, wide_block),
            ((kinds, half), BF16, node_block(wide, kinds)),
            ((parts, bound, 128 + units + 256), BF16, whole_spec((parts, bound, 128 + units + 256))),
        ],
        [vm((units, halo), BF16), vm((units, halo), F8), scalar],
        flops=work // 4,
        grid=(half // wide,),
    )
    z_oth = swap(z_own)
    came = exchange(z_send)
    total = own_part(z_own, z_oth, "layer_three_own")
    came, total = late(total, came)
    came_two = came
    came_oth = swap(came)
    border_rows = [vm((half, halo), BF16), vm((half, halo), F8)]
    sums_out, back, border_grad, grads, grads8, far = run(
        functools.partial(loss_kernel, classes),
        "loss",
        [
            where,
            *placed(VMEM, flags_t, came, came_oth, cache_out.T, out_bias.reshape(1, classes), label_rows, mask_rows),
            (total, HBM),
            *edge,
        ],
        [
            ((64, 128), F32, VMEM),
            ((8, 128), F32, VMEM),
            ((parts, bound, 128), F32, VMEM),
            ((2 * kinds, half), BF16, HBM),
            ((kinds, half), F8, HBM),
            ((kinds, half), F32, HBM),
        ],
        [
            vm((128, halo), F32),
            *border_rows,
            vm((kinds, half), F32),
            vm((2 * kinds, half), BF16),
            vm((kinds, half), F8),
            vm((kinds, half), F32),
            vm((half, half), BF16),
            vm((half, half), F8),
            sems(3, steps),
            sems(2, steps),
            sems(2, steps),
            sems(1, 1),
        ],
        flops=work,
    )
    far = swap(far)
    ret = exchange(border_grad)
    near = run(
        back_three_kernel,
        "back_three",
        [where, *edge, whole(grads), whole(grads8), (back, VMEM)],
        [((kinds, half), F32, node_block(ROWS, kinds))],
        ring_scratch((half, ROWS)),
        flops=work // 2,
        grid=(steps,),
    )[0]
    ret, far, near = late(near, ret, far)
    ret_oth = swap(ret)
    sums_two, back, border, last, grads, grads8, tails8, far = run(
        end_three_kernel,
        "end_three",
        [where, *placed(VMEM, flags_t, ret, ret_oth, last_t, send), (far, ANY)]
        + [*placed(HBM, near, hidden_two, slope_two), *edge],
        [
            ((units, 128), F32, VMEM),
            ((8, 128), F32, VMEM),
            ((units, halo), F32, VMEM),
            ((64, units), F32, VMEM),
            ((units, half), BF16, VMEM),
            ((units, half), F8, VMEM),
            ((units, half), F8, VMEM),
            ((units, half), F32, VMEM),
        ],
        [
            vm((kinds, half), F32),
            vm((kinds, half), F32),
            vm((units, half), BF16),
            vm((units, half), F32),
            *border_rows,
            vm((units, half), F32),
            vm((half, half), BF16),
            vm((half, half), F8),
            sems(4, steps),
            sems(2, steps),
            sems(2, steps),
        ],
        flops=work,
        limit=LOW_LIMIT,
    )
    far, border_oth, last_oth = swap(far), swap(border), swap(last)
    near = run(
        back_kernel,
        "back",
        [where, *placed(VMEM, back, grads, grads8, tails8), *edge],
        [((units, half), F32, VMEM)],
        [vm((half, half), BF16), vm((half, half), F8), sems(2, steps)],
        flops=work // 2,
        limit=LOW_LIMIT,
    )[0]
    mine, theirs = run(
        end_two_kernel,
        "end_two",
        [where, *placed(VMEM, border, border_oth), (packs, OWN), *placed(VMEM, sums_two, sums_out, near, far)]
        + [*placed(HBM, came_one, came_two, hidden_one, slope_one, near_feat)],
        [((192, 128), F32, VMEM)] * 2,
        [
            vm(came_one.shape, BF16),
            vm(came_two.shape, BF16),
            vm((units, half), BF16),
            vm((units, half), F32),
            vm((2 * extra, half), BF16),
            vm((units, 128), F32),
            vm((units, units), F32),
            vm((units, 128), F32),
            sems(2, 1),
            sems(3, steps),
        ],
        flops=work // 4,
        limit=LOW_LIMIT,
    )
    scattered = run(
        scatter_kernel,
        "scatter",
        placed(VMEM, mine, swap(theirs), last, last_oth),
        [((parts, 5 * 64 // parts, 128), F32, VMEM)],
    )[0]
    gathered = run(
        gather_kernel,
        "gather",
        placed(VMEM, exchange(scattered)),
        [(scattered.shape, F32, VMEM)],
    )[0]
    came = exchange(gathered)

    turn = lambda x: x.T
    same = lambda x: x
    row = lambda x: x.reshape(1, -1)
    forms = (turn, turn, turn, same, row)
    weights = (first_weight, second_weight, last_weight, hidden_bias, out_bias)
    moments = (moment_first, moment_second, moment_last, moment_hidden, moment_out)
    squares = (square_first, square_second, square_last, square_hidden, square_out)
    params = [form(x) for form, triple in zip(forms, zip(weights, moments, squares)) for x in triple]
    outs = run(
        update_kernel,
        "update",
        placed(VMEM, came, flags_t, *params),
        [(p.shape, F32, VMEM) for p in params] + [((1, 128), F32, VMEM)] * 2,
    )
    undo = (turn, turn, turn, same, lambda x: x.reshape(-1))
    results = [undo[k // 3](x) for k, x in enumerate(outs[0:15])]
    return (outs[15][0, 0], outs[16][0, 0], *results)


def solution(mesh):
    placed = (
        P("dom", None),
        P("dom"),
        P("dom"),
        P("dom", None),
        P("dom", None),
        P("dom", None, None),
        P(None, "dom"),
        P(None, "dom", "rep"),
        P("dom", None),
        P(None, "rep"),
        P(None, "rep"),
        P(),
        P(None, "rep"),
        P(),
        P(None, "rep"),
        P(None, "rep"),
        P(),
        P(None, "rep"),
        P(),
        P(None, "rep"),
        P(None, "rep"),
        P(),
        P(None, "rep"),
        P(),
    )
    return jax.shard_map(
        functools.partial(body, mesh.shape["dom"], mesh.shape["rep"]),
        mesh=mesh,
        in_specs=placed,
        out_specs=(P(), P()) + (P(None, "rep"),) * 6 + (P(),) * 3 + (P(None, "rep"),) * 3 + (P(),) * 3,
        check_vma=False,
    )
```
